128 devices in a mesh: lon: 16 (over z, x_hi, core), lat: 8 (over y, x_lo).
Axes of the slice: x: 4 (x_hi: 2, x_lo: 2; x = x_hi * 2 + x_lo), y: 4, z: 4, core: 2. Of those that a mesh axis runs over, the one named last changes fastest.
Arguments:
- tokens: bfloat16 [2, 384, 96, 512], P(None, 'lon', 'lat'), may hold values from -6 to 6
- observed: int32 [2, 384, 96], P(None, 'lon', 'lat'), may hold values 0 or 1
- mask_token: float32 [512], replicated, may hold values from -4 to 4
- gain_one: float32 [512], replicated, may hold values from 0.25 to 1.75
- qkv_one: bfloat16 [512, 1536], replicated, may hold values from -0.25 to 0.25
- table_one: float32 [8, 759], replicated, may hold values from -4 to 408
- proj_one: bfloat16 [512, 512], replicated, may hold values from -0.25 to 0.25
- merge_weight: bfloat16 [2048, 1024], replicated, may hold values from -0.125 to 0.125
- gain_two: float32 [1024], replicated, may hold values from 0.25 to 1.75
- qkv_two: bfloat16 [1024, 3072], replicated, may hold values from -0.1875 to 0.1875
- table_two: float32 [16, 759], replicated, may hold values from -4 to 408
- proj_two: bfloat16 [1024, 1024], replicated, may hold values from -0.1875 to 0.1875
- cotangent: bfloat16 [2, 192, 48, 1024], P(None, 'lon', 'lat'), may hold values from -6 to 6
Outputs:
- result: bfloat16 [2, 192, 48, 1024], P(None, 'lon', 'lat')
- grad_tokens: bfloat16 [2, 384, 96, 512], P(None, 'lon', 'lat')
- grad_qkv_one: float32 [512, 1536], P('lon', 'lat')
- grad_qkv_two: float32 [1024, 3072], P('lon', 'lat')
The draws below stay inside these ranges and needn't reach their ends.
All inputs are finite; a program needn't handle non-finite values. No bound on the sum of `observed` on one device may be relied on, other than what follows from the above.
Results may differ from the reference program's by a relative error of at most 0.035.
Values may be sent and summed in bfloat16 or wider, within the bound.
A program may use at most 128 MiB of HBM per device.

```python
import math
import jax
import jax.numpy as jnp
from jax import lax

C1 = 512
H1 = 8
C2 = 1024
H2 = 16
WV = 2
WL = 12
WA = 6
LEV = 2
NLON = 384
NLAT = 96
NREL = 759


def offset_table(key, heads, lowest):
    subkeys = jax.random.split(key, 6)
    ground = jnp.clip(jax.random.normal(subkeys[0], (heads, NREL), jnp.float32), -4.0, 4.0)
    strength = jnp.exp(jax.random.uniform(subkeys[2], (heads,), jnp.float32, math.log(lowest), math.log(400.0)))
    chosen = jax.random.randint(subkeys[3], (heads,), 0, 2) == 1
    forced = jax.random.randint(subkeys[4], (), 0, heads)
    head_ids = jnp.arange(heads)
    chosen = chosen | (head_ids == forced)
    strength = jnp.where(head_ids == forced, 300.0, strength)
    jitter = jax.random.uniform(subkeys[5], (heads, NREL), jnp.float32, 0.0, 3.0)
    lon_offset = jnp.arange(NREL) // (2 * WA - 1) % (2 * WL - 1)
    farthest = lon_offset == 2 * WL - 2
    raised = jnp.where(chosen[:, None] & farthest[None, :], strength[:, None] + jitter, 0.0)
    return (ground + raised).astype(jnp.float32)


def draw_table_one(key, part):
    key = jax.random.fold_in(key, 21)
    return offset_table(key, H1, 120.0)


def draw_table_two(key, part):
    key = jax.random.fold_in(key, 37)
    return offset_table(key, H2, 120.0)


def set_ends(entries, stream_key, smallest, largest):
    place = [jax.random.randint(jax.random.fold_in(stream_key, axis), (), 0, length) for axis, length in enumerate(entries.shape)]
    longest = entries.shape.index(max(entries.shape))
    neighbour = place[:longest] + [(place[longest] + 1) % entries.shape[longest]] + place[longest + 1:]
    return entries.at[tuple(place)].set(smallest).at[tuple(neighbour)].set(largest)


def level_of(stream_key, dims, pieces, smallest, top_value):
    def one(axis_at, blocks):
        steps = jax.random.uniform(jax.random.fold_in(jax.random.fold_in(stream_key, 6), axis_at), (blocks,), jnp.float32, smallest / len(pieces), top_value / len(pieces))
        return jnp.repeat(jnp.exp(steps), dims[axis_at] // blocks).reshape((-1,) + (1,) * (len(dims) - axis_at - 1))

    level = one(*pieces[0])
    for cut in pieces[1:]:
        level = level * one(*cut)
    return level


def normal_values(rng, dims, scale, bound, cuts=(), dtype=jnp.bfloat16):
    array = scale * jax.random.normal(rng, dims, jnp.float32)
    if cuts:
        array = array * level_of(rng, dims, cuts, -0.22, 0.18)
    return jnp.clip(array, -bound, bound).astype(dtype)


def setup_inputs(seed: int = 0) -> dict:
    streams_of = jax.random.split(jax.random.key(seed), 14)
    tokens = normal_values(streams_of[0], (LEV, NLON, NLAT, C1), 1.0, 6.0, ((1, 16), (2, 8)))
    observed = set_ends((jax.random.randint(streams_of[1], (LEV, NLON, NLAT), 0, 4) < 3).astype(jnp.int32), jax.random.fold_in(streams_of[1], 1), 0, 1)
    mask_token = normal_values(streams_of[2], (C1,), 1.0, 4.0, (), jnp.float32)
    gain_one = jnp.clip(1.0 + 0.15 * jax.random.normal(streams_of[3], (C1,), jnp.float32), 0.25, 1.75)
    qkv_one = normal_values(streams_of[4], (C1, 3 * C1), C1 ** -0.5, 0.25)
    table_one = draw_table_one(jax.random.fold_in(streams_of[13], 71), 0)
    proj_one = normal_values(streams_of[6], (C1, C1), C1 ** -0.5, 0.25)
    merge_weight = normal_values(streams_of[7], (4 * C1, C2), (4 * C1) ** -0.5, 0.125)
    gain_two = jnp.clip(1.0 + 0.15 * jax.random.normal(streams_of[8], (C2,), jnp.float32), 0.25, 1.75)
    qkv_two = normal_values(streams_of[9], (C2, 3 * C2), C2 ** -0.5, 0.1875)
    table_two = draw_table_two(jax.random.fold_in(streams_of[13], 71), 0)
    proj_two = normal_values(streams_of[11], (C2, C2), C2 ** -0.5, 0.1875)
    cotangent = normal_values(streams_of[12], (LEV, NLON // 2, NLAT // 2, C2), 1.0, 6.0, ((1, 16), (2, 8)))
    return {"tokens": tokens, "observed": observed, "mask_token": mask_token, "gain_one": gain_one, "qkv_one": qkv_one, "table_one": table_one, "proj_one": proj_one, "merge_weight": merge_weight, "gain_two": gain_two, "qkv_two": qkv_two, "table_two": table_two, "proj_two": proj_two, "cotangent": cotangent}


EPS = 1e-05
NEG = -1000000000.0

def norm_rows(x, gain):
    values = x.astype(jnp.float32)
    centre = lax.optimization_barrier(jnp.mean(values, axis=-1, keepdims=True))
    spread = lax.optimization_barrier(jnp.mean((values - centre) ** 2, axis=-1, keepdims=True))
    return ((values - centre) * lax.rsqrt(spread + EPS) * gain).astype(jnp.bfloat16)

def to_windows(x):
    depth, along, across, width = x.shape
    x = x.reshape(depth // WV, WV, along // WL, WL, across // WA, WA, width)
    x = x.transpose(0, 2, 4, 1, 3, 5, 6)
    return x.reshape(-1, WV * WL * WA, width)

def from_windows(blocks, depth, along, across):
    width = blocks.shape[-1]
    blocks = blocks.reshape(depth // WV, along // WL, across // WA, WV, WL, WA, width)
    blocks = blocks.transpose(0, 3, 1, 4, 2, 5, 6)
    return blocks.reshape(depth, along, across, width)

def relative_index():
    grid = jnp.stack(jnp.meshgrid(jnp.arange(WV), jnp.arange(WL), jnp.arange(WA), indexing='ij'), -1).reshape(-1, 3)
    offset = grid[:, None, :] - grid[None, :, :]
    return ((offset[..., 0] + WV - 1) * (2 * WL - 1) + offset[..., 1] + WL - 1) * (2 * WA - 1) + offset[..., 2] + WA - 1

def window_core(qkv, latitude, table, heads):
    count, cells, triple = qkv.shape
    width = triple // 3
    head = width // heads
    parts = qkv.reshape(count, cells, 3, heads, head).astype(jnp.float32)
    query, key, value = (parts[:, :, 0], parts[:, :, 1], parts[:, :, 2])
    score = jnp.einsum('bnhd,bmhd->bhnm', query, key) * head ** (-0.5)
    score = score + table[:, relative_index()][None]
    apart = jnp.abs(latitude[:, :, None] - latitude[:, None, :]) >= WA
    score = jnp.where(apart[:, None], NEG, score)
    top = lax.optimization_barrier(jnp.max(score, axis=-1, keepdims=True))
    expo = jnp.exp(score - top)
    weights = (expo / lax.optimization_barrier(jnp.sum(expo, axis=-1, keepdims=True))).astype(jnp.bfloat16)
    mixed = jnp.einsum('bhnm,bmhd->bnhd', weights.astype(jnp.float32), value)
    return mixed.astype(jnp.bfloat16).reshape(count, cells, width)

def mapped_core(qkv, latitude, table, heads):
    count, cells, triple = qkv.shape
    group = 8
    stacked = (qkv.reshape(count // group, group, cells, triple), latitude.reshape(count // group, group, cells))
    out = lax.map(lambda pair: window_core(pair[0], pair[1], table, heads), stacked)
    return out.reshape(count, cells, triple // 3)

def level_forward(x, gain, w_qkv, table, w_proj, heads):
    depth, along, across, width = x.shape
    half_lon, half_lat = (WL // 2, WA // 2)
    normed = norm_rows(x, gain)
    rolled = jnp.roll(normed, (-half_lon, -half_lat), (1, 2))
    qkv = jnp.dot(rolled, w_qkv, preferred_element_type=jnp.float32).astype(jnp.bfloat16)
    line = ((jnp.arange(across) + half_lat) % across).astype(jnp.int32)
    lat_grid = jnp.broadcast_to(line[None, None, :, None], (depth, along, across, 1))
    lat_win = to_windows(lat_grid)[:, :, 0]
    qkv_win = to_windows(qkv)
    mixed = from_windows(mapped_core(qkv_win, lat_win, table, heads), depth, along, across)
    branch = jnp.dot(mixed, w_proj, preferred_element_type=jnp.float32).astype(jnp.bfloat16)
    branch = jnp.roll(branch, (half_lon, half_lat), (1, 2))
    out = (x.astype(jnp.float32) + branch.astype(jnp.float32)).astype(jnp.bfloat16)
    return (out, (rolled, qkv_win, mixed, lat_win))

def level_backward(grad_out, x, saved, gain, w_qkv, table, w_proj, heads):
    rolled, qkv_win, mixed, lat_win = saved
    depth, along, across, width = x.shape
    half_lon, half_lat = (WL // 2, WA // 2)
    grad_branch = jnp.roll(grad_out, (-half_lon, -half_lat), (1, 2))
    _, back_proj = jax.vjp(lambda m: jnp.dot(m, w_proj, preferred_element_type=jnp.float32).astype(jnp.bfloat16), mixed)
    grad_mixed, = back_proj(grad_branch)
    _, back_core = jax.vjp(lambda q: mapped_core(q, lat_win, table, heads), qkv_win)
    grad_win, = back_core(to_windows(grad_mixed))
    grad_qkv = from_windows(grad_win, depth, along, across)
    grad_weight = jnp.dot(rolled.reshape(-1, width).T, grad_qkv.reshape(-1, 3 * width), preferred_element_type=jnp.float32)
    _, back_in = jax.vjp(lambda r: jnp.dot(r, w_qkv, preferred_element_type=jnp.float32).astype(jnp.bfloat16), rolled)
    grad_rolled, = back_in(grad_qkv)
    grad_normed = jnp.roll(grad_rolled, (half_lon, half_lat), (1, 2))
    _, back_norm = jax.vjp(lambda z: norm_rows(z, gain), x)
    grad_inner, = back_norm(grad_normed)
    grad_x = (grad_out.astype(jnp.float32) + grad_inner.astype(jnp.float32)).astype(jnp.bfloat16)
    return (grad_x, grad_weight)

def merge_patches(x, weight):
    depth, along, across, width = x.shape
    x = x.reshape(depth, along // 2, 2, across // 2, 2, width).transpose(0, 1, 3, 2, 4, 5)
    x = x.reshape(depth, along // 2, across // 2, 4 * width)
    return jnp.dot(x, weight, preferred_element_type=jnp.float32).astype(jnp.bfloat16)

def reference(tokens, observed, mask_token, gain_one, qkv_one, table_one, proj_one, merge_weight, gain_two, qkv_two, table_two, proj_two, cotangent):
    present = observed[..., None] == 1
    first = jnp.where(present, tokens, mask_token.astype(jnp.bfloat16))
    out_one, saved_one = level_forward(first, gain_one, qkv_one, table_one, proj_one, H1)
    second, back_merge = jax.vjp(lambda z: merge_patches(z, merge_weight), out_one)
    result, saved_two = level_forward(second, gain_two, qkv_two, table_two, proj_two, H2)
    grad_second, grad_qkv_two = level_backward(cotangent, second, saved_two, gain_two, qkv_two, table_two, proj_two, H2)
    grad_one, = back_merge(grad_second)
    grad_first, grad_qkv_one = level_backward(grad_one, first, saved_one, gain_one, qkv_one, table_one, proj_one, H1)
    grad_tokens = jnp.where(present, grad_first, jnp.zeros_like(grad_first))
    return (result, grad_tokens, grad_qkv_one, grad_qkv_two)
```

```python
import functools
from types import SimpleNamespace
import numpy as np
import jax
import jax.numpy as jnp
from jax import lax
from jax.experimental import pallas as pl
from jax.experimental.pallas import tpu as pltpu
from jax.sharding import PartitionSpec as P

BF = jnp.bfloat16
F32 = jnp.float32
EPS = 1e-05
NEG = -1000000000.0
MESH = pl.DeviceIdType.MESH
CELLS = 144
HALF = 72

SEG1 = ((0, 336), (336, 112), (448, 112), (560, 48))
SEG2 = ((0, 48), (48, 48), (96, 48), (144, 48))


def _cells(along, across, half_lon, half_lat):
    out = [[], [], [], []]
    for v in range(2):
        for i in range(along):
            for j in range(across):
                seg = (1 if i < half_lon else 0) + (2 if j < half_lat else 0)
                moved = (v, (i - half_lon) % along, (j - half_lat) % across)
                out[seg].append(((v, i, j), moved))
    return out


def _send_index(segs, cells, row_of):
    out = [-1] * (segs[-1][0] + segs[-1][1])
    for (start, _), members in zip(segs, cells):
        for n, (cell, _) in enumerate(members):
            out[start + n] = row_of(*cell)
    return out


def _recv_index(segs, cells, row_of, rows):
    out = [-1] * rows
    for (start, _), members in zip(segs, cells):
        for n, (_, moved) in enumerate(members):
            out[row_of(*moved)] = start + n
    return out


def _inverse(index, rows):
    out = [-1] * rows
    for n, m in enumerate(index):
        if m >= 0:
            out[m] = n
    return out


def _nat1(v, i, j):
    return (v * 12 + j) * 24 + i


def _win1(v, i, j):
    return ((i // 12) * 2 + j // 6) * CELLS + (j % 6) * 24 + v * 12 + i % 12


def _merge(v, i, j):
    return ((i % 2) * 2 + j % 2) * CELLS + (j // 2) * 24 + v * 12 + i // 2


def _nat2(v, i, j):
    return (i * 6 + j) * 2 + v


def _win2(v, i, j):
    return j * 24 + v * 12 + i


def _indices():
    one = _cells(24, 12, 6, 3)
    two = _cells(12, 6, 6, 3)
    s1 = _send_index(SEG1, one, _nat1)
    r1 = _recv_index(SEG1, one, _win1, 576)
    s2 = _send_index(SEG1, one, _win1)
    r2 = _recv_index(SEG1, one, _merge, 576)
    sc = _send_index(SEG2, two, _nat2)
    rc = _recv_index(SEG2, two, _win2, CELLS)
    flip = [-1] * 768
    for x in range(3):
        for y in range(23):
            for z in range(11):
                flip[((2 - x) * 23 + 22 - y) * 11 + 10 - z] = z * 69 + x * 23 + y
    pick = [-1] * 768
    for z in range(11):
        for v in range(2):
            for l in range(12):
                pick[z * 69 + v * 23 + l] = z * 24 + v * 12 + l
    return dict(s1=s1, r1=r1, s2=s2, r2=r2, s3=_inverse(r2, 608), r3=_inverse(s2, 576), s4=_inverse(r1, 608),
                r4=_inverse(s1, 576), sc=sc, rc=rc, sr=_inverse(rc, 192), rr=_inverse(sc, CELLS), flip=flip, pick=pick)


INDEX = _indices()
TABLE_OF = np.full((768, len(INDEX)), -1, np.int32)
for _n, _rows in enumerate(INDEX.values()):
    TABLE_OF[:len(_rows), _n] = _rows

SHAPES = dict(first=(576, 512), cot=(CELLS, 1024), w1=(512, 1536), p1=(512, 512), p2=(1024, 1024),
              wm=(2048, 1024), w2=(1024, 3072))
LOADS = tuple(SHAPES)


def nn(a, b):
    return lax.dot_general(a, b, (((1,), (0,)), ((), ())), preferred_element_type=F32)


def nt(a, b):
    return lax.dot_general(a, b, (((1,), (1,)), ((), ())), preferred_element_type=F32)


def tn(a, b):
    return lax.dot_general(a, b, (((0,), (0,)), ((), ())), preferred_element_type=F32)


def norm_stats(x):
    centre = jnp.mean(x, axis=-1, keepdims=True)
    dev = x - centre
    spread = jnp.mean(dev * dev, axis=-1, keepdims=True)
    return dev, lax.rsqrt(spread + EPS)


def loop(n, body):
    lax.fori_loop(0, n, lambda i, c: (body(i), c)[1], 0)


SCRATCH = dict(
    {k: pltpu.VMEM(SHAPES[k], BF) for k in LOADS},
    parts=pltpu.VMEM((72, 768), F32),
    ext=pltpu.VMEM((24, 24, 264), F32),
    bias=pltpu.VMEM((24, CELLS, CELLS), F32),
    madd=pltpu.VMEM((2, CELLS, CELLS), F32),
    xr=pltpu.VMEM((4, 608, 512), BF),
    xs=pltpu.VMEM((4, 272, 512), BF),
    cr=pltpu.VMEM((2, 192, 1024), BF),
    cs=pltpu.VMEM((2, 144, 1024), BF),
    x1=pltpu.VMEM((576, 512), BF),
    rolled1=pltpu.VMEM((576, 512), BF),
    rolled1t=pltpu.VMEM((512, 576), BF),
    qkv1=pltpu.VMEM((576, 1536), BF),
    dqkv1=pltpu.VMEM((576, 1536), BF),
    prob1=pltpu.VMEM((16, 288, CELLS), BF),
    mixed1=pltpu.VMEM((576, 512), BF),
    out1=pltpu.VMEM((576, 512), BF),
    gm1=pltpu.VMEM((576, 512), BF),
    g1=pltpu.VMEM((576, 512), BF),
    merged=pltpu.VMEM((576, 512), BF),
    second=pltpu.VMEM((CELLS, 1024), BF),
    rolled2=pltpu.VMEM((CELLS, 1024), BF),
    qkv2=pltpu.VMEM((CELLS, 3072), BF),
    dqkv2=pltpu.VMEM((2, CELLS, 3072), BF),
    half2=pltpu.VMEM((2, CELLS, 512), BF),
    theirs2=pltpu.VMEM((CELLS, 512), BF),
    halft=pltpu.VMEM((2, 512, CELLS), BF),
    prob2=pltpu.VMEM((8, 288, CELLS), BF),
    mixed2=pltpu.VMEM((CELLS, 1024), BF),
    ct=pltpu.VMEM((CELLS, 1024), BF),
    gm2=pltpu.VMEM((CELLS, 1024), BF),
    res=pltpu.VMEM((CELLS, 1024), BF),
    gs=pltpu.VMEM((CELLS, 1024), BF),
    b2=pltpu.VMEM((3, 64, 64, 128), BF),
    b2r0=pltpu.VMEM((3, 3, 16, 64, 128), BF),
    b2r1=pltpu.VMEM((3, 3, 4, 64, 128), BF),
    b2r2=pltpu.VMEM((3, 3, 1, 64, 128), BF),
    b1=pltpu.VMEM((2, 3, 64, 16, 128), BF),
    b1c=pltpu.VMEM((3, 64, 16, 128), BF),
    b1r0=pltpu.VMEM((3, 3, 16, 16, 128), BF),
    b1r1=pltpu.VMEM((3, 3, 4, 16, 128), BF),
    b1r2=pltpu.VMEM((3, 3, 1, 16, 128), BF),
    load_sem=pltpu.SemaphoreType.DMA((len(LOADS),)),
    halo_send=pltpu.SemaphoreType.DMA((18,)),
    halo_recv=pltpu.SemaphoreType.DMA((18,)),
    rs_send=pltpu.SemaphoreType.DMA((54,)),
    rs_recv=pltpu.SemaphoreType.DMA((54,)),
    core_send=pltpu.SemaphoreType.DMA((3,)),
    core_recv=pltpu.SemaphoreType.DMA((3,)),
)
SMALL = ("index", "seen", "mask", "table", "gain1", "gain2")
OUTPUTS = ("o_res", "o_tok", "o_q1", "o_q2")

ORDERS = (("z", "x", "y"), ("x", "y", "z"), ("y", "z", "x"))


def body(sizes, *refs):
    n_lon, n_lat = sizes
    names = ["in_" + n for n in LOADS + SMALL] + list(OUTPUTS) + list(SCRATCH)
    R = SimpleNamespace(**dict(zip(names, refs, strict=True)))

    e = lax.axis_index("lon")
    d = lax.axis_index("lat")
    core, xh, z = lax.rem(e, 2), lax.rem(e // 2, 2), e // 4
    xl, y = lax.rem(d, 2), d // 2
    x = xh * 2 + xl
    place = dict(x=x, y=y, z=z)
    e_up, e_dn = lax.rem(e + 1, n_lon), lax.rem(e + n_lon - 1, n_lon)
    d_up, d_dn = lax.rem(d + 1, n_lat), lax.rem(d + n_lat - 1, n_lat)
    last = d == n_lat - 1
    ahead = ((e_up, d), (e, d_up), (e_up, d_up))
    behind = ((e_dn, d), (e, d_dn), (e_dn, d_dn))
    other = (e + 1 - 2 * core, d)

    def device(x, y, z):
        return (z * 4 + (x // 2) * 2 + core, y * 2 + lax.rem(x, 2))

    def along(axis, k):
        at = dict(place)
        at[axis] = lax.rem(at[axis] + k, 4)
        return device(**at)

    loads = SimpleNamespace()
    for n, name in enumerate(LOADS):
        copy = pltpu.make_async_copy(getattr(R, "in_" + name), getattr(R, name), R.load_sem.at[n])
        copy.start()
        setattr(loads, name, copy)

    barrier = pltpu.get_barrier_semaphore()
    partners = list(ahead) + list(behind) + [other]
    for axis in place:
        for k in (1, 2, 3):
            partners.append(along(axis, k))
    for who in partners:
        pl.semaphore_signal(barrier, inc=1, device_id=who, device_id_type=MESH)
    pl.semaphore_wait(barrier, len(partners))

    def exchange(n, segs, source, target, to):
        copies = []
        for k in range(3):
            start, size = segs[k + 1]
            rows = pl.ds(start, size)
            copies.append(pltpu.make_async_remote_copy(
                src_ref=source.at[pl.ds(start - segs[0][1], size)],
                dst_ref=target.at[rows],
                send_sem=R.halo_send.at[3 * n + k],
                recv_sem=R.halo_recv.at[3 * n + k],
                device_id=to[k],
                device_id_type=MESH))
        for c in copies:
            c.start()
        return copies

    def wait(copies):
        for c in copies:
            c.wait()

    def take(key, start, size, columns):
        n = list(INDEX).index(key)
        col = R.in_index[pl.ds(start, size), n:n + 1]
        hit = col == lax.broadcasted_iota(jnp.int32, (size, columns), 1)
        return jnp.where(hit, 1.0, 0.0).astype(BF)

    row = lax.broadcasted_iota(jnp.int32, (576, 24), 0)
    col = lax.broadcasted_iota(jnp.int32, (576, 24), 1)
    per = nn(jnp.where(row // 24 == col, 1.0, 0.0).astype(BF), R.in_seen[...].astype(F32).astype(BF))
    present = jnp.sum(jnp.where(lax.rem(row, 24) == col, per, 0.0), axis=-1, keepdims=True) > 0.5

    loads.first.wait()
    R.first[...] = jnp.where(present, R.first[...].astype(F32), R.in_mask[...].astype(BF).astype(F32)).astype(BF)
    R.xs[0] = nn(take("s1", 336, 272, 576), R.first[...]).astype(BF)
    halo0 = exchange(0, SEG1, R.xs.at[0], R.xr.at[0], behind)
    R.xr[0, 0:336] = nn(take("s1", 0, 336, 576), R.first[...]).astype(BF)
    loads.cot.wait()
    R.cs[0] = nn(take("sc", 48, 144, CELLS), R.cot[...]).astype(BF)
    halo_c = exchange(4, SEG2, R.cs.at[0], R.cr.at[0], behind)
    R.cr[0, 0:48] = nn(take("sc", 0, 48, CELLS), R.cot[...]).astype(BF)

    table = R.in_table[...]
    high = table.astype(BF).astype(F32)
    mid = (table - high).astype(BF).astype(F32)
    low = table - high - mid
    parts = jnp.concatenate([high, mid, low], axis=0).astype(BF)
    R.parts[...] = nn(parts, take("flip", 0, 768, 768))
    picked = take("pick", 0, 768, 264)
    for v in range(2):
        for l in range(12):
            shift = (1 - v) * 23 + 11 - l
            moved = pltpu.roll(R.parts[...], (768 - shift) % 768, 1) if shift else R.parts[...]
            got = nn(moved.astype(BF), picked)
            R.ext[:, v * 12 + l, :] = got[0:24] + got[24:48] + got[48:72]
    rows = lax.broadcasted_iota(jnp.int32, (CELLS, CELLS), 0)
    cols = lax.broadcasted_iota(jnp.int32, (CELLS, CELLS), 1)
    apart = jnp.logical_xor(rows < HALF, cols < HALF)
    apart_add = jnp.where(apart, NEG, 0.0).astype(F32) * jnp.where(last, 1.0, 0.0).astype(F32)
    R.madd[0] = jnp.zeros((CELLS, CELLS), F32)
    R.madd[1] = apart_add

    def expand(h):
        for a in range(6):
            piece = R.ext[h, :, (5 - a) * 24:(5 - a) * 24 + CELLS]
            R.bias[h, a * 24:(a + 1) * 24, :] = piece

    def expand_masked(h):
        expand(8 + h)
        R.bias[8 + h] = R.bias[8 + h] + R.madd[1]

    loop(8, expand)

    lane = lax.broadcasted_iota(jnp.int32, (1, 128), 1)
    left = jnp.where(lane < 64, 1.0, 0.0).astype(BF)
    right = jnp.where(lane < 64, 0.0, 1.0).astype(BF)
    is_left = lax.broadcasted_iota(jnp.int32, (CELLS, 128), 1) < 64

    def stack(t):
        return jnp.concatenate([t * left, t * right], axis=0)

    def attend(qkv, prob, mixed, unit, rows, pair, width, bias):
        at = lambda part: pl.ds(pl.multiple_of(part * width + pair * 128, 128), 128)
        q = qkv[rows, at(0)] * BF(0.125)
        k = qkv[rows, at(1)]
        v = qkv[rows, at(2)]
        score = nt(stack(q), k) + bias
        top = jnp.max(score, axis=-1, keepdims=True)
        expo = jnp.exp(score - top)
        p = (expo * (1.0 / jnp.sum(expo, axis=-1, keepdims=True))).astype(BF)
        prob[unit] = p
        o = nn(p, v)
        mixed[rows, at(0)] = jnp.where(is_left, o[:CELLS], o[CELLS:]).astype(BF)

    def attend_back(qkv, prob, grad, out, unit, rows, pair, width):
        at = lambda part: pl.ds(pl.multiple_of(part * width + pair * 128, 128), 128)
        q = qkv[rows, at(0)] * BF(0.125)
        k = qkv[rows, at(1)]
        v = qkv[rows, at(2)]
        go = stack(grad[rows, at(0)])
        pb = prob[unit]
        p = pb.astype(F32)
        gw = nt(go, v)
        gs = (p * (gw - jnp.sum(p * gw, axis=-1, keepdims=True))).astype(BF)
        gq = nn(gs, k)
        out[rows, at(0)] = (jnp.where(is_left, gq[:CELLS], gq[CELLS:]) * 0.125).astype(BF)
        out[rows, at(1)] = tn(gs, stack(q)).astype(BF)
        out[rows, at(2)] = tn(pb, go).astype(BF)

    wait(halo0)
    gain1 = R.in_gain1[...]

    def norm1(w):
        rows = pl.ds(pl.multiple_of(w * CELLS, 16), CELLS)
        t = nn(take("r1", pl.multiple_of(w * CELLS, 16), CELLS, 608), R.xr[0])
        R.x1[rows, :] = t.astype(BF)
        dev, inv = norm_stats(t)
        R.rolled1[rows, :] = (dev * inv * gain1).astype(BF)

    loop(4, norm1)
    loads.w1.wait()

    def qkv1(n):
        c = pl.ds(pl.multiple_of(n * 256, 256), 256)
        R.qkv1[:, c] = nn(R.rolled1[...], R.w1[:, c]).astype(BF)

    loop(6, qkv1)

    def fwd1(u):
        pair, w = u // 4, lax.rem(u, 4)
        rows = pl.ds(pl.multiple_of(w * CELLS, 16), CELLS)
        bias = R.bias[pl.ds(pair * 2, 2)] + R.madd[lax.rem(w, 2)][None]
        attend(R.qkv1, R.prob1, R.mixed1, u, rows, pair, 512, bias.reshape(288, CELLS))

    loop(16, fwd1)
    loads.p1.wait()

    def proj1(w):
        rows = pl.ds(pl.multiple_of(w * CELLS, 16), CELLS)
        branch = nn(R.mixed1[rows, :], R.p1[...]).astype(BF).astype(F32)
        R.out1[rows, :] = (R.x1[rows, :].astype(F32) + branch).astype(BF)

    loop(4, proj1)

    R.xs[1] = nn(take("s2", 336, 272, 576), R.out1[...]).astype(BF)
    halo1 = exchange(1, SEG1, R.xs.at[1], R.xr.at[1], behind)
    R.xr[1, 0:336] = nn(take("s2", 0, 336, 576), R.out1[...]).astype(BF)
    loop(16, expand_masked)
    wait(halo_c)
    R.ct[...] = nn(take("rc", 0, CELLS, 192), R.cr[0]).astype(BF)
    loads.p2.wait()

    def grad_mixed2(n):
        c = pl.ds(pl.multiple_of(n * 256, 256), 256)
        R.gm2[:, c] = nt(R.ct[...], R.p2[c, :]).astype(BF)

    loop(4, grad_mixed2)
    R.rolled1t[...] = R.rolled1[...].T
    wait(halo1)
    R.merged[...] = nn(take("r2", 0, 576, 608), R.xr[1]).astype(BF)
    loads.wm.wait()
    acc = nn(R.merged[0:CELLS, :], R.wm[0:512, :])
    for s in range(1, 4):
        acc = acc + nn(R.merged[s * CELLS:(s + 1) * CELLS, :], R.wm[s * 512:(s + 1) * 512, :])
    second = acc.astype(BF)
    R.second[...] = second
    gain2 = R.in_gain2[...]
    dev, inv = norm_stats(second.astype(F32))
    rolled2 = (dev * inv * gain2).astype(BF)
    R.rolled2[...] = rolled2
    loads.w2.wait()

    def qkv2(n):
        c = pl.ds(pl.multiple_of(n * 512, 512), 512)
        R.qkv2[:, c] = nn(R.rolled2[...], R.w2[:, c]).astype(BF)

    loop(6, qkv2)

    r2f = rolled2.astype(F32)
    for t in range(4):
        a = r2f[:, t * 256:t * 256 + 128]
        b = r2f[:, t * 256 + 128:t * 256 + 256]
        c = slice(t * 128, t * 128 + 128)
        R.half2[0, :, c] = jnp.where(is_left, a, pltpu.roll(b, 64, 1)).astype(BF)
        R.half2[1, :, c] = jnp.where(is_left, pltpu.roll(a, 64, 1), b).astype(BF)
    core0 = pltpu.make_async_remote_copy(
        src_ref=R.half2.at[1 - core], dst_ref=R.theirs2, send_sem=R.core_send.at[0],
        recv_sem=R.core_recv.at[0], device_id=other, device_id_type=MESH)
    core0.start()

    everyrow = pl.ds(0, CELLS)

    def fwd2(u):
        bias = R.bias[pl.ds(8 + u * 2, 2)].reshape(288, CELLS)
        attend(R.qkv2, R.prob2, R.mixed2, u, everyrow, u, 1024, bias)
        attend_back(R.qkv2, R.prob2, R.gm2, R.dqkv2.at[0], u, everyrow, u, 1024)

    loop(8, fwd2)
    core1 = pltpu.make_async_remote_copy(
        src_ref=R.dqkv2.at[0], dst_ref=R.dqkv2.at[1], send_sem=R.core_send.at[1],
        recv_sem=R.core_recv.at[1], device_id=other, device_id_type=MESH)
    core1.start()

    grad_rolled = nt(R.dqkv2[0, :, 0:1024], R.w2[:, 0:1024])
    grad_rolled = grad_rolled + nt(R.dqkv2[0, :, 1024:2048], R.w2[:, 1024:2048])
    grad_rolled = grad_rolled + nt(R.dqkv2[0, :, 2048:3072], R.w2[:, 2048:3072])

    def norm_back(grad, xin, gain, grad_out):
        grad = grad.astype(BF).astype(F32) * gain
        dev, inv = norm_stats(xin.astype(F32))
        hat = dev * inv
        inner = inv * (grad - jnp.mean(grad, axis=-1, keepdims=True)
                       - hat * jnp.mean(grad * hat, axis=-1, keepdims=True))
        return (grad_out.astype(F32) + inner.astype(BF).astype(F32)).astype(BF)

    R.gs[...] = norm_back(grad_rolled, R.second[...], gain2, R.ct[...])
    for s in range(4):
        R.merged[s * CELLS:(s + 1) * CELLS, :] = nt(R.gs[...], R.wm[s * 512:(s + 1) * 512, :]).astype(BF)
    R.xs[2] = nn(take("s3", 336, 272, 576), R.merged[...]).astype(BF)
    halo2 = exchange(2, SEG1, R.xs.at[2], R.xr.at[2], ahead)
    R.xr[2, 0:336] = nn(take("s3", 0, 336, 576), R.merged[...]).astype(BF)

    branch = nn(R.mixed2[...], R.p2[...]).astype(BF).astype(F32)
    R.res[...] = (R.second[...].astype(F32) + branch).astype(BF)
    R.cs[1] = nn(take("sr", 48, 144, CELLS), R.res[...]).astype(BF)
    halo_r = exchange(5, SEG2, R.cs.at[1], R.cr.at[1], ahead)
    R.cr[1, 0:48] = nn(take("sr", 0, 48, CELLS), R.res[...]).astype(BF)

    R.halft[0] = R.half2[core].T
    core0.wait()
    R.halft[1] = R.theirs2[...].T
    core1.wait()

    def term2(t):
        c = pl.ds(pl.multiple_of(t * 384, 128), 384)
        g = nn(R.halft[0], R.dqkv2[0, :, c]) + nn(R.halft[1], R.dqkv2[1, :, c])
        g = g.astype(BF)
        yy, xx = t // 2, lax.rem(t, 2)
        for zz in range(4):
            for hh in range(2):
                r = (zz * 2 + hh) * 64
                at = dict(z=zz, x=hh * 2 + xx, y=yy)
                for p, order in enumerate(ORDERS):
                    block = (at[order[0]] * 4 + at[order[1]]) * 4 + at[order[2]]
                    R.b2[p, block] = g[r:r + 64, p * 128:(p + 1) * 128]

    loop(8, term2)

    def rs_start(buf, recv, sem0, step):
        copies = []
        for p, order in enumerate(ORDERS):
            base = 0
            for s in range(step):
                base = base + place[order[s]] * (16 >> (2 * s))
            size = 16 >> (2 * step)
            axis = order[step]
            for k in (1, 2, 3):
                to = lax.rem(place[axis] + k, 4)
                n = sem0 + (step * 3 + p) * 3 + k - 1
                copies.append(pltpu.make_async_remote_copy(
                    src_ref=buf.at[p, pl.ds(base + to * size, size)],
                    dst_ref=recv.at[p, k - 1],
                    send_sem=R.rs_send.at[n],
                    recv_sem=R.rs_recv.at[n],
                    device_id=along(axis, k),
                    device_id_type=MESH))
        for c in copies:
            c.start()
        return copies

    def rs_add(buf, recv, step, copies):
        wait(copies)
        size = 16 >> (2 * step)
        for p, order in enumerate(ORDERS):
            base = 0
            for s in range(step + 1):
                base = base + place[order[s]] * (16 >> (2 * s))

            def add(b):
                t = buf[p, base + b].astype(F32) + recv[p, 0, b].astype(F32)
                t = t + recv[p, 1, b].astype(F32) + recv[p, 2, b].astype(F32)
                buf[p, base + b] = t.astype(BF)

            loop(size, add)

    def rs_last(buf, recv, p, copies):
        order = ORDERS[p]
        base = (place[order[0]] * 4 + place[order[1]]) * 4 + place[order[2]]
        t = buf[p, base].astype(F32) + recv[p, 0, 0].astype(F32)
        return t + recv[p, 1, 0].astype(F32) + recv[p, 2, 0].astype(F32)

    big = rs_start(R.b2, R.b2r0, 0, 0)

    wait(halo2)
    R.g1[...] = nn(take("r3", 0, 576, 608), R.xr[2]).astype(BF)

    def grad_mixed1(w):
        rows = pl.ds(pl.multiple_of(w * CELLS, 16), CELLS)
        R.gm1[rows, :] = nt(R.g1[rows, :], R.p1[...]).astype(BF)

    loop(4, grad_mixed1)

    def bwd1(u):
        pair, w = u // 4, lax.rem(u, 4)
        rows = pl.ds(pl.multiple_of(w * CELLS, 16), CELLS)
        attend_back(R.qkv1, R.prob1, R.gm1, R.dqkv1, u, rows, pair, 512)

    loop(16, bwd1)

    def term1(t):
        c = pl.ds(pl.multiple_of(t * 384, 128), 384)
        g = nn(R.rolled1t[...], R.dqkv1[:, c])
        for zz in range(4):
            for hh in range(2):
                for cc in range(2):
                    r = ((zz * 2 + hh) * 2 + cc) * 32
                    upper = g[r:r + 16, 128:256]
                    lower = pltpu.roll(g[r + 16:r + 32, 128:256], 64, 1)
                    pick = is_left[0:16]
                    mixes = (jnp.where(pick, upper, lower), jnp.where(pick, lower, upper))
                    for odd in range(2):
                        at = dict(z=zz, x=hh * 2 + odd, y=t)
                        lanes = slice(odd * 256, odd * 256 + 128)
                        pieces = (g[r:r + 16, lanes], g[r + 16:r + 32, lanes], mixes[odd])
                        for p, order in enumerate(ORDERS):
                            block = (at[order[0]] * 4 + at[order[1]]) * 4 + at[order[2]]
                            R.b1[cc, p, block] = pieces[p].astype(BF)

    loop(4, term1)
    core2 = pltpu.make_async_remote_copy(
        src_ref=R.b1.at[1 - core], dst_ref=R.b1c, send_sem=R.core_send.at[2],
        recv_sem=R.core_recv.at[2], device_id=other, device_id_type=MESH)
    core2.start()
    rs_add(R.b2, R.b2r0, 0, big)
    big = rs_start(R.b2, R.b2r1, 0, 1)

    core2.wait()
    mine = R.b1.at[core]

    def add_core(b):
        for p in range(3):
            mine[p, b] = (mine[p, b].astype(F32) + R.b1c[p, b].astype(F32)).astype(BF)

    loop(64, add_core)
    small = rs_start(mine, R.b1r0, 27, 0)

    def tail1(w):
        rows = pl.ds(pl.multiple_of(w * CELLS, 16), CELLS)
        grad = nt(R.dqkv1[rows, :], R.w1[...])
        R.out1[rows, :] = norm_back(grad, R.x1[rows, :], gain1, R.g1[rows, :])

    loop(4, tail1)
    R.xs[3] = nn(take("s4", 336, 272, 576), R.out1[...]).astype(BF)
    halo3 = exchange(3, SEG1, R.xs.at[3], R.xr.at[3], ahead)
    R.xr[3, 0:336] = nn(take("s4", 0, 336, 576), R.out1[...]).astype(BF)

    rs_add(mine, R.b1r0, 0, small)
    small = rs_start(mine, R.b1r1, 27, 1)
    rs_add(R.b2, R.b2r1, 1, big)
    big = rs_start(R.b2, R.b2r2, 0, 2)
    wait(halo_r)
    R.o_res[...] = nn(take("rr", 0, CELLS, 192), R.cr[1]).astype(BF)
    rs_add(mine, R.b1r1, 1, small)
    small = rs_start(mine, R.b1r2, 27, 2)
    wait(halo3)
    R.o_tok[...] = jnp.where(present, nn(take("r4", 0, 576, 608), R.xr[3]), 0.0).astype(BF)
    wait(big)
    for p in range(3):
        R.o_q2[:, p * 128:(p + 1) * 128] = rs_last(R.b2, R.b2r2, p, big)
    wait(small)
    a, b, m = [rs_last(mine, R.b1r2, p, small) for p in range(3)]
    turned = pltpu.roll(m, 64, 1)
    even = xl == 0
    a_turned = pltpu.roll(a, 64, 1)
    b_turned = pltpu.roll(b, 64, 1)
    pick = is_left[0:16]
    R.o_q1[0:16, 0:128] = jnp.where(even, a, jnp.where(pick, turned, a_turned))
    R.o_q1[16:32, 0:128] = jnp.where(even, b, jnp.where(pick, m, b_turned))
    R.o_q1[0:16, 128:192] = jnp.where(even, m, a_turned)[:, 0:64]
    R.o_q1[16:32, 128:192] = jnp.where(even, turned, b_turned)[:, 0:64]


def shards(tokens, observed, mask_token, gain_one, qkv_one, table_one, proj_one, merge_weight, gain_two, qkv_two,
           table_two, proj_two, cotangent, sizes):
    first = tokens.transpose(0, 2, 1, 3).reshape(576, 512)
    cot = cotangent.transpose(1, 2, 0, 3).reshape(CELLS, 1024)
    seen = observed.transpose(0, 2, 1).reshape(24, 24)
    table = jnp.pad(jnp.concatenate([table_one, table_two], axis=0), ((0, 0), (0, 9)))
    given = dict(first=first, cot=cot, w1=qkv_one, p1=proj_one, wm=merge_weight, w2=qkv_two, p2=proj_two)
    args = [given[k] for k in LOADS]
    args += [jnp.asarray(TABLE_OF), seen, mask_token[None], table, gain_one[None], gain_two[None]]
    res, tok, q1, q2 = pl.pallas_call(
        functools.partial(body, sizes),
        out_shape=(
            jax.ShapeDtypeStruct((CELLS, 1024), BF),
            jax.ShapeDtypeStruct((576, 512), BF),
            jax.ShapeDtypeStruct((32, 192), F32),
            jax.ShapeDtypeStruct((64, 384), F32),
        ),
        in_specs=[pl.BlockSpec(memory_space=pl.ANY)] * len(LOADS) + [pl.BlockSpec(memory_space=pltpu.VMEM)] * len(SMALL),
        out_specs=[pl.BlockSpec(memory_space=pltpu.VMEM)] * 4,
        scratch_shapes=list(SCRATCH.values()),
        compiler_params=pltpu.CompilerParams(
            collective_id=0, has_side_effects=True, vmem_limit_bytes=62 * 1024 * 1024),
        cost_estimate=pl.CostEstimate(flops=9 * 10 ** 9, bytes_accessed=24 * 10 ** 6, transcendentals=10 ** 6),
    )(*args)
    result = res.reshape(12, 6, 2, 1024).transpose(2, 0, 1, 3)
    grad_tokens = tok.reshape(2, 12, 24, 512).transpose(0, 2, 1, 3)
    return (result, grad_tokens, q1, q2)


def solution(mesh):
    sizes = (mesh.shape["lon"], mesh.shape["lat"])
    split = P(None, "lon", "lat", None)

    def run(*args):
        return shards(*args, sizes)

    return jax.shard_map(
        run,
        mesh=mesh,
        in_specs=(split, P(None, "lon", "lat")) + (P(),) * 10 + (split,),
        out_specs=(split, split, P("lon", "lat"), P("lon", "lat")),
        check_vma=False,
    )
```

```python
import functools
from types import SimpleNamespace
import numpy as np
import jax
import jax.numpy as jnp
from jax import lax
from jax.experimental import pallas as pl
from jax.experimental.pallas import tpu as pltpu
from jax.sharding import PartitionSpec as P

BF = jnp.bfloat16
F32 = jnp.float32
EPS = 1e-05
NEG = -1000000000.0
MESH = pl.DeviceIdType.MESH
CELLS = 144
HALF = 72

SEG1 = ((0, 336), (336, 112), (448, 112), (560, 48))
SEG2 = ((0, 48), (48, 48), (96, 48), (144, 48))


def _cells(along, across, half_lon, half_lat):
    out = [[], [], [], []]
    for v in range(2):
        for i in range(along):
            for j in range(across):
                seg = (1 if i < half_lon else 0) + (2 if j < half_lat else 0)
                moved = (v, (i - half_lon) % along, (j - half_lat) % across)
                out[seg].append(((v, i, j), moved))
    return out


def _send_index(segs, cells, row_of):
    out = [-1] * (segs[-1][0] + segs[-1][1])
    for (start, _), members in zip(segs, cells):
        for n, (cell, _) in enumerate(members):
            out[start + n] = row_of(*cell)
    return out


def _recv_index(segs, cells, row_of, rows):
    out = [-1] * rows
    for (start, _), members in zip(segs, cells):
        for n, (_, moved) in enumerate(members):
            out[row_of(*moved)] = start + n
    return out


def _inverse(index, rows):
    out = [-1] * rows
    for n, m in enumerate(index):
        if m >= 0:
            out[m] = n
    return out


def _nat1(v, i, j):
    return (v * 12 + j) * 24 + i


def _win1(v, i, j):
    return ((i // 12) * 2 + j // 6) * CELLS + (j % 6) * 24 + v * 12 + i % 12


def _merge(v, i, j):
    return ((i % 2) * 2 + j % 2) * CELLS + (j // 2) * 24 + v * 12 + i // 2


def _nat2(v, i, j):
    return (i * 6 + j) * 2 + v


def _win2(v, i, j):
    return j * 24 + v * 12 + i


def _indices():
    one = _cells(24, 12, 6, 3)
    two = _cells(12, 6, 6, 3)
    s1 = _send_index(SEG1, one, _nat1)
    r1 = _recv_index(SEG1, one, _win1, 576)
    s2 = _send_index(SEG1, one, _win1)
    r2 = _recv_index(SEG1, one, _merge, 576)
    sc = _send_index(SEG2, two, _nat2)
    rc = _recv_index(SEG2, two, _win2, CELLS)
    flip = [-1] * 768
    for x in range(3):
        for y in range(23):
            for z in range(11):
                flip[(x * 23 + y) * 11 + z] = z * 69 + x * 23 + y
    pick = [-1] * 768
    for z in range(11):
        for v in range(2):
            for l in range(12):
                pick[z * 69 + v * 23 + l] = z * 24 + v * 12 + l
    return dict(s1=s1, r1=r1, s2=s2, r2=r2, s3=_inverse(r2, 608), r3=_inverse(s2, 576), s4=_inverse(r1, 608),
                r4=_inverse(s1, 576), sc=sc, rc=rc, sr=_inverse(rc, 192), rr=_inverse(sc, CELLS), flip=flip, pick=pick)


INDEX = _indices()
TABLE_OF = np.full((768, len(INDEX)), -1, np.int32)
for _n, _rows in enumerate(INDEX.values()):
    TABLE_OF[:len(_rows), _n] = _rows

SHAPES = dict(first=(576, 512), cot=(72, 2, 1024), w1=(512, 1536), p1=(512, 512), p2=(1024, 1024),
              wm=(2048, 1024), w2=(1024, 3072))
LOADS = tuple(SHAPES)


def nn(a, b):
    return lax.dot_general(a, b, (((1,), (0,)), ((), ())), preferred_element_type=F32)


def nt(a, b):
    return lax.dot_general(a, b, (((1,), (1,)), ((), ())), preferred_element_type=F32)


def tn(a, b):
    return lax.dot_general(a, b, (((0,), (0,)), ((), ())), preferred_element_type=F32)


def norm_stats(x):
    centre = jnp.mean(x, axis=-1, keepdims=True)
    dev = x - centre
    spread = jnp.mean(dev * dev, axis=-1, keepdims=True)
    return dev, lax.rsqrt(spread + EPS)


def loop(n, body):
    lax.fori_loop(0, n, lambda i, c: (body(i), c)[1], 0)


SCRATCH = dict(
    {k: pltpu.VMEM(SHAPES[k], BF) for k in LOADS},
    mats=pltpu.VMEM((608, 576), BF),
    matr=pltpu.VMEM((576, 608), BF),
    tables=pltpu.VMEM((24, 768), F32),
    shifted=pltpu.VMEM((1152, 768), F32),
    ext=pltpu.VMEM((24, 24, 264), F32),
    bias=pltpu.VMEM((12, CELLS, 288), F32),
    madd=pltpu.VMEM((CELLS, 288), F32),
    xr=pltpu.VMEM((4, 608, 512), BF),
    xs=pltpu.VMEM((4, 272, 512), BF),
    cr=pltpu.VMEM((2, 192, 1024), BF),
    cs=pltpu.VMEM((2, 144, 1024), BF),
    x1=pltpu.VMEM((576, 512), BF),
    rolled1=pltpu.VMEM((576, 512), BF),
    rolled1t=pltpu.VMEM((512, 576), BF),
    qkv1=pltpu.VMEM((576, 1536), BF),
    dqkv1=pltpu.VMEM((576, 1536), BF),
    prob1=pltpu.VMEM((16, CELLS, 288), BF),
    mixed1=pltpu.VMEM((576, 512), BF),
    out1=pltpu.VMEM((576, 512), BF),
    gm1=pltpu.VMEM((576, 512), BF),
    g1=pltpu.VMEM((576, 512), BF),
    merged=pltpu.VMEM((576, 512), BF),
    second=pltpu.VMEM((CELLS, 1024), BF),
    rolled2=pltpu.VMEM((CELLS, 1024), BF),
    qkv2=pltpu.VMEM((CELLS, 3072), BF),
    dqkv2=pltpu.VMEM((2, CELLS, 3072), BF),
    half2=pltpu.VMEM((2, CELLS, 512), BF),
    theirs2=pltpu.VMEM((CELLS, 512), BF),
    halft=pltpu.VMEM((2, 512, CELLS), BF),
    mixed2=pltpu.VMEM((CELLS, 1024), BF),
    ct=pltpu.VMEM((CELLS, 1024), BF),
    gm2=pltpu.VMEM((CELLS, 1024), BF),
    res=pltpu.VMEM((CELLS, 1024), BF),
    gs=pltpu.VMEM((CELLS, 1024), BF),
    v_res=pltpu.VMEM((72, 2, 1024), BF),
    v_tok=pltpu.VMEM((576, 512), BF),
    v_q1=pltpu.VMEM((32, 192), F32),
    v_q2=pltpu.VMEM((64, 384), F32),
    out_sem=pltpu.SemaphoreType.DMA((4,)),
    b2=pltpu.VMEM((3, 64, 64, 128), BF),
    b2r0=pltpu.VMEM((3, 3, 16, 64, 128), BF),
    b2r1=pltpu.VMEM((3, 3, 4, 64, 128), BF),
    b2r2=pltpu.VMEM((3, 3, 1, 64, 128), BF),
    b1=pltpu.VMEM((2, 3, 64, 16, 128), BF),
    b1c=pltpu.VMEM((3, 64, 16, 128), BF),
    b1r0=pltpu.VMEM((3, 3, 16, 16, 128), BF),
    b1r1=pltpu.VMEM((3, 3, 4, 16, 128), BF),
    b1r2=pltpu.VMEM((3, 3, 1, 16, 128), BF),
    load_sem=pltpu.SemaphoreType.DMA((len(LOADS),)),
    halo_send=pltpu.SemaphoreType.DMA((18,)),
    halo_recv=pltpu.SemaphoreType.DMA((18,)),
    rs_send=pltpu.SemaphoreType.DMA((54,)),
    rs_recv=pltpu.SemaphoreType.DMA((54,)),
    core_send=pltpu.SemaphoreType.DMA((3,)),
    core_recv=pltpu.SemaphoreType.DMA((3,)),
)
SMALL = ("index", "seen", "mask", "table1", "table2", "gain1", "gain2")
OUTPUTS = ("o_res", "o_tok", "o_q1", "o_q2")

ORDERS = (("z", "x", "y"), ("x", "y", "z"), ("y", "z", "x"))


def body(sizes, *refs):
    n_lon, n_lat = sizes
    names = ["in_" + n for n in LOADS + SMALL] + list(OUTPUTS) + list(SCRATCH)
    R = SimpleNamespace(**dict(zip(names, refs, strict=True)))

    e = lax.axis_index("lon")
    d = lax.axis_index("lat")
    core, xh, z = lax.rem(e, 2), lax.rem(e // 2, 2), e // 4
    xl, y = lax.rem(d, 2), d // 2
    x = xh * 2 + xl
    place = dict(x=x, y=y, z=z)
    e_up, e_dn = lax.rem(e + 1, n_lon), lax.rem(e + n_lon - 1, n_lon)
    d_up, d_dn = lax.rem(d + 1, n_lat), lax.rem(d + n_lat - 1, n_lat)
    last = d == n_lat - 1
    ahead = ((e_up, d), (e, d_up), (e_up, d_up))
    behind = ((e_dn, d), (e, d_dn), (e_dn, d_dn))
    other = (e + 1 - 2 * core, d)

    def device(x, y, z):
        return (z * 4 + (x // 2) * 2 + core, y * 2 + lax.rem(x, 2))

    def along(axis, k):
        at = dict(place)
        at[axis] = lax.rem(at[axis] + k, 4)
        return device(**at)

    loads = SimpleNamespace()
    for n, name in enumerate(LOADS):
        copy = pltpu.make_async_copy(getattr(R, "in_" + name), getattr(R, name), R.load_sem.at[n])
        copy.start()
        setattr(loads, name, copy)

    barrier = pltpu.get_barrier_semaphore()
    partners = list(ahead) + list(behind) + [other]
    for axis in place:
        for k in (1, 2, 3):
            partners.append(along(axis, k))
    for who in partners:
        pl.semaphore_signal(barrier, inc=1, device_id=who, device_id_type=MESH)

    def exchange(n, segs, source, target, to):
        copies = []
        for k in range(3):
            start, size = segs[k + 1]
            rows = pl.ds(start, size)
            copies.append(pltpu.make_async_remote_copy(
                src_ref=source.at[pl.ds(start - segs[0][1], size)],
                dst_ref=target.at[rows],
                send_sem=R.halo_send.at[3 * n + k],
                recv_sem=R.halo_recv.at[3 * n + k],
                device_id=to[k],
                device_id_type=MESH))
        for c in copies:
            c.start()
        return copies

    def wait(copies):
        for c in copies:
            c.wait()

    def take(key, start, size, columns):
        n = list(INDEX).index(key)
        col = R.in_index[pl.ds(start, size), n:n + 1]
        hit = col == lax.broadcasted_iota(jnp.int32, (size, columns), 1)
        return jnp.where(hit, 1.0, 0.0).astype(BF)

    def put(n, name):
        copy = pltpu.make_async_copy(getattr(R, "v_" + name), getattr(R, "o_" + name), R.out_sem.at[n])
        copy.start()
        return copy

    seen = R.in_seen[...]
    seen = jnp.concatenate([seen[:, 0, :], seen[:, 1, :]], axis=0).astype(F32).astype(BF)
    row = lax.broadcasted_iota(jnp.int32, (576, 24), 0)
    col = lax.broadcasted_iota(jnp.int32, (576, 24), 1)
    per = nn(jnp.where(row // 24 == col, 1.0, 0.0).astype(BF), seen)
    present = jnp.sum(jnp.where(lax.rem(row, 24) == col, per, 0.0), axis=-1, keepdims=True) > 0.5

    R.mats[...] = take("s1", 0, 608, 576)
    loads.first.wait()
    R.first[...] = jnp.where(present, R.first[...].astype(F32), R.in_mask[...].astype(BF).astype(F32)).astype(BF)
    R.xs[0] = nn(R.mats[336:, :], R.first[...]).astype(BF)
    pl.semaphore_wait(barrier, len(partners))
    halo0 = exchange(0, SEG1, R.xs.at[0], R.xr.at[0], behind)
    R.xr[0, 0:336] = nn(R.mats[0:336, :], R.first[...]).astype(BF)
    loads.cot.wait()
    cot = R.cot[...].reshape(CELLS, 1024)
    R.cs[0] = nn(take("sc", 48, 144, CELLS), cot).astype(BF)
    halo_c = exchange(4, SEG2, R.cs.at[0], R.cr.at[0], behind)
    R.cr[0, 0:48] = nn(take("sc", 0, 48, CELLS), cot).astype(BF)
    R.matr[...] = take("r1", 0, 576, 608)
    R.mats[...] = take("s2", 0, 608, 576)

    R.tables[...] = jnp.zeros((24, 768), F32)
    R.tables[0:8, 0:759] = R.in_table1[...]
    R.tables[8:24, 0:759] = R.in_table2[...]
    table = R.tables[...]
    high = table.astype(BF).astype(F32)
    mid = (table - high).astype(BF).astype(F32)
    low = table - high - mid
    parts = jnp.concatenate([high, mid, low], axis=0).astype(BF)
    parts = nn(parts, take("flip", 0, 768, 768))
    picked = take("pick", 0, 768, 264)

    def extend(first, heads):
        part = jnp.concatenate([parts[24 * k + first:24 * k + first + heads] for k in range(3)], axis=0)
        for v in range(2):
            for l in range(12):
                shift = (1 - v) * 23 + 11 - l
                moved = pltpu.roll(part, (768 - shift) % 768, 1) if shift else part
                at = (v * 12 + l) * 3 * heads
                R.shifted[at:at + 3 * heads] = moved
        got = nn(R.shifted[0:72 * heads].astype(BF), picked)
        for n in range(24):
            at = n * 3 * heads
            R.ext[first:first + heads, n, :] = (
                got[at:at + heads] + got[at + heads:at + 2 * heads] + got[at + 2 * heads:at + 3 * heads])

    extend(0, 8)
    rows = lax.broadcasted_iota(jnp.int32, (CELLS, CELLS), 0)
    cols = lax.broadcasted_iota(jnp.int32, (CELLS, CELLS), 1)
    apart = jnp.where(jnp.logical_xor(rows < HALF, cols < HALF), NEG, 0.0).astype(F32)
    apart = apart * jnp.where(last, 1.0, 0.0).astype(F32)
    R.madd[...] = jnp.concatenate([apart, apart], axis=1)

    def expand(pair):
        one, two = R.ext[2 * pair], R.ext[2 * pair + 1]
        for a in range(6):
            at = slice((5 - a) * 24, (5 - a) * 24 + CELLS)
            R.bias[pair, a * 24:(a + 1) * 24, :] = jnp.concatenate([one[:, at], two[:, at]], axis=1)

    def expand_masked(pair):
        expand(4 + pair)
        R.bias[4 + pair] = R.bias[4 + pair] + R.madd[...]

    loop(4, expand)

    lane = lax.broadcasted_iota(jnp.int32, (1, 128), 1)
    left = jnp.where(lane < 64, 1.0, 0.0).astype(BF)
    right = jnp.where(lane < 64, 0.0, 1.0).astype(BF)
    is_left = lax.broadcasted_iota(jnp.int32, (CELLS, 128), 1) < 64

    def stack(t):
        return jnp.concatenate([t * left, t * right], axis=0)

    def at(part, pair, width):
        return pl.ds(pl.multiple_of(part * width + pair * 128, 128), 128)

    def heads_of(t):
        return jnp.where(is_left, t[:CELLS], t[CELLS:])

    def attend(q2, k, v, bias):
        score = [nt(b, a) + c for a, b, c in zip(q2, k, bias)]
        expo = [jnp.exp(t - jnp.max(t, axis=0, keepdims=True)) for t in score]
        p = [t * (1.0 / jnp.sum(t, axis=0, keepdims=True)) for t in expo]
        pb = [t.astype(BF) for t in p]
        o = [heads_of(tn(a, b)).astype(BF) for a, b in zip(pb, v)]
        return p, pb, o

    def attend_back(q2, k, v, p, pb, go):
        gw = [nt(a, b) for a, b in zip(v, go)]
        gs = [(a * (b - jnp.sum(a * b, axis=0, keepdims=True))).astype(BF) for a, b in zip(p, gw)]
        gv = [nn(a, b).astype(BF) for a, b in zip(pb, go)]
        gk = [nn(a, b).astype(BF) for a, b in zip(gs, q2)]
        gq = [(heads_of(tn(a, b)) * 0.125).astype(BF) for a, b in zip(gs, k)]
        return gq, gk, gv

    gain1 = R.in_gain1[...]
    wait(halo0)

    def norm1(w):
        rows = pl.ds(pl.multiple_of(w * CELLS, 16), CELLS)
        t = nn(R.matr[rows, :], R.xr[0])
        R.x1[rows, :] = t.astype(BF)
        dev, inv = norm_stats(t)
        R.rolled1[rows, :] = (dev * inv * gain1).astype(BF)

    loop(4, norm1)
    loads.w1.wait()

    def qkv1(n):
        c = pl.ds(pl.multiple_of(n * 256, 256), 256)
        R.qkv1[:, c] = nn(R.rolled1[...], R.w1[:, c]).astype(BF)

    loop(6, qkv1)

    def two_windows(u):
        pair, half = u // 2, lax.rem(u, 2)
        return pair, [pl.ds(pl.multiple_of((half * 2 + k) * CELLS, 16), CELLS) for k in range(2)]

    def fwd1(u):
        pair, rows = two_windows(u)
        q2 = [stack(R.qkv1[r, at(0, pair, 512)] * BF(0.125)) for r in rows]
        k = [R.qkv1[r, at(1, pair, 512)] for r in rows]
        v = [R.qkv1[r, at(2, pair, 512)] for r in rows]
        bias = R.bias[pair]
        _, pb, o = attend(q2, k, v, [bias, bias + R.madd[...]])
        for n in range(2):
            R.prob1[u * 2 + n] = pb[n]
            R.mixed1[rows[n], at(0, pair, 512)] = o[n]

    loop(8, fwd1)
    loads.p1.wait()

    def proj1(w):
        rows = pl.ds(pl.multiple_of(w * CELLS, 16), CELLS)
        branch = nn(R.mixed1[rows, :], R.p1[...]).astype(BF).astype(F32)
        R.out1[rows, :] = (R.x1[rows, :].astype(F32) + branch).astype(BF)

    loop(4, proj1)

    R.xs[1] = nn(R.mats[336:, :], R.out1[...]).astype(BF)
    halo1 = exchange(1, SEG1, R.xs.at[1], R.xr.at[1], behind)
    R.xr[1, 0:336] = nn(R.mats[0:336, :], R.out1[...]).astype(BF)
    extend(8, 16)
    loop(8, expand_masked)
    R.mats[...] = take("s3", 0, 608, 576)
    R.matr[...] = take("r2", 0, 576, 608)
    wait(halo_c)
    R.ct[...] = nn(take("rc", 0, CELLS, 192), R.cr[0]).astype(BF)
    loads.p2.wait()

    def grad_mixed2(n):
        c = pl.ds(pl.multiple_of(n * 256, 256), 256)
        R.gm2[:, c] = nt(R.ct[...], R.p2[c, :]).astype(BF)

    loop(4, grad_mixed2)
    R.rolled1t[...] = R.rolled1[...].T
    wait(halo1)
    R.merged[...] = nn(R.matr[...], R.xr[1]).astype(BF)
    loads.wm.wait()
    acc = nn(R.merged[0:CELLS, :], R.wm[0:512, :])
    for s in range(1, 4):
        acc = acc + nn(R.merged[s * CELLS:(s + 1) * CELLS, :], R.wm[s * 512:(s + 1) * 512, :])
    second = acc.astype(BF)
    R.second[...] = second
    gain2 = R.in_gain2[...]
    dev, inv = norm_stats(second.astype(F32))
    rolled2 = (dev * inv * gain2).astype(BF)
    R.rolled2[...] = rolled2
    loads.w2.wait()

    def qkv2(n):
        c = pl.ds(pl.multiple_of(n * 512, 512), 512)
        R.qkv2[:, c] = nn(R.rolled2[...], R.w2[:, c]).astype(BF)

    loop(6, qkv2)

    r2f = rolled2.astype(F32)
    for t in range(4):
        a = r2f[:, t * 256:t * 256 + 128]
        b = r2f[:, t * 256 + 128:t * 256 + 256]
        c = slice(t * 128, t * 128 + 128)
        R.half2[0, :, c] = jnp.where(is_left, a, pltpu.roll(b, 64, 1)).astype(BF)
        R.half2[1, :, c] = jnp.where(is_left, pltpu.roll(a, 64, 1), b).astype(BF)
    core0 = pltpu.make_async_remote_copy(
        src_ref=R.half2.at[1 - core], dst_ref=R.theirs2, send_sem=R.core_send.at[0],
        recv_sem=R.core_recv.at[0], device_id=other, device_id_type=MESH)
    core0.start()

    def both2(u):
        pairs = (u * 2, u * 2 + 1)
        q2 = [stack(R.qkv2[:, at(0, c, 1024)] * BF(0.125)) for c in pairs]
        k = [R.qkv2[:, at(1, c, 1024)] for c in pairs]
        v = [R.qkv2[:, at(2, c, 1024)] for c in pairs]
        go = [stack(R.gm2[:, at(0, c, 1024)]) for c in pairs]
        p, pb, o = attend(q2, k, v, [R.bias[4 + c] for c in pairs])
        back = attend_back(q2, k, v, p, pb, go)
        for n, c in enumerate(pairs):
            R.mixed2[:, at(0, c, 1024)] = o[n]
            for part in range(3):
                R.dqkv2[0, :, at(part, c, 1024)] = back[part][n]

    loop(4, both2)
    core1 = pltpu.make_async_remote_copy(
        src_ref=R.dqkv2.at[0], dst_ref=R.dqkv2.at[1], send_sem=R.core_send.at[1],
        recv_sem=R.core_recv.at[1], device_id=other, device_id_type=MESH)
    core1.start()

    grad_rolled = nt(R.dqkv2[0, :, 0:1024], R.w2[:, 0:1024])
    grad_rolled = grad_rolled + nt(R.dqkv2[0, :, 1024:2048], R.w2[:, 1024:2048])
    grad_rolled = grad_rolled + nt(R.dqkv2[0, :, 2048:3072], R.w2[:, 2048:3072])

    def norm_back(grad, xin, gain, grad_out):
        grad = grad.astype(BF).astype(F32) * gain
        dev, inv = norm_stats(xin.astype(F32))
        hat = dev * inv
        inner = inv * (grad - jnp.mean(grad, axis=-1, keepdims=True)
                       - hat * jnp.mean(grad * hat, axis=-1, keepdims=True))
        return (grad_out.astype(F32) + inner.astype(BF).astype(F32)).astype(BF)

    R.gs[...] = norm_back(grad_rolled, R.second[...], gain2, R.ct[...])
    for s in range(4):
        R.merged[s * CELLS:(s + 1) * CELLS, :] = nt(R.gs[...], R.wm[s * 512:(s + 1) * 512, :]).astype(BF)
    R.xs[2] = nn(R.mats[336:, :], R.merged[...]).astype(BF)
    halo2 = exchange(2, SEG1, R.xs.at[2], R.xr.at[2], ahead)
    R.xr[2, 0:336] = nn(R.mats[0:336, :], R.merged[...]).astype(BF)

    R.mats[...] = take("s4", 0, 608, 576)
    R.matr[...] = take("r3", 0, 576, 608)

    branch = nn(R.mixed2[...], R.p2[...]).astype(BF).astype(F32)
    R.res[...] = (R.second[...].astype(F32) + branch).astype(BF)
    R.cs[1] = nn(take("sr", 48, 144, CELLS), R.res[...]).astype(BF)
    halo_r = exchange(5, SEG2, R.cs.at[1], R.cr.at[1], ahead)
    R.cr[1, 0:48] = nn(take("sr", 0, 48, CELLS), R.res[...]).astype(BF)

    R.halft[0] = R.half2[core].T
    core0.wait()
    R.halft[1] = R.theirs2[...].T
    core1.wait()

    def term2(t):
        c = pl.ds(pl.multiple_of(t * 384, 128), 384)
        g = nn(R.halft[0], R.dqkv2[0, :, c]) + nn(R.halft[1], R.dqkv2[1, :, c])
        g = g.astype(BF)
        yy, xx = t // 2, lax.rem(t, 2)
        for zz in range(4):
            for hh in range(2):
                r = (zz * 2 + hh) * 64
                at = dict(z=zz, x=hh * 2 + xx, y=yy)
                for p, order in enumerate(ORDERS):
                    block = (at[order[0]] * 4 + at[order[1]]) * 4 + at[order[2]]
                    R.b2[p, block] = g[r:r + 64, p * 128:(p + 1) * 128]

    loop(8, term2)

    def rs_start(buf, recv, sem0, step):
        copies = []
        for p, order in enumerate(ORDERS):
            base = 0
            for s in range(step):
                base = base + place[order[s]] * (16 >> (2 * s))
            size = 16 >> (2 * step)
            axis = order[step]
            for k in (1, 2, 3):
                to = lax.rem(place[axis] + k, 4)
                n = sem0 + (step * 3 + p) * 3 + k - 1
                copies.append(pltpu.make_async_remote_copy(
                    src_ref=buf.at[p, pl.ds(base + to * size, size)],
                    dst_ref=recv.at[p, k - 1],
                    send_sem=R.rs_send.at[n],
                    recv_sem=R.rs_recv.at[n],
                    device_id=along(axis, k),
                    device_id_type=MESH))
        for c in copies:
            c.start()
        return copies

    def rs_add(buf, recv, step, copies):
        wait(copies)
        size = 16 >> (2 * step)
        for p, order in enumerate(ORDERS):
            base = 0
            for s in range(step + 1):
                base = base + place[order[s]] * (16 >> (2 * s))

            def add(b):
                t = buf[p, base + b].astype(F32) + recv[p, 0, b].astype(F32)
                t = t + recv[p, 1, b].astype(F32) + recv[p, 2, b].astype(F32)
                buf[p, base + b] = t.astype(BF)

            loop(size, add)

    def rs_last(buf, recv, p, copies):
        order = ORDERS[p]
        base = (place[order[0]] * 4 + place[order[1]]) * 4 + place[order[2]]
        t = buf[p, base].astype(F32) + recv[p, 0, 0].astype(F32)
        return t + recv[p, 1, 0].astype(F32) + recv[p, 2, 0].astype(F32)

    big = rs_start(R.b2, R.b2r0, 0, 0)

    wait(halo2)
    R.g1[...] = nn(R.matr[...], R.xr[2]).astype(BF)

    def grad_mixed1(w):
        rows = pl.ds(pl.multiple_of(w * CELLS, 16), CELLS)
        R.gm1[rows, :] = nt(R.g1[rows, :], R.p1[...]).astype(BF)

    loop(4, grad_mixed1)

    def bwd1(u):
        pair, rows = two_windows(u)
        q2 = [stack(R.qkv1[r, at(0, pair, 512)] * BF(0.125)) for r in rows]
        k = [R.qkv1[r, at(1, pair, 512)] for r in rows]
        v = [R.qkv1[r, at(2, pair, 512)] for r in rows]
        go = [stack(R.gm1[r, at(0, pair, 512)]) for r in rows]
        pb = [R.prob1[u * 2 + n] for n in range(2)]
        back = attend_back(q2, k, v, [t.astype(F32) for t in pb], pb, go)
        for n in range(2):
            for part in range(3):
                R.dqkv1[rows[n], at(part, pair, 512)] = back[part][n]

    loop(8, bwd1)

    def term1(t):
        c = pl.ds(pl.multiple_of(t * 384, 128), 384)
        g = nn(R.rolled1t[...], R.dqkv1[:, c])
        for zz in range(4):
            for hh in range(2):
                for cc in range(2):
                    r = ((zz * 2 + hh) * 2 + cc) * 32
                    upper = g[r:r + 16, 128:256]
                    lower = pltpu.roll(g[r + 16:r + 32, 128:256], 64, 1)
                    pick = is_left[0:16]
                    mixes = (jnp.where(pick, upper, lower), jnp.where(pick, lower, upper))
                    for odd in range(2):
                        at = dict(z=zz, x=hh * 2 + odd, y=t)
                        lanes = slice(odd * 256, odd * 256 + 128)
                        pieces = (g[r:r + 16, lanes], g[r + 16:r + 32, lanes], mixes[odd])
                        for p, order in enumerate(ORDERS):
                            block = (at[order[0]] * 4 + at[order[1]]) * 4 + at[order[2]]
                            R.b1[cc, p, block] = pieces[p].astype(BF)

    loop(4, term1)
    core2 = pltpu.make_async_remote_copy(
        src_ref=R.b1.at[1 - core], dst_ref=R.b1c, send_sem=R.core_send.at[2],
        recv_sem=R.core_recv.at[2], device_id=other, device_id_type=MESH)
    core2.start()
    rs_add(R.b2, R.b2r0, 0, big)
    big = rs_start(R.b2, R.b2r1, 0, 1)

    core2.wait()
    mine = R.b1.at[core]

    def add_core(b):
        for p in range(3):
            mine[p, b] = (mine[p, b].astype(F32) + R.b1c[p, b].astype(F32)).astype(BF)

    loop(64, add_core)
    small = rs_start(mine, R.b1r0, 27, 0)

    def tail1(w):
        rows = pl.ds(pl.multiple_of(w * CELLS, 16), CELLS)
        grad = nt(R.dqkv1[rows, :], R.w1[...])
        R.out1[rows, :] = norm_back(grad, R.x1[rows, :], gain1, R.g1[rows, :])

    loop(4, tail1)
    R.xs[3] = nn(R.mats[336:, :], R.out1[...]).astype(BF)
    halo3 = exchange(3, SEG1, R.xs.at[3], R.xr.at[3], ahead)
    R.xr[3, 0:336] = nn(R.mats[0:336, :], R.out1[...]).astype(BF)

    R.matr[...] = take("r4", 0, 576, 608)
    rs_add(mine, R.b1r0, 0, small)
    small = rs_start(mine, R.b1r1, 27, 1)
    rs_add(R.b2, R.b2r1, 1, big)
    big = rs_start(R.b2, R.b2r2, 0, 2)
    wait(halo_r)
    R.v_res[...] = nn(take("rr", 0, CELLS, 192), R.cr[1]).astype(BF).reshape(72, 2, 1024)
    puts = [put(0, "res")]
    rs_add(mine, R.b1r1, 1, small)
    small = rs_start(mine, R.b1r2, 27, 2)
    wait(halo3)
    R.v_tok[...] = jnp.where(present, nn(R.matr[...], R.xr[3]), 0.0).astype(BF)
    puts.append(put(1, "tok"))
    wait(big)
    for p in range(3):
        R.v_q2[:, p * 128:(p + 1) * 128] = rs_last(R.b2, R.b2r2, p, big)
    puts.append(put(3, "q2"))
    wait(small)
    a, b, m = [rs_last(mine, R.b1r2, p, small) for p in range(3)]
    turned = pltpu.roll(m, 64, 1)
    even = xl == 0
    a_turned = pltpu.roll(a, 64, 1)
    b_turned = pltpu.roll(b, 64, 1)
    pick = is_left[0:16]
    R.v_q1[0:16, 0:128] = jnp.where(even, a, jnp.where(pick, turned, a_turned))
    R.v_q1[16:32, 0:128] = jnp.where(even, b, jnp.where(pick, m, b_turned))
    R.v_q1[0:16, 128:192] = jnp.where(even, m, a_turned)[:, 0:64]
    R.v_q1[16:32, 128:192] = jnp.where(even, turned, b_turned)[:, 0:64]
    puts.append(put(2, "q1"))
    wait(puts)


def hand_on(*refs):
    copies = [pltpu.make_async_copy(refs[n], refs[4 + n], refs[8].at[n]) for n in range(4)]
    for c in copies:
        c.start()
    for c in copies:
        c.wait()


def shards(tokens, observed, mask_token, gain_one, qkv_one, table_one, proj_one, merge_weight, gain_two, qkv_two,
           table_two, proj_two, cotangent, sizes):
    first = tokens.transpose(0, 2, 1, 3).reshape(576, 512)
    cot = cotangent.transpose(1, 2, 0, 3).reshape(72, 2, 1024)
    seen = observed.transpose(2, 0, 1)
    given = dict(first=first, cot=cot, w1=qkv_one, p1=proj_one, wm=merge_weight, w2=qkv_two, p2=proj_two)
    args = [given[k] for k in LOADS]
    args += [jnp.asarray(TABLE_OF), seen, mask_token[None], table_one, table_two, gain_one[None], gain_two[None]]
    shapes = (
        jax.ShapeDtypeStruct((72, 2, 1024), BF),
        jax.ShapeDtypeStruct((576, 512), BF),
        jax.ShapeDtypeStruct((32, 192), F32),
        jax.ShapeDtypeStruct((64, 384), F32),
    )
    outs = pl.pallas_call(
        functools.partial(body, sizes),
        out_shape=shapes,
        in_specs=[pl.BlockSpec(memory_space=pl.ANY)] * len(LOADS) + [pl.BlockSpec(memory_space=pltpu.VMEM)] * len(SMALL),
        out_specs=[pl.BlockSpec(memory_space=pl.ANY)] * 4,
        scratch_shapes=list(SCRATCH.values()),
        compiler_params=pltpu.CompilerParams(
            collective_id=0, has_side_effects=True, vmem_limit_bytes=62 * 1024 * 1024),
        cost_estimate=pl.CostEstimate(flops=9 * 10 ** 9, bytes_accessed=24 * 10 ** 6, transcendentals=10 ** 6),
    )(*args)
    res, tok, q1, q2 = pl.pallas_call(
        hand_on,
        out_shape=shapes,
        in_specs=[pl.BlockSpec(memory_space=pl.ANY)] * 4,
        out_specs=[pl.BlockSpec(memory_space=pl.ANY)] * 4,
        scratch_shapes=[pltpu.SemaphoreType.DMA((4,))],
    )(*outs)
    result = res.reshape(12, 6, 2, 1024).transpose(2, 0, 1, 3)
    grad_tokens = tok.reshape(2, 12, 24, 512).transpose(0, 2, 1, 3)
    return (result, grad_tokens, q1, q2)


def solution(mesh):
    sizes = (mesh.shape["lon"], mesh.shape["lat"])
    split = P(None, "lon", "lat", None)

    def run(*args):
        return shards(*args, sizes)

    return jax.shard_map(
        run,
        mesh=mesh,
        in_specs=(split, P(None, "lon", "lat")) + (P(),) * 10 + (split,),
        out_specs=(split, split, P("lon", "lat"), P("lon", "lat")),
        check_vma=False,
    )
```

```python
import functools
from types import SimpleNamespace
import numpy as np
import jax
import jax.numpy as jnp
from jax import lax
from jax.experimental import pallas as pl
from jax.experimental.pallas import tpu as pltpu
from jax.sharding import PartitionSpec as P

BF = jnp.bfloat16
F32 = jnp.float32
EPS = 1e-05
NEG = -1000000000.0
MESH = pl.DeviceIdType.MESH
CELLS = 144
HALF = 72

SEG1 = ((0, 336), (336, 112), (448, 112), (560, 48))
SEG2 = ((0, 48), (48, 48), (96, 48), (144, 48))


def _cells(along, across, half_lon, half_lat):
    out = [[], [], [], []]
    for v in range(2):
        for i in range(along):
            for j in range(across):
                seg = (1 if i < half_lon else 0) + (2 if j < half_lat else 0)
                moved = (v, (i - half_lon) % along, (j - half_lat) % across)
                out[seg].append(((v, i, j), moved))
    return out


def _send_index(segs, cells, row_of):
    out = [-1] * (segs[-1][0] + segs[-1][1])
    for (start, _), members in zip(segs, cells):
        for n, (cell, _) in enumerate(members):
            out[start + n] = row_of(*cell)
    return out


def _recv_index(segs, cells, row_of, rows):
    out = [-1] * rows
    for (start, _), members in zip(segs, cells):
        for n, (_, moved) in enumerate(members):
            out[row_of(*moved)] = start + n
    return out


def _inverse(index, rows):
    out = [-1] * rows
    for n, m in enumerate(index):
        if m >= 0:
            out[m] = n
    return out


def _nat1(v, i, j):
    return (v * 12 + j) * 24 + i


def _win1(v, i, j):
    return ((i // 12) * 2 + j // 6) * CELLS + (j % 6) * 24 + v * 12 + i % 12


def _merge(v, i, j):
    return ((i % 2) * 2 + j % 2) * CELLS + (j // 2) * 24 + v * 12 + i // 2


def _nat2(v, i, j):
    return (i * 6 + j) * 2 + v


def _win2(v, i, j):
    return j * 24 + v * 12 + i


def _indices():
    one = _cells(24, 12, 6, 3)
    two = _cells(12, 6, 6, 3)
    s1 = _send_index(SEG1, one, _nat1)
    r1 = _recv_index(SEG1, one, _win1, 576)
    s2 = _send_index(SEG1, one, _win1)
    r2 = _recv_index(SEG1, one, _merge, 576)
    sc = _send_index(SEG2, two, _nat2)
    rc = _recv_index(SEG2, two, _win2, CELLS)
    flip = [-1] * 768
    for x in range(3):
        for y in range(23):
            for z in range(11):
                flip[(x * 23 + y) * 11 + z] = z * 69 + x * 23 + y
    pick = [-1] * 768
    for z in range(11):
        for v in range(2):
            for l in range(12):
                pick[z * 69 + v * 23 + l] = z * 24 + v * 12 + l
    return dict(s1=s1, r1=r1, s2=s2, r2=r2, s3=_inverse(r2, 608), r3=_inverse(s2, 576), s4=_inverse(r1, 608),
                r4=_inverse(s1, 576), sc=sc, rc=rc, sr=_inverse(rc, 192), rr=_inverse(sc, CELLS), flip=flip, pick=pick)


INDEX = _indices()
TABLE_OF = np.full((768, len(INDEX)), -1, np.int32)
for _n, _rows in enumerate(INDEX.values()):
    TABLE_OF[:len(_rows), _n] = _rows

SHAPES = dict(first=(576, 512), cot=(72, 2, 1024), w1=(512, 1536), p1=(512, 512), p2=(1024, 1024),
              wm=(2048, 1024), w2=(1024, 3072))
LOADS = tuple(SHAPES)


def nn(a, b):
    return lax.dot_general(a, b, (((1,), (0,)), ((), ())), preferred_element_type=F32)


def nt(a, b):
    return lax.dot_general(a, b, (((1,), (1,)), ((), ())), preferred_element_type=F32)


def tn(a, b):
    return lax.dot_general(a, b, (((0,), (0,)), ((), ())), preferred_element_type=F32)


def norm_stats(x):
    centre = jnp.mean(x, axis=-1, keepdims=True)
    dev = x - centre
    spread = jnp.mean(dev * dev, axis=-1, keepdims=True)
    return dev, lax.rsqrt(spread + EPS)


def loop(n, body):
    lax.fori_loop(0, n, lambda i, c: (body(i), c)[1], 0)


SCRATCH = dict(
    {k: pltpu.VMEM(SHAPES[k], BF) for k in LOADS},
    mats=pltpu.VMEM((608, 576), BF),
    matr=pltpu.VMEM((576, 608), BF),
    tables=pltpu.VMEM((24, 768), F32),
    shifted=pltpu.VMEM((1152, 768), F32),
    ext=pltpu.VMEM((24, 24, 264), F32),
    bias=pltpu.VMEM((12, CELLS, 288), F32),
    madd=pltpu.VMEM((CELLS, 288), F32),
    xr=pltpu.VMEM((4, 608, 512), BF),
    xs=pltpu.VMEM((4, 272, 512), BF),
    cr=pltpu.VMEM((2, 192, 1024), BF),
    cs=pltpu.VMEM((2, 144, 1024), BF),
    x1=pltpu.VMEM((576, 512), BF),
    rolled1=pltpu.VMEM((576, 512), BF),
    rolled1t=pltpu.VMEM((512, 576), BF),
    qkv1=pltpu.VMEM((576, 1536), BF),
    dqkv1=pltpu.VMEM((576, 1536), BF),
    prob1=pltpu.VMEM((16, CELLS, 288), BF),
    mixed1=pltpu.VMEM((576, 512), BF),
    out1=pltpu.VMEM((576, 512), BF),
    gm1=pltpu.VMEM((576, 512), BF),
    g1=pltpu.VMEM((576, 512), BF),
    merged=pltpu.VMEM((576, 512), BF),
    second=pltpu.VMEM((CELLS, 1024), BF),
    rolled2=pltpu.VMEM((CELLS, 1024), BF),
    qkv2=pltpu.VMEM((CELLS, 3072), BF),
    dqkv2=pltpu.VMEM((2, CELLS, 3072), BF),
    half2=pltpu.VMEM((2, CELLS, 512), BF),
    theirs2=pltpu.VMEM((CELLS, 512), BF),
    halft=pltpu.VMEM((2, 512, CELLS), BF),
    mixed2=pltpu.VMEM((CELLS, 1024), BF),
    ct=pltpu.VMEM((CELLS, 1024), BF),
    gm2=pltpu.VMEM((CELLS, 1024), BF),
    res=pltpu.VMEM((CELLS, 1024), BF),
    gs=pltpu.VMEM((CELLS, 1024), BF),
    v_res=pltpu.VMEM((72, 2, 1024), BF),
    v_tok=pltpu.VMEM((576, 512), BF),
    v_q1=pltpu.VMEM((32, 192), F32),
    v_q2=pltpu.VMEM((64, 384), F32),
    out_sem=pltpu.SemaphoreType.DMA((4,)),
    b2=pltpu.VMEM((3, 64, 64, 128), BF),
    b2r0=pltpu.VMEM((3, 3, 16, 64, 128), BF),
    b2r1=pltpu.VMEM((3, 3, 4, 64, 128), BF),
    b2r2=pltpu.VMEM((3, 3, 1, 64, 128), BF),
    b1=pltpu.VMEM((2, 3, 64, 16, 128), BF),
    b1c=pltpu.VMEM((3, 64, 16, 128), BF),
    b1r0=pltpu.VMEM((3, 3, 16, 16, 128), BF),
    b1r1=pltpu.VMEM((3, 3, 4, 16, 128), BF),
    b1r2=pltpu.VMEM((3, 3, 1, 16, 128), BF),
    load_sem=pltpu.SemaphoreType.DMA((len(LOADS),)),
    halo_send=pltpu.SemaphoreType.DMA((18,)),
    halo_recv=pltpu.SemaphoreType.DMA((18,)),
    rs_send=pltpu.SemaphoreType.DMA((54,)),
    rs_recv=pltpu.SemaphoreType.DMA((54,)),
    core_send=pltpu.SemaphoreType.DMA((3,)),
    core_recv=pltpu.SemaphoreType.DMA((3,)),
)
SMALL = ("index", "seen", "mask", "table1", "table2", "gain1", "gain2")
OUTPUTS = ("o_res", "o_tok", "o_q1", "o_q2")

ORDERS = (("z", "x", "y"), ("x", "y", "z"), ("y", "z", "x"))


def body(sizes, *refs):
    n_lon, n_lat = sizes
    names = ["in_" + n for n in LOADS + SMALL] + list(OUTPUTS) + list(SCRATCH)
    R = SimpleNamespace(**dict(zip(names, refs, strict=True)))

    e = lax.axis_index("lon")
    d = lax.axis_index("lat")
    core, xh, z = lax.rem(e, 2), lax.rem(e // 2, 2), e // 4
    xl, y = lax.rem(d, 2), d // 2
    x = xh * 2 + xl
    place = dict(x=x, y=y, z=z)
    e_up, e_dn = lax.rem(e + 1, n_lon), lax.rem(e + n_lon - 1, n_lon)
    d_up, d_dn = lax.rem(d + 1, n_lat), lax.rem(d + n_lat - 1, n_lat)
    last = d == n_lat - 1
    ahead = ((e_up, d), (e, d_up), (e_up, d_up))
    behind = ((e_dn, d), (e, d_dn), (e_dn, d_dn))
    other = (e + 1 - 2 * core, d)

    def device(x, y, z):
        return (z * 4 + (x // 2) * 2 + core, y * 2 + lax.rem(x, 2))

    def along(axis, k):
        at = dict(place)
        at[axis] = lax.rem(at[axis] + k, 4)
        return device(**at)

    loads = SimpleNamespace()
    for n, name in enumerate(LOADS):
        copy = pltpu.make_async_copy(getattr(R, "in_" + name), getattr(R, name), R.load_sem.at[n])
        copy.start()
        setattr(loads, name, copy)

    barrier = pltpu.get_barrier_semaphore()
    partners = list(ahead) + list(behind) + [other]
    for axis in place:
        for k in (1, 2, 3):
            partners.append(along(axis, k))
    for who in partners:
        pl.semaphore_signal(barrier, inc=1, device_id=who, device_id_type=MESH)

    def exchange(n, segs, source, target, to):
        copies = []
        for k in range(3):
            start, size = segs[k + 1]
            rows = pl.ds(start, size)
            copies.append(pltpu.make_async_remote_copy(
                src_ref=source.at[pl.ds(start - segs[0][1], size)],
                dst_ref=target.at[rows],
                send_sem=R.halo_send.at[3 * n + k],
                recv_sem=R.halo_recv.at[3 * n + k],
                device_id=to[k],
                device_id_type=MESH))
        for c in copies:
            c.start()
        return copies

    def wait(copies):
        for c in copies:
            c.wait()

    def take(key, start, size, columns):
        n = list(INDEX).index(key)
        col = R.in_index[pl.ds(start, size), n:n + 1]
        hit = col == lax.broadcasted_iota(jnp.int32, (size, columns), 1)
        return jnp.where(hit, 1.0, 0.0).astype(BF)

    def put(n, name):
        copy = pltpu.make_async_copy(getattr(R, "v_" + name), getattr(R, "o_" + name), R.out_sem.at[n])
        copy.start()
        return copy

    seen = R.in_seen[...]
    seen = jnp.concatenate([seen[:, 0, :], seen[:, 1, :]], axis=0).astype(F32).astype(BF)
    row = lax.broadcasted_iota(jnp.int32, (576, 24), 0)
    col = lax.broadcasted_iota(jnp.int32, (576, 24), 1)
    per = nn(jnp.where(row // 24 == col, 1.0, 0.0).astype(BF), seen)
    present = jnp.sum(jnp.where(lax.rem(row, 24) == col, per, 0.0), axis=-1, keepdims=True) > 0.5

    R.mats[...] = take("s1", 0, 608, 576)
    loads.first.wait()
    R.first[...] = jnp.where(present, R.first[...].astype(F32), R.in_mask[...].astype(BF).astype(F32)).astype(BF)
    R.xs[0] = nn(R.mats[336:, :], R.first[...]).astype(BF)
    pl.semaphore_wait(barrier, len(partners))
    halo0 = exchange(0, SEG1, R.xs.at[0], R.xr.at[0], behind)
    R.xr[0, 0:336] = nn(R.mats[0:336, :], R.first[...]).astype(BF)
    loads.cot.wait()
    cot = R.cot[...].reshape(CELLS, 1024)
    R.cs[0] = nn(take("sc", 48, 144, CELLS), cot).astype(BF)
    halo_c = exchange(4, SEG2, R.cs.at[0], R.cr.at[0], behind)
    R.cr[0, 0:48] = nn(take("sc", 0, 48, CELLS), cot).astype(BF)
    R.matr[...] = take("r1", 0, 576, 608)
    R.mats[...] = take("s2", 0, 608, 576)

    R.tables[...] = jnp.zeros((24, 768), F32)
    R.tables[0:8, 0:759] = R.in_table1[...]
    R.tables[8:24, 0:759] = R.in_table2[...]
    table = R.tables[...]
    high = table.astype(BF).astype(F32)
    mid = (table - high).astype(BF).astype(F32)
    low = table - high - mid
    parts = jnp.concatenate([high, mid, low], axis=0).astype(BF)
    parts = nn(parts, take("flip", 0, 768, 768))
    picked = take("pick", 0, 768, 264)

    def extend(first, heads):
        part = jnp.concatenate([parts[24 * k + first:24 * k + first + heads] for k in range(3)], axis=0)
        for v in range(2):
            for l in range(12):
                shift = (1 - v) * 23 + 11 - l
                moved = pltpu.roll(part, (768 - shift) % 768, 1) if shift else part
                at = (v * 12 + l) * 3 * heads
                R.shifted[at:at + 3 * heads] = moved
        got = nn(R.shifted[0:72 * heads].astype(BF), picked)
        for n in range(24):
            at = n * 3 * heads
            R.ext[first:first + heads, n, :] = (
                got[at:at + heads] + got[at + heads:at + 2 * heads] + got[at + 2 * heads:at + 3 * heads])

    extend(0, 8)
    rows = lax.broadcasted_iota(jnp.int32, (CELLS, CELLS), 0)
    cols = lax.broadcasted_iota(jnp.int32, (CELLS, CELLS), 1)
    apart = jnp.where(jnp.logical_xor(rows < HALF, cols < HALF), NEG, 0.0).astype(F32)
    apart = apart * jnp.where(last, 1.0, 0.0).astype(F32)
    R.madd[...] = jnp.concatenate([apart, apart], axis=1)

    def expand(pair):
        one, two = R.ext[2 * pair], R.ext[2 * pair + 1]
        for a in range(6):
            at = slice((5 - a) * 24, (5 - a) * 24 + CELLS)
            R.bias[pair, a * 24:(a + 1) * 24, :] = jnp.concatenate([one[:, at], two[:, at]], axis=1)

    def expand_masked(pair):
        expand(4 + pair)
        R.bias[4 + pair] = R.bias[4 + pair] + R.madd[...]

    loop(4, expand)

    lane = lax.broadcasted_iota(jnp.int32, (1, 128), 1)
    left = jnp.where(lane < 64, 1.0, 0.0).astype(BF)
    right = jnp.where(lane < 64, 0.0, 1.0).astype(BF)
    is_left = lax.broadcasted_iota(jnp.int32, (CELLS, 128), 1) < 64

    def stack(t):
        return jnp.concatenate([t * left, t * right], axis=0)

    def at(part, pair, width):
        return pl.ds(pl.multiple_of(part * width + pair * 128, 128), 128)

    def heads_of(t):
        return jnp.where(is_left, t[:CELLS], t[CELLS:])

    def attend(q2, k, v, bias):
        score = [nt(b, a) + c for a, b, c in zip(q2, k, bias)]
        expo = [jnp.exp(t - jnp.max(t, axis=0, keepdims=True)) for t in score]
        p = [t * (1.0 / jnp.sum(t, axis=0, keepdims=True)) for t in expo]
        pb = [t.astype(BF) for t in p]
        o = [heads_of(tn(a, b)).astype(BF) for a, b in zip(pb, v)]
        return p, pb, o

    def attend_back(q2, k, v, p, pb, go):
        gw = [nt(a, b) for a, b in zip(v, go)]
        gs = [(a * (b - jnp.sum(a * b, axis=0, keepdims=True))).astype(BF) for a, b in zip(p, gw)]
        gv = [nn(a, b).astype(BF) for a, b in zip(pb, go)]
        gk = [nn(a, b).astype(BF) for a, b in zip(gs, q2)]
        gq = [(heads_of(tn(a, b)) * 0.125).astype(BF) for a, b in zip(gs, k)]
        return gq, gk, gv

    gain1 = R.in_gain1[...]
    wait(halo0)

    def window(w):
        return pl.ds(pl.multiple_of(w * CELLS, 16), CELLS)

    def tile(n, size=256):
        return pl.ds(pl.multiple_of(n * size, size), size)

    def place1(n):
        R.x1[:, tile(n)] = nn(R.matr[...], R.xr[0, :, tile(n)]).astype(BF)

    def norm1(w):
        dev, inv = norm_stats(R.x1[window(w), :].astype(F32))
        R.rolled1[window(w), :] = (dev * inv * gain1).astype(BF)

    loop(2, place1)
    loop(4, norm1)
    loads.w1.wait()

    def qkv1(n):
        c = pl.ds(pl.multiple_of(n * 256, 256), 256)
        R.qkv1[:, c] = nn(R.rolled1[...], R.w1[:, c]).astype(BF)

    loop(6, qkv1)

    def four(pair):
        q2 = [stack(R.qkv1[window(w), at(0, pair, 512)] * BF(0.125)) for w in range(4)]
        k = [R.qkv1[window(w), at(1, pair, 512)] for w in range(4)]
        v = [R.qkv1[window(w), at(2, pair, 512)] for w in range(4)]
        return q2, k, v

    def fwd1(pair):
        bias = R.bias[pair]
        masked = bias + R.madd[...]
        _, pb, o = attend(*four(pair), [bias, masked, bias, masked])
        for w in range(4):
            R.prob1[pair * 4 + w] = pb[w]
            R.mixed1[window(w), at(0, pair, 512)] = o[w]

    loop(4, fwd1)
    loads.p1.wait()

    def proj1(n):
        branch = nn(R.mixed1[...], R.p1[:, tile(n)]).astype(BF).astype(F32)
        R.out1[:, tile(n)] = (R.x1[:, tile(n)].astype(F32) + branch).astype(BF)

    loop(2, proj1)

    R.xs[1] = nn(R.mats[336:, :], R.out1[...]).astype(BF)
    halo1 = exchange(1, SEG1, R.xs.at[1], R.xr.at[1], behind)
    R.xr[1, 0:336] = nn(R.mats[0:336, :], R.out1[...]).astype(BF)
    extend(8, 16)
    loop(8, expand_masked)
    R.mats[...] = take("s3", 0, 608, 576)
    R.matr[...] = take("r2", 0, 576, 608)
    wait(halo_c)
    R.ct[...] = nn(take("rc", 0, CELLS, 192), R.cr[0]).astype(BF)
    loads.p2.wait()

    def grad_mixed2(n):
        c = pl.ds(pl.multiple_of(n * 256, 256), 256)
        R.gm2[:, c] = nt(R.ct[...], R.p2[c, :]).astype(BF)

    loop(4, grad_mixed2)
    R.rolled1t[...] = R.rolled1[...].T
    wait(halo1)
    R.merged[...] = nn(R.matr[...], R.xr[1]).astype(BF)
    loads.wm.wait()
    acc = nn(R.merged[0:CELLS, :], R.wm[0:512, :])
    for s in range(1, 4):
        acc = acc + nn(R.merged[s * CELLS:(s + 1) * CELLS, :], R.wm[s * 512:(s + 1) * 512, :])
    second = acc.astype(BF)
    R.second[...] = second
    gain2 = R.in_gain2[...]
    dev, inv = norm_stats(second.astype(F32))
    rolled2 = (dev * inv * gain2).astype(BF)
    R.rolled2[...] = rolled2
    loads.w2.wait()

    def qkv2(n):
        c = pl.ds(pl.multiple_of(n * 512, 512), 512)
        R.qkv2[:, c] = nn(R.rolled2[...], R.w2[:, c]).astype(BF)

    loop(6, qkv2)

    r2f = rolled2.astype(F32)
    for t in range(4):
        a = r2f[:, t * 256:t * 256 + 128]
        b = r2f[:, t * 256 + 128:t * 256 + 256]
        c = slice(t * 128, t * 128 + 128)
        R.half2[0, :, c] = jnp.where(is_left, a, pltpu.roll(b, 64, 1)).astype(BF)
        R.half2[1, :, c] = jnp.where(is_left, pltpu.roll(a, 64, 1), b).astype(BF)
    core0 = pltpu.make_async_remote_copy(
        src_ref=R.half2.at[1 - core], dst_ref=R.theirs2, send_sem=R.core_send.at[0],
        recv_sem=R.core_recv.at[0], device_id=other, device_id_type=MESH)
    core0.start()

    def both2(u):
        pairs = [u * 4 + n for n in range(4)]
        q2 = [stack(R.qkv2[:, at(0, c, 1024)] * BF(0.125)) for c in pairs]
        k = [R.qkv2[:, at(1, c, 1024)] for c in pairs]
        v = [R.qkv2[:, at(2, c, 1024)] for c in pairs]
        go = [stack(R.gm2[:, at(0, c, 1024)]) for c in pairs]
        p, pb, o = attend(q2, k, v, [R.bias[4 + c] for c in pairs])
        back = attend_back(q2, k, v, p, pb, go)
        for n, c in enumerate(pairs):
            R.mixed2[:, at(0, c, 1024)] = o[n]
            for part in range(3):
                R.dqkv2[0, :, at(part, c, 1024)] = back[part][n]

    loop(2, both2)
    core1 = pltpu.make_async_remote_copy(
        src_ref=R.dqkv2.at[0], dst_ref=R.dqkv2.at[1], send_sem=R.core_send.at[1],
        recv_sem=R.core_recv.at[1], device_id=other, device_id_type=MESH)
    core1.start()

    grad_rolled = nt(R.dqkv2[0, :, 0:1024], R.w2[:, 0:1024])
    grad_rolled = grad_rolled + nt(R.dqkv2[0, :, 1024:2048], R.w2[:, 1024:2048])
    grad_rolled = grad_rolled + nt(R.dqkv2[0, :, 2048:3072], R.w2[:, 2048:3072])

    def norm_back(grad, xin, gain, grad_out):
        grad = grad.astype(BF).astype(F32) * gain
        dev, inv = norm_stats(xin.astype(F32))
        hat = dev * inv
        inner = inv * (grad - jnp.mean(grad, axis=-1, keepdims=True)
                       - hat * jnp.mean(grad * hat, axis=-1, keepdims=True))
        return (grad_out.astype(F32) + inner.astype(BF).astype(F32)).astype(BF)

    R.gs[...] = norm_back(grad_rolled, R.second[...], gain2, R.ct[...])
    for s in range(4):
        R.merged[s * CELLS:(s + 1) * CELLS, :] = nt(R.gs[...], R.wm[s * 512:(s + 1) * 512, :]).astype(BF)
    R.xs[2] = nn(R.mats[336:, :], R.merged[...]).astype(BF)
    halo2 = exchange(2, SEG1, R.xs.at[2], R.xr.at[2], ahead)
    R.xr[2, 0:336] = nn(R.mats[0:336, :], R.merged[...]).astype(BF)

    R.mats[...] = take("s4", 0, 608, 576)
    R.matr[...] = take("r3", 0, 576, 608)

    branch = nn(R.mixed2[...], R.p2[...]).astype(BF).astype(F32)
    R.res[...] = (R.second[...].astype(F32) + branch).astype(BF)
    R.cs[1] = nn(take("sr", 48, 144, CELLS), R.res[...]).astype(BF)
    halo_r = exchange(5, SEG2, R.cs.at[1], R.cr.at[1], ahead)
    R.cr[1, 0:48] = nn(take("sr", 0, 48, CELLS), R.res[...]).astype(BF)

    R.halft[0] = R.half2[core].T
    core0.wait()
    R.halft[1] = R.theirs2[...].T
    core1.wait()

    def term2(t):
        c = pl.ds(pl.multiple_of(t * 384, 128), 384)
        g = nn(R.halft[0], R.dqkv2[0, :, c]) + nn(R.halft[1], R.dqkv2[1, :, c])
        g = g.astype(BF)
        yy, xx = t // 2, lax.rem(t, 2)
        for zz in range(4):
            for hh in range(2):
                r = (zz * 2 + hh) * 64
                at = dict(z=zz, x=hh * 2 + xx, y=yy)
                for p, order in enumerate(ORDERS):
                    block = (at[order[0]] * 4 + at[order[1]]) * 4 + at[order[2]]
                    R.b2[p, block] = g[r:r + 64, p * 128:(p + 1) * 128]

    loop(8, term2)

    def rs_start(buf, recv, sem0, step):
        copies = []
        for p, order in enumerate(ORDERS):
            base = 0
            for s in range(step):
                base = base + place[order[s]] * (16 >> (2 * s))
            size = 16 >> (2 * step)
            axis = order[step]
            for k in (1, 2, 3):
                to = lax.rem(place[axis] + k, 4)
                n = sem0 + (step * 3 + p) * 3 + k - 1
                copies.append(pltpu.make_async_remote_copy(
                    src_ref=buf.at[p, pl.ds(base + to * size, size)],
                    dst_ref=recv.at[p, k - 1],
                    send_sem=R.rs_send.at[n],
                    recv_sem=R.rs_recv.at[n],
                    device_id=along(axis, k),
                    device_id_type=MESH))
        for c in copies:
            c.start()
        return copies

    def rs_add(buf, recv, step, copies):
        wait(copies)
        size = 16 >> (2 * step)
        for p, order in enumerate(ORDERS):
            base = 0
            for s in range(step + 1):
                base = base + place[order[s]] * (16 >> (2 * s))

            def add(b):
                t = buf[p, base + b].astype(F32) + recv[p, 0, b].astype(F32)
                t = t + recv[p, 1, b].astype(F32) + recv[p, 2, b].astype(F32)
                buf[p, base + b] = t.astype(BF)

            loop(size, add)

    def rs_last(buf, recv, p, copies):
        order = ORDERS[p]
        base = (place[order[0]] * 4 + place[order[1]]) * 4 + place[order[2]]
        t = buf[p, base].astype(F32) + recv[p, 0, 0].astype(F32)
        return t + recv[p, 1, 0].astype(F32) + recv[p, 2, 0].astype(F32)

    big = rs_start(R.b2, R.b2r0, 0, 0)

    wait(halo2)
    R.g1[...] = nn(R.matr[...], R.xr[2]).astype(BF)

    def grad_mixed1(n):
        R.gm1[:, tile(n)] = nt(R.g1[...], R.p1[tile(n), :]).astype(BF)

    loop(2, grad_mixed1)

    def bwd1(pair):
        q2, k, v = four(pair)
        go = [stack(R.gm1[window(w), at(0, pair, 512)]) for w in range(4)]
        pb = [R.prob1[pair * 4 + w] for w in range(4)]
        back = attend_back(q2, k, v, [t.astype(F32) for t in pb], pb, go)
        for w in range(4):
            for part in range(3):
                R.dqkv1[window(w), at(part, pair, 512)] = back[part][w]

    loop(4, bwd1)

    def term1(t):
        c = pl.ds(pl.multiple_of(t * 384, 128), 384)
        g = nn(R.rolled1t[...], R.dqkv1[:, c])
        for zz in range(4):
            for hh in range(2):
                for cc in range(2):
                    r = ((zz * 2 + hh) * 2 + cc) * 32
                    upper = g[r:r + 16, 128:256]
                    lower = pltpu.roll(g[r + 16:r + 32, 128:256], 64, 1)
                    pick = is_left[0:16]
                    mixes = (jnp.where(pick, upper, lower), jnp.where(pick, lower, upper))
                    for odd in range(2):
                        at = dict(z=zz, x=hh * 2 + odd, y=t)
                        lanes = slice(odd * 256, odd * 256 + 128)
                        pieces = (g[r:r + 16, lanes], g[r + 16:r + 32, lanes], mixes[odd])
                        for p, order in enumerate(ORDERS):
                            block = (at[order[0]] * 4 + at[order[1]]) * 4 + at[order[2]]
                            R.b1[cc, p, block] = pieces[p].astype(BF)

    loop(4, term1)
    core2 = pltpu.make_async_remote_copy(
        src_ref=R.b1.at[1 - core], dst_ref=R.b1c, send_sem=R.core_send.at[2],
        recv_sem=R.core_recv.at[2], device_id=other, device_id_type=MESH)
    core2.start()
    rs_add(R.b2, R.b2r0, 0, big)
    big = rs_start(R.b2, R.b2r1, 0, 1)

    core2.wait()
    mine = R.b1.at[core]

    def add_core(b):
        for p in range(3):
            mine[p, b] = (mine[p, b].astype(F32) + R.b1c[p, b].astype(F32)).astype(BF)

    loop(64, add_core)
    small = rs_start(mine, R.b1r0, 27, 0)

    def grad_rolled1(n):
        R.gm1[:, tile(n)] = nt(R.dqkv1[...], R.w1[tile(n), :]).astype(BF)

    def tail1(w):
        r = window(w)
        R.out1[r, :] = norm_back(R.gm1[r, :], R.x1[r, :], gain1, R.g1[r, :])

    loop(2, grad_rolled1)
    loop(4, tail1)
    R.xs[3] = nn(R.mats[336:, :], R.out1[...]).astype(BF)
    halo3 = exchange(3, SEG1, R.xs.at[3], R.xr.at[3], ahead)
    R.xr[3, 0:336] = nn(R.mats[0:336, :], R.out1[...]).astype(BF)

    R.matr[...] = take("r4", 0, 576, 608)
    rs_add(mine, R.b1r0, 0, small)
    small = rs_start(mine, R.b1r1, 27, 1)
    rs_add(R.b2, R.b2r1, 1, big)
    big = rs_start(R.b2, R.b2r2, 0, 2)
    wait(halo_r)
    R.v_res[...] = nn(take("rr", 0, CELLS, 192), R.cr[1]).astype(BF).reshape(72, 2, 1024)
    puts = [put(0, "res")]
    rs_add(mine, R.b1r1, 1, small)
    small = rs_start(mine, R.b1r2, 27, 2)
    wait(halo3)
    R.v_tok[...] = jnp.where(present, nn(R.matr[...], R.xr[3]), 0.0).astype(BF)
    puts.append(put(1, "tok"))
    wait(big)
    for p in range(3):
        R.v_q2[:, p * 128:(p + 1) * 128] = rs_last(R.b2, R.b2r2, p, big)
    puts.append(put(3, "q2"))
    wait(small)
    a, b, m = [rs_last(mine, R.b1r2, p, small) for p in range(3)]
    turned = pltpu.roll(m, 64, 1)
    even = xl == 0
    a_turned = pltpu.roll(a, 64, 1)
    b_turned = pltpu.roll(b, 64, 1)
    pick = is_left[0:16]
    R.v_q1[0:16, 0:128] = jnp.where(even, a, jnp.where(pick, turned, a_turned))
    R.v_q1[16:32, 0:128] = jnp.where(even, b, jnp.where(pick, m, b_turned))
    R.v_q1[0:16, 128:192] = jnp.where(even, m, a_turned)[:, 0:64]
    R.v_q1[16:32, 128:192] = jnp.where(even, turned, b_turned)[:, 0:64]
    puts.append(put(2, "q1"))
    wait(puts)


def hand_on(*refs):
    given, out, held, sem = refs[0:4], refs[4:8], refs[8:12], refs[12]
    come = [pltpu.make_async_copy(given[n], held[n], sem.at[n]) for n in range(4)]
    leave = [pltpu.make_async_copy(held[n], out[n], sem.at[4 + n]) for n in range(4)]
    for c in come:
        c.start()
    for n in range(4):
        come[n].wait()
        leave[n].start()
    for c in leave:
        c.wait()


def shards(tokens, observed, mask_token, gain_one, qkv_one, table_one, proj_one, merge_weight, gain_two, qkv_two,
           table_two, proj_two, cotangent, sizes):
    first = tokens.transpose(0, 2, 1, 3).reshape(576, 512)
    cot = cotangent.transpose(1, 2, 0, 3).reshape(72, 2, 1024)
    seen = observed.transpose(2, 0, 1)
    given = dict(first=first, cot=cot, w1=qkv_one, p1=proj_one, wm=merge_weight, w2=qkv_two, p2=proj_two)
    args = [given[k] for k in LOADS]
    args += [jnp.asarray(TABLE_OF), seen, mask_token[None], table_one, table_two, gain_one[None], gain_two[None]]
    shapes = (
        jax.ShapeDtypeStruct((72, 2, 1024), BF),
        jax.ShapeDtypeStruct((576, 512), BF),
        jax.ShapeDtypeStruct((32, 192), F32),
        jax.ShapeDtypeStruct((64, 384), F32),
    )
    outs = pl.pallas_call(
        functools.partial(body, sizes),
        out_shape=shapes,
        in_specs=[pl.BlockSpec(memory_space=pl.ANY)] * len(LOADS) + [pl.BlockSpec(memory_space=pltpu.VMEM)] * len(SMALL),
        out_specs=[pl.BlockSpec(memory_space=pl.ANY)] * 4,
        scratch_shapes=list(SCRATCH.values()),
        compiler_params=pltpu.CompilerParams(
            collective_id=0, has_side_effects=True, vmem_limit_bytes=62 * 1024 * 1024),
        cost_estimate=pl.CostEstimate(flops=9 * 10 ** 9, bytes_accessed=24 * 10 ** 6, transcendentals=10 ** 6),
    )(*args)
    res, tok, q1, q2 = pl.pallas_call(
        hand_on,
        out_shape=shapes,
        in_specs=[pl.BlockSpec(memory_space=pl.ANY)] * 4,
        out_specs=[pl.BlockSpec(memory_space=pl.ANY)] * 4,
        scratch_shapes=[pltpu.VMEM(s.shape, s.dtype) for s in shapes] + [pltpu.SemaphoreType.DMA((8,))],
    )(*outs)
    result = res.reshape(12, 6, 2, 1024).transpose(2, 0, 1, 3)
    grad_tokens = tok.reshape(2, 12, 24, 512).transpose(0, 2, 1, 3)
    return (result, grad_tokens, q1, q2)


def solution(mesh):
    sizes = (mesh.shape["lon"], mesh.shape["lat"])
    split = P(None, "lon", "lat", None)

    def run(*args):
        return shards(*args, sizes)

    return jax.shard_map(
        run,
        mesh=mesh,
        in_specs=(split, P(None, "lon", "lat")) + (P(),) * 10 + (split,),
        out_specs=(split, split, P("lon", "lat"), P("lon", "lat")),
        check_vma=False,
    )
```

```python
import functools
from types import SimpleNamespace
import numpy as np
import jax
import jax.numpy as jnp
from jax import lax
from jax.experimental import pallas as pl
from jax.experimental.pallas import tpu as pltpu
from jax.sharding import PartitionSpec as P

BF = jnp.bfloat16
F32 = jnp.float32
EPS = 1e-05
NEG = -1000000000.0
MESH = pl.DeviceIdType.MESH
CELLS = 144
HALF = 72

SEG1 = ((0, 336), (336, 112), (448, 112), (560, 48))
SEG2 = ((0, 48), (48, 48), (96, 48), (144, 48))


def _cells(along, across, half_lon, half_lat):
    out = [[], [], [], []]
    for v in range(2):
        for i in range(along):
            for j in range(across):
                seg = (1 if i < half_lon else 0) + (2 if j < half_lat else 0)
                moved = (v, (i - half_lon) % along, (j - half_lat) % across)
                out[seg].append(((v, i, j), moved))
    return out


def _send_index(segs, cells, row_of):
    out = [-1] * (segs[-1][0] + segs[-1][1])
    for (start, _), members in zip(segs, cells):
        for n, (cell, _) in enumerate(members):
            out[start + n] = row_of(*cell)
    return out


def _recv_index(segs, cells, row_of, rows):
    out = [-1] * rows
    for (start, _), members in zip(segs, cells):
        for n, (_, moved) in enumerate(members):
            out[row_of(*moved)] = start + n
    return out


def _inverse(index, rows):
    out = [-1] * rows
    for n, m in enumerate(index):
        if m >= 0:
            out[m] = n
    return out


def _nat1(v, i, j):
    return (v * 12 + j) * 24 + i


def _win1(v, i, j):
    return ((i // 12) * 2 + j // 6) * CELLS + (j % 6) * 24 + v * 12 + i % 12


def _merge(v, i, j):
    return ((i % 2) * 2 + j % 2) * CELLS + (j // 2) * 24 + v * 12 + i // 2


def _nat2(v, i, j):
    return (i * 6 + j) * 2 + v


def _win2(v, i, j):
    return j * 24 + v * 12 + i


def _indices():
    one = _cells(24, 12, 6, 3)
    two = _cells(12, 6, 6, 3)
    s1 = _send_index(SEG1, one, _nat1)
    r1 = _recv_index(SEG1, one, _win1, 576)
    s2 = _send_index(SEG1, one, _win1)
    r2 = _recv_index(SEG1, one, _merge, 576)
    sc = _send_index(SEG2, two, _nat2)
    rc = _recv_index(SEG2, two, _win2, CELLS)
    flip = [-1] * 768
    for x in range(3):
        for y in range(23):
            for z in range(11):
                flip[(x * 23 + y) * 11 + z] = z * 69 + x * 23 + y
    pick = [-1] * 768
    for z in range(11):
        for v in range(2):
            for l in range(12):
                pick[z * 69 + v * 23 + l] = z * 24 + v * 12 + l
    return dict(s1=s1, r1=r1, s2=s2, r2=r2, s3=_inverse(r2, 608), r3=_inverse(s2, 576), s4=_inverse(r1, 608),
                r4=_inverse(s1, 576), sc=sc, rc=rc, sr=_inverse(rc, 192), rr=_inverse(sc, CELLS), flip=flip, pick=pick)


INDEX = _indices()
TABLE_OF = np.full((768, len(INDEX)), -1, np.int32)
for _n, _rows in enumerate(INDEX.values()):
    TABLE_OF[:len(_rows), _n] = _rows

SHAPES = dict(first=(576, 512), cot=(72, 2, 1024), w1=(512, 1536), p1=(512, 512), p2=(1024, 1024),
              wm=(2048, 1024), w2=(1024, 3072))
LOADS = tuple(SHAPES)


def nn(a, b):
    return lax.dot_general(a, b, (((1,), (0,)), ((), ())), preferred_element_type=F32)


def nt(a, b):
    return lax.dot_general(a, b, (((1,), (1,)), ((), ())), preferred_element_type=F32)


def tn(a, b):
    return lax.dot_general(a, b, (((0,), (0,)), ((), ())), preferred_element_type=F32)


def norm_stats(x):
    centre = jnp.mean(x, axis=-1, keepdims=True)
    dev = x - centre
    spread = jnp.mean(dev * dev, axis=-1, keepdims=True)
    return dev, lax.rsqrt(spread + EPS)


def loop(n, body):
    lax.fori_loop(0, n, lambda i, c: (body(i), c)[1], 0)


SCRATCH = dict(
    {k: pltpu.VMEM(SHAPES[k], BF) for k in LOADS},
    mats=pltpu.VMEM((608, 576), BF),
    matr=pltpu.VMEM((576, 608), BF),
    tables=pltpu.VMEM((24, 768), F32),
    shifted=pltpu.VMEM((1152, 768), F32),
    ext=pltpu.VMEM((24, 24, 264), F32),
    bias=pltpu.VMEM((12, CELLS, 288), F32),
    madd=pltpu.VMEM((CELLS, 288), F32),
    xr=pltpu.VMEM((4, 608, 512), BF),
    xs=pltpu.VMEM((4, 272, 512), BF),
    cr=pltpu.VMEM((2, 192, 1024), BF),
    cs=pltpu.VMEM((2, 144, 1024), BF),
    x1=pltpu.VMEM((576, 512), BF),
    rolled1=pltpu.VMEM((576, 512), BF),
    rolled1t=pltpu.VMEM((512, 576), BF),
    qkv1=pltpu.VMEM((576, 1536), BF),
    dqkv1=pltpu.VMEM((576, 1536), BF),
    prob1=pltpu.VMEM((16, CELLS, 288), BF),
    mixed1=pltpu.VMEM((576, 512), BF),
    out1=pltpu.VMEM((576, 512), BF),
    gm1=pltpu.VMEM((576, 512), BF),
    g1=pltpu.VMEM((576, 512), BF),
    merged=pltpu.VMEM((576, 512), BF),
    second=pltpu.VMEM((CELLS, 1024), BF),
    rolled2=pltpu.VMEM((CELLS, 1024), BF),
    qkv2=pltpu.VMEM((CELLS, 3072), BF),
    dqkv2=pltpu.VMEM((2, CELLS, 3072), BF),
    half2=pltpu.VMEM((2, CELLS, 512), BF),
    theirs2=pltpu.VMEM((CELLS, 512), BF),
    halft=pltpu.VMEM((2, 512, CELLS), BF),
    mixed2=pltpu.VMEM((CELLS, 1024), BF),
    ct=pltpu.VMEM((CELLS, 1024), BF),
    gm2=pltpu.VMEM((CELLS, 1024), BF),
    res=pltpu.VMEM((CELLS, 1024), BF),
    gs=pltpu.VMEM((CELLS, 1024), BF),
    v_res=pltpu.VMEM((72, 2, 1024), BF),
    v_tok=pltpu.VMEM((576, 512), BF),
    v_q1=pltpu.VMEM((32, 192), F32),
    v_q2=pltpu.VMEM((64, 384), F32),
    out_sem=pltpu.SemaphoreType.DMA((4,)),
    b2=pltpu.VMEM((3, 64, 64, 128), BF),
    b2r0=pltpu.VMEM((3, 3, 16, 64, 128), BF),
    b2r1=pltpu.VMEM((3, 3, 4, 64, 128), BF),
    b2r2=pltpu.VMEM((3, 3, 1, 64, 128), BF),
    b1=pltpu.VMEM((3, 64, 16, 128), BF),
    b1h=pltpu.VMEM((4, 2, 3, 16, 16, 128), BF),
    b1c=pltpu.VMEM((4, 3, 16, 16, 128), BF),
    b1r0=pltpu.VMEM((3, 3, 16, 16, 128), BF),
    b1r1=pltpu.VMEM((3, 3, 4, 16, 128), BF),
    b1r2=pltpu.VMEM((3, 3, 1, 16, 128), BF),
    load_sem=pltpu.SemaphoreType.DMA((len(LOADS),)),
    halo_send=pltpu.SemaphoreType.DMA((18,)),
    halo_recv=pltpu.SemaphoreType.DMA((18,)),
    rs_send=pltpu.SemaphoreType.DMA((54,)),
    rs_recv=pltpu.SemaphoreType.DMA((54,)),
    core_send=pltpu.SemaphoreType.DMA((6,)),
    core_recv=pltpu.SemaphoreType.DMA((6,)),
)
SMALL = ("index", "seen", "mask", "table1", "table2", "gain1", "gain2")
OUTPUTS = ("o_res", "o_tok", "o_q1", "o_q2")

ORDERS = (("z", "x", "y"), ("x", "y", "z"), ("y", "z", "x"))


def body(sizes, *refs):
    n_lon, n_lat = sizes
    names = ["in_" + n for n in LOADS + SMALL] + list(OUTPUTS) + list(SCRATCH)
    R = SimpleNamespace(**dict(zip(names, refs, strict=True)))

    e = lax.axis_index("lon")
    d = lax.axis_index("lat")
    core, xh, z = lax.rem(e, 2), lax.rem(e // 2, 2), e // 4
    xl, y = lax.rem(d, 2), d // 2
    x = xh * 2 + xl
    place = dict(x=x, y=y, z=z)
    e_up, e_dn = lax.rem(e + 1, n_lon), lax.rem(e + n_lon - 1, n_lon)
    d_up, d_dn = lax.rem(d + 1, n_lat), lax.rem(d + n_lat - 1, n_lat)
    last = d == n_lat - 1
    ahead = ((e_up, d), (e, d_up), (e_up, d_up))
    behind = ((e_dn, d), (e, d_dn), (e_dn, d_dn))
    other = (e + 1 - 2 * core, d)

    def device(x, y, z):
        return (z * 4 + (x // 2) * 2 + core, y * 2 + lax.rem(x, 2))

    def along(axis, k):
        at = dict(place)
        at[axis] = lax.rem(at[axis] + k, 4)
        return device(**at)

    loads = SimpleNamespace()
    for n, name in enumerate(LOADS):
        copy = pltpu.make_async_copy(getattr(R, "in_" + name), getattr(R, name), R.load_sem.at[n])
        copy.start()
        setattr(loads, name, copy)

    barrier = pltpu.get_barrier_semaphore()
    partners = list(ahead) + list(behind) + [other]
    for axis in place:
        for k in (1, 2, 3):
            partners.append(along(axis, k))
    for who in partners:
        pl.semaphore_signal(barrier, inc=1, device_id=who, device_id_type=MESH)

    def exchange(n, segs, source, target, to):
        copies = []
        for k in range(3):
            start, size = segs[k + 1]
            rows = pl.ds(start, size)
            copies.append(pltpu.make_async_remote_copy(
                src_ref=source.at[pl.ds(start - segs[0][1], size)],
                dst_ref=target.at[rows],
                send_sem=R.halo_send.at[3 * n + k],
                recv_sem=R.halo_recv.at[3 * n + k],
                device_id=to[k],
                device_id_type=MESH))
        for c in copies:
            c.start()
        return copies

    def wait(copies):
        for c in copies:
            c.wait()

    def take(key, start, size, columns):
        n = list(INDEX).index(key)
        col = R.in_index[pl.ds(start, size), n:n + 1]
        hit = col == lax.broadcasted_iota(jnp.int32, (size, columns), 1)
        return jnp.where(hit, 1.0, 0.0).astype(BF)

    def put(n, name):
        copy = pltpu.make_async_copy(getattr(R, "v_" + name), getattr(R, "o_" + name), R.out_sem.at[n])
        copy.start()
        return copy

    seen = R.in_seen[...]
    seen = jnp.concatenate([seen[:, 0, :], seen[:, 1, :]], axis=0).astype(F32).astype(BF)
    row = lax.broadcasted_iota(jnp.int32, (576, 24), 0)
    col = lax.broadcasted_iota(jnp.int32, (576, 24), 1)
    per = nn(jnp.where(row // 24 == col, 1.0, 0.0).astype(BF), seen)
    present = jnp.sum(jnp.where(lax.rem(row, 24) == col, per, 0.0), axis=-1, keepdims=True) > 0.5

    R.mats[...] = take("s1", 0, 608, 576)
    loads.first.wait()
    R.first[...] = jnp.where(present, R.first[...].astype(F32), R.in_mask[...].astype(BF).astype(F32)).astype(BF)
    R.xs[0] = nn(R.mats[336:, :], R.first[...]).astype(BF)

    R.tables[...] = jnp.zeros((24, 768), F32)
    R.tables[0:8, 0:759] = R.in_table1[...]
    R.tables[8:24, 0:759] = R.in_table2[...]
    table = R.tables[...]
    high = table.astype(BF).astype(F32)
    mid = (table - high).astype(BF).astype(F32)
    low = table - high - mid
    parts = jnp.concatenate([high, mid, low], axis=0).astype(BF)
    parts = nn(parts, take("flip", 0, 768, 768))
    picked = take("pick", 0, 768, 264)

    pl.semaphore_wait(barrier, len(partners))
    halo0 = exchange(0, SEG1, R.xs.at[0], R.xr.at[0], behind)
    R.xr[0, 0:336] = nn(R.mats[0:336, :], R.first[...]).astype(BF)
    loads.cot.wait()
    cot = R.cot[...].reshape(CELLS, 1024)
    R.cs[0] = nn(take("sc", 48, 144, CELLS), cot).astype(BF)
    halo_c = exchange(4, SEG2, R.cs.at[0], R.cr.at[0], behind)
    R.cr[0, 0:48] = nn(take("sc", 0, 48, CELLS), cot).astype(BF)
    R.matr[...] = take("r1", 0, 576, 608)
    R.mats[...] = take("s2", 0, 608, 576)

    def extend(first, heads):
        part = jnp.concatenate([parts[24 * k + first:24 * k + first + heads] for k in range(3)], axis=0)
        for v in range(2):
            for l in range(12):
                shift = (1 - v) * 23 + 11 - l
                moved = pltpu.roll(part, (768 - shift) % 768, 1) if shift else part
                at = (v * 12 + l) * 3 * heads
                R.shifted[at:at + 3 * heads] = moved
        got = nn(R.shifted[0:72 * heads].astype(BF), picked)
        for n in range(24):
            at = n * 3 * heads
            R.ext[first:first + heads, n, :] = (
                got[at:at + heads] + got[at + heads:at + 2 * heads] + got[at + 2 * heads:at + 3 * heads])

    extend(0, 8)
    rows = lax.broadcasted_iota(jnp.int32, (CELLS, CELLS), 0)
    cols = lax.broadcasted_iota(jnp.int32, (CELLS, CELLS), 1)
    apart = jnp.where(jnp.logical_xor(rows < HALF, cols < HALF), NEG, 0.0).astype(F32)
    apart = apart * jnp.where(last, 1.0, 0.0).astype(F32)
    R.madd[...] = jnp.concatenate([apart, apart], axis=1)

    def expand(pair):
        one, two = R.ext[2 * pair], R.ext[2 * pair + 1]
        for a in range(6):
            at = slice((5 - a) * 24, (5 - a) * 24 + CELLS)
            R.bias[pair, a * 24:(a + 1) * 24, :] = jnp.concatenate([one[:, at], two[:, at]], axis=1)

    def expand_masked(pair):
        expand(4 + pair)
        R.bias[4 + pair] = R.bias[4 + pair] + R.madd[...]

    loop(4, expand)

    lane = lax.broadcasted_iota(jnp.int32, (1, 128), 1)
    left = jnp.where(lane < 64, 1.0, 0.0).astype(BF)
    right = jnp.where(lane < 64, 0.0, 1.0).astype(BF)
    is_left = lax.broadcasted_iota(jnp.int32, (CELLS, 128), 1) < 64

    def stack(t):
        return jnp.concatenate([t * left, t * right], axis=0)

    def at(part, pair, width):
        return pl.ds(pl.multiple_of(part * width + pair * 128, 128), 128)

    def heads_of(t):
        return jnp.where(is_left, t[:CELLS], t[CELLS:])

    def attend(q2, k, v, bias):
        score = [nt(b, a) + c for a, b, c in zip(q2, k, bias)]
        expo = [jnp.exp(t - jnp.max(t, axis=0, keepdims=True)) for t in score]
        p = [t * (1.0 / jnp.sum(t, axis=0, keepdims=True)) for t in expo]
        pb = [t.astype(BF) for t in p]
        o = [heads_of(tn(a, b)).astype(BF) for a, b in zip(pb, v)]
        return p, pb, o

    def attend_back(q2, k, v, p, pb, go):
        gw = [nt(a, b) for a, b in zip(v, go)]
        gs = [(a * (b - jnp.sum(a * b, axis=0, keepdims=True))).astype(BF) for a, b in zip(p, gw)]
        gv = [nn(a, b).astype(BF) for a, b in zip(pb, go)]
        gk = [nn(a, b).astype(BF) for a, b in zip(gs, q2)]
        gq = [(heads_of(tn(a, b)) * 0.125).astype(BF) for a, b in zip(gs, k)]
        return gq, gk, gv

    gain1 = R.in_gain1[...]
    wait(halo0)

    def window(w):
        return pl.ds(pl.multiple_of(w * CELLS, 16), CELLS)

    def tile(n, size=256):
        return pl.ds(pl.multiple_of(n * size, size), size)

    def place1(n):
        R.x1[:, tile(n)] = nn(R.matr[...], R.xr[0, :, tile(n)]).astype(BF)

    def norm1(w):
        dev, inv = norm_stats(R.x1[window(w), :].astype(F32))
        R.rolled1[window(w), :] = (dev * inv * gain1).astype(BF)

    loop(2, place1)
    loop(4, norm1)
    loads.w1.wait()

    def qkv1(n):
        c = pl.ds(pl.multiple_of(n * 256, 256), 256)
        R.qkv1[:, c] = nn(R.rolled1[...], R.w1[:, c]).astype(BF)

    loop(6, qkv1)

    def four(pair):
        q2 = [stack(R.qkv1[window(w), at(0, pair, 512)] * BF(0.125)) for w in range(4)]
        k = [R.qkv1[window(w), at(1, pair, 512)] for w in range(4)]
        v = [R.qkv1[window(w), at(2, pair, 512)] for w in range(4)]
        return q2, k, v

    def fwd1(pair):
        bias = R.bias[pair]
        masked = bias + R.madd[...]
        _, pb, o = attend(*four(pair), [bias, masked, bias, masked])
        for w in range(4):
            R.prob1[pair * 4 + w] = pb[w]
            R.mixed1[window(w), at(0, pair, 512)] = o[w]

    loop(4, fwd1)
    loads.p1.wait()

    def proj1(n):
        branch = nn(R.mixed1[...], R.p1[:, tile(n)]).astype(BF).astype(F32)
        R.out1[:, tile(n)] = (R.x1[:, tile(n)].astype(F32) + branch).astype(BF)

    loop(2, proj1)

    R.xs[1] = nn(R.mats[336:, :], R.out1[...]).astype(BF)
    halo1 = exchange(1, SEG1, R.xs.at[1], R.xr.at[1], behind)
    R.xr[1, 0:336] = nn(R.mats[0:336, :], R.out1[...]).astype(BF)
    extend(8, 16)
    loop(8, expand_masked)
    R.mats[...] = take("s3", 0, 608, 576)
    R.matr[...] = take("r2", 0, 576, 608)
    wait(halo_c)
    R.ct[...] = nn(take("rc", 0, CELLS, 192), R.cr[0]).astype(BF)
    loads.p2.wait()

    def grad_mixed2(n):
        c = pl.ds(pl.multiple_of(n * 256, 256), 256)
        R.gm2[:, c] = nt(R.ct[...], R.p2[c, :]).astype(BF)

    loop(4, grad_mixed2)
    R.rolled1t[...] = R.rolled1[...].T
    wait(halo1)
    R.merged[...] = nn(R.matr[...], R.xr[1]).astype(BF)
    loads.wm.wait()
    acc = nn(R.merged[0:CELLS, :], R.wm[0:512, :])
    for s in range(1, 4):
        acc = acc + nn(R.merged[s * CELLS:(s + 1) * CELLS, :], R.wm[s * 512:(s + 1) * 512, :])
    second = acc.astype(BF)
    R.second[...] = second
    gain2 = R.in_gain2[...]
    dev, inv = norm_stats(second.astype(F32))
    rolled2 = (dev * inv * gain2).astype(BF)
    R.rolled2[...] = rolled2
    loads.w2.wait()

    def qkv2(n):
        c = pl.ds(pl.multiple_of(n * 512, 512), 512)
        R.qkv2[:, c] = nn(R.rolled2[...], R.w2[:, c]).astype(BF)

    loop(6, qkv2)

    r2f = rolled2.astype(F32)
    for t in range(4):
        a = r2f[:, t * 256:t * 256 + 128]
        b = r2f[:, t * 256 + 128:t * 256 + 256]
        c = slice(t * 128, t * 128 + 128)
        R.half2[0, :, c] = jnp.where(is_left, a, pltpu.roll(b, 64, 1)).astype(BF)
        R.half2[1, :, c] = jnp.where(is_left, pltpu.roll(a, 64, 1), b).astype(BF)
    core0 = pltpu.make_async_remote_copy(
        src_ref=R.half2.at[1 - core], dst_ref=R.theirs2, send_sem=R.core_send.at[0],
        recv_sem=R.core_recv.at[0], device_id=other, device_id_type=MESH)
    core0.start()

    def both2(u):
        pairs = [u * 4 + n for n in range(4)]
        q2 = [stack(R.qkv2[:, at(0, c, 1024)] * BF(0.125)) for c in pairs]
        k = [R.qkv2[:, at(1, c, 1024)] for c in pairs]
        v = [R.qkv2[:, at(2, c, 1024)] for c in pairs]
        go = [stack(R.gm2[:, at(0, c, 1024)]) for c in pairs]
        p, pb, o = attend(q2, k, v, [R.bias[4 + c] for c in pairs])
        back = attend_back(q2, k, v, p, pb, go)
        for n, c in enumerate(pairs):
            R.mixed2[:, at(0, c, 1024)] = o[n]
            for part in range(3):
                R.dqkv2[0, :, at(part, c, 1024)] = back[part][n]

    loop(2, both2)
    core1 = pltpu.make_async_remote_copy(
        src_ref=R.dqkv2.at[0], dst_ref=R.dqkv2.at[1], send_sem=R.core_send.at[1],
        recv_sem=R.core_recv.at[1], device_id=other, device_id_type=MESH)
    core1.start()

    grad_rolled = nt(R.dqkv2[0, :, 0:1024], R.w2[:, 0:1024])
    grad_rolled = grad_rolled + nt(R.dqkv2[0, :, 1024:2048], R.w2[:, 1024:2048])
    grad_rolled = grad_rolled + nt(R.dqkv2[0, :, 2048:3072], R.w2[:, 2048:3072])

    def norm_back(grad, xin, gain, grad_out):
        grad = grad.astype(BF).astype(F32) * gain
        dev, inv = norm_stats(xin.astype(F32))
        hat = dev * inv
        inner = inv * (grad - jnp.mean(grad, axis=-1, keepdims=True)
                       - hat * jnp.mean(grad * hat, axis=-1, keepdims=True))
        return (grad_out.astype(F32) + inner.astype(BF).astype(F32)).astype(BF)

    R.gs[...] = norm_back(grad_rolled, R.second[...], gain2, R.ct[...])
    for s in range(4):
        R.merged[s * CELLS:(s + 1) * CELLS, :] = nt(R.gs[...], R.wm[s * 512:(s + 1) * 512, :]).astype(BF)
    R.xs[2] = nn(R.mats[336:, :], R.merged[...]).astype(BF)
    halo2 = exchange(2, SEG1, R.xs.at[2], R.xr.at[2], ahead)
    R.xr[2, 0:336] = nn(R.mats[0:336, :], R.merged[...]).astype(BF)

    R.halft[0] = R.half2[core].T
    core0.wait()
    R.halft[1] = R.theirs2[...].T
    core1.wait()

    def term2(yy):
        c = tile(yy, 768)
        g = nn(R.halft[0], R.dqkv2[0, :, c]) + nn(R.halft[1], R.dqkv2[1, :, c])
        g = g.astype(BF)
        for zz in range(4):
            for hh in range(2):
                r = (zz * 2 + hh) * 64
                for xx in range(2):
                    at = dict(z=zz, x=hh * 2 + xx, y=yy)
                    for p, order in enumerate(ORDERS):
                        block = (at[order[0]] * 4 + at[order[1]]) * 4 + at[order[2]]
                        lanes = xx * 384 + p * 128
                        R.b2[p, block] = g[r:r + 64, lanes:lanes + 128]

    loop(4, term2)

    def rs_start(buf, recv, sem0, step):
        copies = []
        for p, order in enumerate(ORDERS):
            base = 0
            for s in range(step):
                base = base + place[order[s]] * (16 >> (2 * s))
            size = 16 >> (2 * step)
            axis = order[step]
            for k in (1, 2, 3):
                to = lax.rem(place[axis] + k, 4)
                n = sem0 + (step * 3 + p) * 3 + k - 1
                copies.append(pltpu.make_async_remote_copy(
                    src_ref=buf.at[p, pl.ds(base + to * size, size)],
                    dst_ref=recv.at[p, k - 1],
                    send_sem=R.rs_send.at[n],
                    recv_sem=R.rs_recv.at[n],
                    device_id=along(axis, k),
                    device_id_type=MESH))
        for c in copies:
            c.start()
        return copies

    def rs_add(buf, recv, step, copies):
        wait(copies)
        size = 16 >> (2 * step)
        for p, order in enumerate(ORDERS):
            base = 0
            for s in range(step + 1):
                base = base + place[order[s]] * (16 >> (2 * s))

            step_of = min(size, 65536 // (buf.shape[2] * buf.shape[3]))

            def add(n):
                at = pl.ds(base + n * step_of, step_of)
                near = pl.ds(n * step_of, step_of)
                t = buf[p, at].astype(F32) + recv[p, 0, near].astype(F32)
                t = t + recv[p, 1, near].astype(F32) + recv[p, 2, near].astype(F32)
                buf[p, at] = t.astype(BF)

            loop(size // step_of, add)

    def rs_last(buf, recv, p, copies):
        order = ORDERS[p]
        base = (place[order[0]] * 4 + place[order[1]]) * 4 + place[order[2]]
        t = buf[p, base].astype(F32) + recv[p, 0, 0].astype(F32)
        return t + recv[p, 1, 0].astype(F32) + recv[p, 2, 0].astype(F32)

    big = rs_start(R.b2, R.b2r0, 0, 0)
    R.mats[...] = take("s4", 0, 608, 576)
    R.matr[...] = take("r3", 0, 576, 608)

    wait(halo2)
    R.g1[...] = nn(R.matr[...], R.xr[2]).astype(BF)

    def grad_mixed1(n):
        R.gm1[:, tile(n)] = nt(R.g1[...], R.p1[tile(n), :]).astype(BF)

    loop(2, grad_mixed1)

    def bwd1(pair):
        q2, k, v = four(pair)
        go = [stack(R.gm1[window(w), at(0, pair, 512)]) for w in range(4)]
        pb = [R.prob1[pair * 4 + w] for w in range(4)]
        back = attend_back(q2, k, v, [t.astype(F32) for t in pb], pb, go)
        for w in range(4):
            for part in range(3):
                R.dqkv1[window(w), at(part, pair, 512)] = back[part][w]

    loop(4, bwd1)

    def to_core(t):
        return pltpu.make_async_remote_copy(
            src_ref=R.b1h.at[t, 1 - core], dst_ref=R.b1c.at[t], send_sem=R.core_send.at[2 + t],
            recv_sem=R.core_recv.at[2 + t], device_id=other, device_id_type=MESH)

    def term1(t):
        c = pl.ds(pl.multiple_of(t * 384, 128), 384)
        g = nn(R.rolled1t[...], R.dqkv1[:, c])
        pick = is_left[0:16]
        for zz in range(4):
            for hh in range(2):
                for cc in range(2):
                    r = ((zz * 2 + hh) * 2 + cc) * 32
                    upper = g[r:r + 16, 128:256]
                    lower = pltpu.roll(g[r + 16:r + 32, 128:256], 64, 1)
                    mixes = (jnp.where(pick, upper, lower), jnp.where(pick, lower, upper))
                    for odd in range(2):
                        lanes = slice(odd * 256, odd * 256 + 128)
                        pieces = (g[r:r + 16, lanes], g[r + 16:r + 32, lanes], mixes[odd])
                        for p in range(3):
                            R.b1h[t, cc, p, zz * 4 + hh * 2 + odd] = pieces[p].astype(BF)
        to_core(t).start()

    loop(4, term1)
    rs_add(R.b2, R.b2r0, 0, big)
    big = rs_start(R.b2, R.b2r1, 0, 1)

    for t in range(4):
        to_core(t).wait()
        for p, order in enumerate(ORDERS):
            g = R.b1h[t, core, p].astype(F32) + R.b1c[t, p].astype(F32)
            for n in range(16):
                at = dict(z=n // 4, x=n % 4, y=t)
                block = (at[order[0]] * 4 + at[order[1]]) * 4 + at[order[2]]
                R.b1[p, block] = g[n].astype(BF)
    mine = R.b1
    small = rs_start(mine, R.b1r0, 27, 0)

    def grad_rolled1(n):
        R.gm1[:, tile(n)] = nt(R.dqkv1[...], R.w1[tile(n), :]).astype(BF)

    def tail1(w):
        r = window(w)
        R.out1[r, :] = norm_back(R.gm1[r, :], R.x1[r, :], gain1, R.g1[r, :])

    loop(2, grad_rolled1)
    loop(4, tail1)
    R.xs[3] = nn(R.mats[336:, :], R.out1[...]).astype(BF)
    halo3 = exchange(3, SEG1, R.xs.at[3], R.xr.at[3], ahead)
    R.xr[3, 0:336] = nn(R.mats[0:336, :], R.out1[...]).astype(BF)

    branch = nn(R.mixed2[...], R.p2[...]).astype(BF).astype(F32)
    R.res[...] = (R.second[...].astype(F32) + branch).astype(BF)
    R.cs[1] = nn(take("sr", 48, 144, CELLS), R.res[...]).astype(BF)
    halo_r = exchange(5, SEG2, R.cs.at[1], R.cr.at[1], ahead)
    R.cr[1, 0:48] = nn(take("sr", 0, 48, CELLS), R.res[...]).astype(BF)

    R.matr[...] = take("r4", 0, 576, 608)
    rs_add(mine, R.b1r0, 0, small)
    small = rs_start(mine, R.b1r1, 27, 1)
    rs_add(R.b2, R.b2r1, 1, big)
    big = rs_start(R.b2, R.b2r2, 0, 2)
    wait(halo_r)
    R.v_res[...] = nn(take("rr", 0, CELLS, 192), R.cr[1]).astype(BF).reshape(72, 2, 1024)
    puts = [put(0, "res")]
    rs_add(mine, R.b1r1, 1, small)
    small = rs_start(mine, R.b1r2, 27, 2)
    wait(halo3)
    R.v_tok[...] = jnp.where(present, nn(R.matr[...], R.xr[3]), 0.0).astype(BF)
    puts.append(put(1, "tok"))
    wait(big)
    for p in range(3):
        R.v_q2[:, p * 128:(p + 1) * 128] = rs_last(R.b2, R.b2r2, p, big)
    puts.append(put(3, "q2"))
    wait(small)
    a, b, m = [rs_last(mine, R.b1r2, p, small) for p in range(3)]
    turned = pltpu.roll(m, 64, 1)
    even = xl == 0
    a_turned = pltpu.roll(a, 64, 1)
    b_turned = pltpu.roll(b, 64, 1)
    pick = is_left[0:16]
    R.v_q1[0:16, 0:128] = jnp.where(even, a, jnp.where(pick, turned, a_turned))
    R.v_q1[16:32, 0:128] = jnp.where(even, b, jnp.where(pick, m, b_turned))
    R.v_q1[0:16, 128:192] = jnp.where(even, m, a_turned)[:, 0:64]
    R.v_q1[16:32, 128:192] = jnp.where(even, turned, b_turned)[:, 0:64]
    puts.append(put(2, "q1"))
    wait(puts)


def hand_on(*refs):
    given, out, held, sem = refs[0:4], refs[4:8], refs[8:12], refs[12]
    come = [pltpu.make_async_copy(given[n], held[n], sem.at[n]) for n in range(4)]
    leave = [pltpu.make_async_copy(held[n], out[n], sem.at[4 + n]) for n in range(4)]
    for c in come:
        c.start()
    for n in range(4):
        come[n].wait()
        leave[n].start()
    for c in leave:
        c.wait()


def shards(tokens, observed, mask_token, gain_one, qkv_one, table_one, proj_one, merge_weight, gain_two, qkv_two,
           table_two, proj_two, cotangent, sizes):
    first = tokens.transpose(0, 2, 1, 3).reshape(576, 512)
    cot = cotangent.transpose(1, 2, 0, 3).reshape(72, 2, 1024)
    seen = observed.transpose(2, 0, 1)
    given = dict(first=first, cot=cot, w1=qkv_one, p1=proj_one, wm=merge_weight, w2=qkv_two, p2=proj_two)
    args = [given[k] for k in LOADS]
    args += [jnp.asarray(TABLE_OF), seen, mask_token[None], table_one, table_two, gain_one[None], gain_two[None]]
    shapes = (
        jax.ShapeDtypeStruct((72, 2, 1024), BF),
        jax.ShapeDtypeStruct((576, 512), BF),
        jax.ShapeDtypeStruct((32, 192), F32),
        jax.ShapeDtypeStruct((64, 384), F32),
    )
    outs = pl.pallas_call(
        functools.partial(body, sizes),
        out_shape=shapes,
        in_specs=[pl.BlockSpec(memory_space=pl.ANY)] * len(LOADS) + [pl.BlockSpec(memory_space=pltpu.VMEM)] * len(SMALL),
        out_specs=[pl.BlockSpec(memory_space=pl.ANY)] * 4,
        scratch_shapes=list(SCRATCH.values()),
        compiler_params=pltpu.CompilerParams(
            collective_id=0, has_side_effects=True, vmem_limit_bytes=62 * 1024 * 1024),
        cost_estimate=pl.CostEstimate(flops=9 * 10 ** 9, bytes_accessed=24 * 10 ** 6, transcendentals=10 ** 6),
    )(*args)
    res, tok, q1, q2 = pl.pallas_call(
        hand_on,
        out_shape=shapes,
        in_specs=[pl.BlockSpec(memory_space=pl.ANY)] * 4,
        out_specs=[pl.BlockSpec(memory_space=pl.ANY)] * 4,
        scratch_shapes=[pltpu.VMEM(s.shape, s.dtype) for s in shapes] + [pltpu.SemaphoreType.DMA((8,))],
    )(*outs)
    result = res.reshape(12, 6, 2, 1024).transpose(2, 0, 1, 3)
    grad_tokens = tok.reshape(2, 12, 24, 512).transpose(0, 2, 1, 3)
    return (result, grad_tokens, q1, q2)


def solution(mesh):
    sizes = (mesh.shape["lon"], mesh.shape["lat"])
    split = P(None, "lon", "lat", None)

    def run(*args):
        return shards(*args, sizes)

    return jax.shard_map(
        run,
        mesh=mesh,
        in_specs=(split, P(None, "lon", "lat")) + (P(),) * 10 + (split,),
        out_specs=(split, split, P("lon", "lat"), P("lon", "lat")),
        check_vma=False,
    )
```

```python
import functools
from types import SimpleNamespace
import numpy as np
import jax
import jax.numpy as jnp
from jax import lax
from jax.experimental import pallas as pl
from jax.experimental.pallas import tpu as pltpu
from jax.sharding import PartitionSpec as P

BF = jnp.bfloat16
F32 = jnp.float32
EPS = 1e-05
NEG = -1000000000.0
MESH = pl.DeviceIdType.MESH
CELLS = 144
HALF = 72

SEG1 = ((0, 336), (336, 112), (448, 112), (560, 48))
SEG2 = ((0, 48), (48, 48), (96, 48), (144, 48))


def _cells(along, across, half_lon, half_lat):
    out = [[], [], [], []]
    for v in range(2):
        for i in range(along):
            for j in range(across):
                seg = (1 if i < half_lon else 0) + (2 if j < half_lat else 0)
                moved = (v, (i - half_lon) % along, (j - half_lat) % across)
                out[seg].append(((v, i, j), moved))
    return out


def _send_index(segs, cells, row_of):
    out = [-1] * (segs[-1][0] + segs[-1][1])
    for (start, _), members in zip(segs, cells):
        for n, (cell, _) in enumerate(members):
            out[start + n] = row_of(*cell)
    return out


def _recv_index(segs, cells, row_of, rows):
    out = [-1] * rows
    for (start, _), members in zip(segs, cells):
        for n, (_, moved) in enumerate(members):
            out[row_of(*moved)] = start + n
    return out


def _inverse(index, rows):
    out = [-1] * rows
    for n, m in enumerate(index):
        if m >= 0:
            out[m] = n
    return out


def _nat1(v, i, j):
    return (v * 12 + j) * 24 + i


def _win1(v, i, j):
    return ((i // 12) * 2 + j // 6) * CELLS + (j % 6) * 24 + v * 12 + i % 12


def _merge(v, i, j):
    return ((i % 2) * 2 + j % 2) * CELLS + (j // 2) * 24 + v * 12 + i // 2


def _nat2(v, i, j):
    return (i * 6 + j) * 2 + v


def _win2(v, i, j):
    return j * 24 + v * 12 + i


def _indices():
    one = _cells(24, 12, 6, 3)
    two = _cells(12, 6, 6, 3)
    s1 = _send_index(SEG1, one, _nat1)
    r1 = _recv_index(SEG1, one, _win1, 576)
    s2 = _send_index(SEG1, one, _win1)
    r2 = _recv_index(SEG1, one, _merge, 576)
    sc = _send_index(SEG2, two, _nat2)
    rc = _recv_index(SEG2, two, _win2, CELLS)
    flip = [-1] * 768
    for x in range(3):
        for y in range(23):
            for z in range(11):
                flip[(x * 23 + y) * 11 + z] = z * 69 + x * 23 + y
    pick = [-1] * 768
    for z in range(11):
        for v in range(2):
            for l in range(12):
                pick[z * 69 + v * 23 + l] = z * 24 + v * 12 + l
    return dict(s1=s1, r1=r1, s2=s2, r2=r2, s3=_inverse(r2, 608), r3=_inverse(s2, 576), s4=_inverse(r1, 608),
                r4=_inverse(s1, 576), sc=sc, rc=rc, sr=_inverse(rc, 192), rr=_inverse(sc, CELLS), flip=flip, pick=pick)


INDEX = _indices()
TABLE_OF = np.full((768, len(INDEX)), -1, np.int32)
for _n, _rows in enumerate(INDEX.values()):
    TABLE_OF[:len(_rows), _n] = _rows

SHAPES = dict(first=(576, 512), cot=(72, 2, 1024), w1=(512, 1536), p1=(512, 512), p2=(1024, 1024),
              wm=(2048, 1024), w2=(1024, 3072))
LOADS = tuple(SHAPES)


def nn(a, b):
    return lax.dot_general(a, b, (((1,), (0,)), ((), ())), preferred_element_type=F32)


def nt(a, b):
    return lax.dot_general(a, b, (((1,), (1,)), ((), ())), preferred_element_type=F32)


def tn(a, b):
    return lax.dot_general(a, b, (((0,), (0,)), ((), ())), preferred_element_type=F32)


def norm_stats(x):
    centre = jnp.mean(x, axis=-1, keepdims=True)
    dev = x - centre
    spread = jnp.mean(dev * dev, axis=-1, keepdims=True)
    return dev, lax.rsqrt(spread + EPS)


def loop(n, body):
    lax.fori_loop(0, n, lambda i, c: (body(i), c)[1], 0)


SCRATCH = dict(
    {k: pltpu.VMEM(SHAPES[k], BF) for k in LOADS},
    mats=pltpu.VMEM((608, 576), BF),
    matr=pltpu.VMEM((576, 608), BF),
    tables=pltpu.VMEM((24, 768), F32),
    shifted=pltpu.VMEM((1152, 768), F32),
    ext=pltpu.VMEM((24, 24, 264), F32),
    bias=pltpu.VMEM((12, CELLS, 288), F32),
    madd=pltpu.VMEM((CELLS, 288), F32),
    xr=pltpu.VMEM((4, 608, 512), BF),
    xs=pltpu.VMEM((4, 272, 512), BF),
    cr=pltpu.VMEM((2, 192, 1024), BF),
    cs=pltpu.VMEM((2, 144, 1024), BF),
    x1=pltpu.VMEM((576, 512), BF),
    rolled1=pltpu.VMEM((576, 512), BF),
    rolled1t=pltpu.VMEM((512, 576), BF),
    qkv1=pltpu.VMEM((576, 1536), BF),
    dqkv1=pltpu.VMEM((576, 1536), BF),
    prob1=pltpu.VMEM((16, CELLS, 288), BF),
    mixed1=pltpu.VMEM((576, 512), BF),
    out1=pltpu.VMEM((576, 512), BF),
    gm1=pltpu.VMEM((576, 512), BF),
    g1=pltpu.VMEM((576, 512), BF),
    merged=pltpu.VMEM((576, 512), BF),
    second=pltpu.VMEM((CELLS, 1024), BF),
    rolled2=pltpu.VMEM((CELLS, 1024), BF),
    qkv2=pltpu.VMEM((CELLS, 3072), BF),
    dqkv2=pltpu.VMEM((2, CELLS, 3072), BF),
    half2=pltpu.VMEM((2, CELLS, 512), BF),
    theirs2=pltpu.VMEM((CELLS, 512), BF),
    halft=pltpu.VMEM((2, 512, CELLS), BF),
    mixed2=pltpu.VMEM((CELLS, 1024), BF),
    ct=pltpu.VMEM((CELLS, 1024), BF),
    gm2=pltpu.VMEM((CELLS, 1024), BF),
    res=pltpu.VMEM((CELLS, 1024), BF),
    gs=pltpu.VMEM((CELLS, 1024), BF),
    v_res=pltpu.VMEM((72, 2, 1024), BF),
    v_tok=pltpu.VMEM((576, 512), BF),
    v_q1=pltpu.VMEM((32, 192), F32),
    v_q2=pltpu.VMEM((64, 384), F32),
    out_sem=pltpu.SemaphoreType.DMA((4,)),
    b2=pltpu.VMEM((3, 64, 64, 128), BF),
    b2v0=pltpu.VMEM((3, 2, 8, 64, 128), BF),
    b2r0=pltpu.VMEM((3, 2, 16, 64, 128), BF),
    b2v1=pltpu.VMEM((3, 2, 2, 64, 128), BF),
    b2r1=pltpu.VMEM((3, 2, 4, 64, 128), BF),
    b2r2=pltpu.VMEM((3, 3, 1, 64, 128), BF),
    b1=pltpu.VMEM((3, 64, 16, 128), BF),
    b1h=pltpu.VMEM((4, 2, 3, 16, 16, 128), BF),
    b1c=pltpu.VMEM((4, 3, 16, 16, 128), BF),
    b1r0=pltpu.VMEM((3, 3, 16, 16, 128), BF),
    b1r1=pltpu.VMEM((3, 3, 4, 16, 128), BF),
    b1r2=pltpu.VMEM((3, 3, 1, 16, 128), BF),
    load_sem=pltpu.SemaphoreType.DMA((len(LOADS),)),
    halo_send=pltpu.SemaphoreType.DMA((18,)),
    halo_recv=pltpu.SemaphoreType.DMA((18,)),
    rs_send=pltpu.SemaphoreType.DMA((54,)),
    rs_recv=pltpu.SemaphoreType.DMA((54,)),
    ring_send=pltpu.SemaphoreType.DMA((36,)),
    ring_recv=pltpu.SemaphoreType.DMA((36,)),
    core_send=pltpu.SemaphoreType.DMA((6,)),
    core_recv=pltpu.SemaphoreType.DMA((6,)),
)
SMALL = ("index", "seen", "mask", "table1", "table2", "gain1", "gain2")
OUTPUTS = ("o_res", "o_tok", "o_q1", "o_q2")

ORDERS = (("z", "x", "y"), ("x", "y", "z"), ("y", "z", "x"))


def body(sizes, *refs):
    n_lon, n_lat = sizes
    names = ["in_" + n for n in LOADS + SMALL] + list(OUTPUTS) + list(SCRATCH)
    R = SimpleNamespace(**dict(zip(names, refs, strict=True)))

    e = lax.axis_index("lon")
    d = lax.axis_index("lat")
    core, xh, z = lax.rem(e, 2), lax.rem(e // 2, 2), e // 4
    xl, y = lax.rem(d, 2), d // 2
    x = xh * 2 + xl
    place = dict(x=x, y=y, z=z)
    e_up, e_dn = lax.rem(e + 1, n_lon), lax.rem(e + n_lon - 1, n_lon)
    d_up, d_dn = lax.rem(d + 1, n_lat), lax.rem(d + n_lat - 1, n_lat)
    last = d == n_lat - 1
    ahead = ((e_up, d), (e, d_up), (e_up, d_up))
    behind = ((e_dn, d), (e, d_dn), (e_dn, d_dn))
    other = (e + 1 - 2 * core, d)

    def device(x, y, z):
        return (z * 4 + (x // 2) * 2 + core, y * 2 + lax.rem(x, 2))

    def along(axis, k):
        at = dict(place)
        at[axis] = lax.rem(at[axis] + k, 4)
        return device(**at)

    loads = SimpleNamespace()
    for n, name in enumerate(LOADS):
        copy = pltpu.make_async_copy(getattr(R, "in_" + name), getattr(R, name), R.load_sem.at[n])
        copy.start()
        setattr(loads, name, copy)

    barrier = pltpu.get_barrier_semaphore()
    partners = list(ahead) + list(behind) + [other]
    for axis in place:
        for k in (1, 2, 3):
            partners.append(along(axis, k))
    for who in partners:
        pl.semaphore_signal(barrier, inc=1, device_id=who, device_id_type=MESH)

    def exchange(n, segs, source, target, to):
        copies = []
        for k in range(3):
            start, size = segs[k + 1]
            rows = pl.ds(start, size)
            copies.append(pltpu.make_async_remote_copy(
                src_ref=source.at[pl.ds(start - segs[0][1], size)],
                dst_ref=target.at[rows],
                send_sem=R.halo_send.at[3 * n + k],
                recv_sem=R.halo_recv.at[3 * n + k],
                device_id=to[k],
                device_id_type=MESH))
        for c in copies:
            c.start()
        return copies

    def wait(copies):
        for c in copies:
            c.wait()

    def take(key, start, size, columns):
        n = list(INDEX).index(key)
        col = R.in_index[pl.ds(start, size), n:n + 1]
        hit = col == lax.broadcasted_iota(jnp.int32, (size, columns), 1)
        return jnp.where(hit, 1.0, 0.0).astype(BF)

    def put(n, name):
        copy = pltpu.make_async_copy(getattr(R, "v_" + name), getattr(R, "o_" + name), R.out_sem.at[n])
        copy.start()
        return copy

    seen = R.in_seen[...]
    seen = jnp.concatenate([seen[:, 0, :], seen[:, 1, :]], axis=0).astype(F32).astype(BF)
    row = lax.broadcasted_iota(jnp.int32, (576, 24), 0)
    col = lax.broadcasted_iota(jnp.int32, (576, 24), 1)
    per = nn(jnp.where(row // 24 == col, 1.0, 0.0).astype(BF), seen)
    present = jnp.sum(jnp.where(lax.rem(row, 24) == col, per, 0.0), axis=-1, keepdims=True) > 0.5

    R.mats[...] = take("s1", 0, 608, 576)
    loads.first.wait()
    R.first[...] = jnp.where(present, R.first[...].astype(F32), R.in_mask[...].astype(BF).astype(F32)).astype(BF)
    R.xs[0] = nn(R.mats[336:, :], R.first[...]).astype(BF)

    R.tables[...] = jnp.zeros((24, 768), F32)
    R.tables[0:8, 0:759] = R.in_table1[...]
    R.tables[8:24, 0:759] = R.in_table2[...]
    table = R.tables[...]
    high = table.astype(BF).astype(F32)
    mid = (table - high).astype(BF).astype(F32)
    low = table - high - mid
    parts = jnp.concatenate([high, mid, low], axis=0).astype(BF)
    parts = nn(parts, take("flip", 0, 768, 768))
    picked = take("pick", 0, 768, 264)

    pl.semaphore_wait(barrier, len(partners))
    halo0 = exchange(0, SEG1, R.xs.at[0], R.xr.at[0], behind)
    R.xr[0, 0:336] = nn(R.mats[0:336, :], R.first[...]).astype(BF)
    loads.cot.wait()
    cot = R.cot[...].reshape(CELLS, 1024)
    R.cs[0] = nn(take("sc", 48, 144, CELLS), cot).astype(BF)
    halo_c = exchange(4, SEG2, R.cs.at[0], R.cr.at[0], behind)
    R.cr[0, 0:48] = nn(take("sc", 0, 48, CELLS), cot).astype(BF)
    R.matr[...] = take("r1", 0, 576, 608)
    R.mats[...] = take("s2", 0, 608, 576)

    def extend(first, heads):
        part = jnp.concatenate([parts[24 * k + first:24 * k + first + heads] for k in range(3)], axis=0)
        for v in range(2):
            for l in range(12):
                shift = (1 - v) * 23 + 11 - l
                moved = pltpu.roll(part, (768 - shift) % 768, 1) if shift else part
                at = (v * 12 + l) * 3 * heads
                R.shifted[at:at + 3 * heads] = moved
        got = nn(R.shifted[0:72 * heads].astype(BF), picked)
        for n in range(24):
            at = n * 3 * heads
            R.ext[first:first + heads, n, :] = (
                got[at:at + heads] + got[at + heads:at + 2 * heads] + got[at + 2 * heads:at + 3 * heads])

    extend(0, 8)
    rows = lax.broadcasted_iota(jnp.int32, (CELLS, CELLS), 0)
    cols = lax.broadcasted_iota(jnp.int32, (CELLS, CELLS), 1)
    apart = jnp.where(jnp.logical_xor(rows < HALF, cols < HALF), NEG, 0.0).astype(F32)
    apart = apart * jnp.where(last, 1.0, 0.0).astype(F32)
    R.madd[...] = jnp.concatenate([apart, apart], axis=1)

    def expand(pair):
        one, two = R.ext[2 * pair], R.ext[2 * pair + 1]
        for a in range(6):
            at = slice((5 - a) * 24, (5 - a) * 24 + CELLS)
            R.bias[pair, a * 24:(a + 1) * 24, :] = jnp.concatenate([one[:, at], two[:, at]], axis=1)

    def expand_masked(pair):
        expand(4 + pair)
        R.bias[4 + pair] = R.bias[4 + pair] + R.madd[...]

    loop(4, expand)

    lane = lax.broadcasted_iota(jnp.int32, (1, 128), 1)
    left = jnp.where(lane < 64, 1.0, 0.0).astype(BF)
    right = jnp.where(lane < 64, 0.0, 1.0).astype(BF)
    is_left = lax.broadcasted_iota(jnp.int32, (CELLS, 128), 1) < 64

    def stack(t):
        return jnp.concatenate([t * left, t * right], axis=0)

    def at(part, pair, width):
        return pl.ds(pl.multiple_of(part * width + pair * 128, 128), 128)

    def heads_of(t):
        return jnp.where(is_left, t[:CELLS], t[CELLS:])

    def attend(q2, k, v, bias):
        score = [nt(b, a) + c for a, b, c in zip(q2, k, bias)]
        expo = [jnp.exp(t - jnp.max(t, axis=0, keepdims=True)) for t in score]
        p = [t * (1.0 / jnp.sum(t, axis=0, keepdims=True)) for t in expo]
        pb = [t.astype(BF) for t in p]
        o = [heads_of(tn(a, b)).astype(BF) for a, b in zip(pb, v)]
        return p, pb, o

    def attend_back(q2, k, v, p, pb, go):
        gw = [nt(a, b) for a, b in zip(v, go)]
        gs = [(a * (b - jnp.sum(a * b, axis=0, keepdims=True))).astype(BF) for a, b in zip(p, gw)]
        gv = [nn(a, b).astype(BF) for a, b in zip(pb, go)]
        gk = [nn(a, b).astype(BF) for a, b in zip(gs, q2)]
        gq = [(heads_of(tn(a, b)) * 0.125).astype(BF) for a, b in zip(gs, k)]
        return gq, gk, gv

    gain1 = R.in_gain1[...]
    wait(halo0)

    def window(w):
        return pl.ds(pl.multiple_of(w * CELLS, 16), CELLS)

    def tile(n, size=256):
        return pl.ds(pl.multiple_of(n * size, size), size)

    def place1(n):
        R.x1[:, tile(n)] = nn(R.matr[...], R.xr[0, :, tile(n)]).astype(BF)

    def norm1(w):
        dev, inv = norm_stats(R.x1[window(w), :].astype(F32))
        R.rolled1[window(w), :] = (dev * inv * gain1).astype(BF)

    loop(2, place1)
    loop(4, norm1)
    loads.w1.wait()

    def qkv1(n):
        c = pl.ds(pl.multiple_of(n * 256, 256), 256)
        R.qkv1[:, c] = nn(R.rolled1[...], R.w1[:, c]).astype(BF)

    loop(6, qkv1)

    def four(pair):
        q2 = [stack(R.qkv1[window(w), at(0, pair, 512)] * BF(0.125)) for w in range(4)]
        k = [R.qkv1[window(w), at(1, pair, 512)] for w in range(4)]
        v = [R.qkv1[window(w), at(2, pair, 512)] for w in range(4)]
        return q2, k, v

    def fwd1(pair):
        bias = R.bias[pair]
        masked = bias + R.madd[...]
        _, pb, o = attend(*four(pair), [bias, masked, bias, masked])
        for w in range(4):
            R.prob1[pair * 4 + w] = pb[w]
            R.mixed1[window(w), at(0, pair, 512)] = o[w]

    loop(4, fwd1)
    loads.p1.wait()

    def proj1(n):
        branch = nn(R.mixed1[...], R.p1[:, tile(n)]).astype(BF).astype(F32)
        R.out1[:, tile(n)] = (R.x1[:, tile(n)].astype(F32) + branch).astype(BF)

    loop(2, proj1)

    R.xs[1] = nn(R.mats[336:, :], R.out1[...]).astype(BF)
    halo1 = exchange(1, SEG1, R.xs.at[1], R.xr.at[1], behind)
    R.xr[1, 0:336] = nn(R.mats[0:336, :], R.out1[...]).astype(BF)
    extend(8, 16)
    loop(8, expand_masked)
    R.mats[...] = take("s3", 0, 608, 576)
    R.matr[...] = take("r2", 0, 576, 608)
    wait(halo_c)
    R.ct[...] = nn(take("rc", 0, CELLS, 192), R.cr[0]).astype(BF)
    loads.p2.wait()

    def grad_mixed2(n):
        c = pl.ds(pl.multiple_of(n * 256, 256), 256)
        R.gm2[:, c] = nt(R.ct[...], R.p2[c, :]).astype(BF)

    loop(4, grad_mixed2)
    R.rolled1t[...] = R.rolled1[...].T
    wait(halo1)
    R.merged[...] = nn(R.matr[...], R.xr[1]).astype(BF)
    loads.wm.wait()
    acc = nn(R.merged[0:CELLS, :], R.wm[0:512, :])
    for s in range(1, 4):
        acc = acc + nn(R.merged[s * CELLS:(s + 1) * CELLS, :], R.wm[s * 512:(s + 1) * 512, :])
    second = acc.astype(BF)
    R.second[...] = second
    gain2 = R.in_gain2[...]
    dev, inv = norm_stats(second.astype(F32))
    rolled2 = (dev * inv * gain2).astype(BF)
    R.rolled2[...] = rolled2
    loads.w2.wait()

    def qkv2(n):
        c = pl.ds(pl.multiple_of(n * 512, 512), 512)
        R.qkv2[:, c] = nn(R.rolled2[...], R.w2[:, c]).astype(BF)

    loop(6, qkv2)

    r2f = rolled2.astype(F32)
    for t in range(4):
        a = r2f[:, t * 256:t * 256 + 128]
        b = r2f[:, t * 256 + 128:t * 256 + 256]
        c = slice(t * 128, t * 128 + 128)
        R.half2[0, :, c] = jnp.where(is_left, a, pltpu.roll(b, 64, 1)).astype(BF)
        R.half2[1, :, c] = jnp.where(is_left, pltpu.roll(a, 64, 1), b).astype(BF)
    core0 = pltpu.make_async_remote_copy(
        src_ref=R.half2.at[1 - core], dst_ref=R.theirs2, send_sem=R.core_send.at[0],
        recv_sem=R.core_recv.at[0], device_id=other, device_id_type=MESH)
    core0.start()

    def both2(u):
        pairs = [u * 4 + n for n in range(4)]
        q2 = [stack(R.qkv2[:, at(0, c, 1024)] * BF(0.125)) for c in pairs]
        k = [R.qkv2[:, at(1, c, 1024)] for c in pairs]
        v = [R.qkv2[:, at(2, c, 1024)] for c in pairs]
        go = [stack(R.gm2[:, at(0, c, 1024)]) for c in pairs]
        p, pb, o = attend(q2, k, v, [R.bias[4 + c] for c in pairs])
        back = attend_back(q2, k, v, p, pb, go)
        for n, c in enumerate(pairs):
            R.mixed2[:, at(0, c, 1024)] = o[n]
            for part in range(3):
                R.dqkv2[0, :, at(part, c, 1024)] = back[part][n]

    loop(2, both2)
    core1 = pltpu.make_async_remote_copy(
        src_ref=R.dqkv2.at[0], dst_ref=R.dqkv2.at[1], send_sem=R.core_send.at[1],
        recv_sem=R.core_recv.at[1], device_id=other, device_id_type=MESH)
    core1.start()

    grad_rolled = nt(R.dqkv2[0, :, 0:1024], R.w2[:, 0:1024])
    grad_rolled = grad_rolled + nt(R.dqkv2[0, :, 1024:2048], R.w2[:, 1024:2048])
    grad_rolled = grad_rolled + nt(R.dqkv2[0, :, 2048:3072], R.w2[:, 2048:3072])

    def norm_back(grad, xin, gain, grad_out):
        grad = grad.astype(BF).astype(F32) * gain
        dev, inv = norm_stats(xin.astype(F32))
        hat = dev * inv
        inner = inv * (grad - jnp.mean(grad, axis=-1, keepdims=True)
                       - hat * jnp.mean(grad * hat, axis=-1, keepdims=True))
        return (grad_out.astype(F32) + inner.astype(BF).astype(F32)).astype(BF)

    R.gs[...] = norm_back(grad_rolled, R.second[...], gain2, R.ct[...])
    for s in range(4):
        R.merged[s * CELLS:(s + 1) * CELLS, :] = nt(R.gs[...], R.wm[s * 512:(s + 1) * 512, :]).astype(BF)
    R.xs[2] = nn(R.mats[336:, :], R.merged[...]).astype(BF)
    halo2 = exchange(2, SEG1, R.xs.at[2], R.xr.at[2], ahead)
    R.xr[2, 0:336] = nn(R.mats[0:336, :], R.merged[...]).astype(BF)

    R.halft[0] = R.half2[core].T
    core0.wait()
    R.halft[1] = R.theirs2[...].T
    core1.wait()

    def term2(yy):
        c = tile(yy, 768)
        g = nn(R.halft[0], R.dqkv2[0, :, c]) + nn(R.halft[1], R.dqkv2[1, :, c])
        g = g.astype(BF)
        for zz in range(4):
            for hh in range(2):
                r = (zz * 2 + hh) * 64
                for xx in range(2):
                    at = dict(z=zz, x=hh * 2 + xx, y=yy)
                    for p, order in enumerate(ORDERS):
                        block = (at[order[0]] * 4 + at[order[1]]) * 4 + at[order[2]]
                        lanes = xx * 384 + p * 128
                        R.b2[p, block] = g[r:r + 64, lanes:lanes + 128]

    loop(4, term2)

    def rs_start(buf, recv, sem0, step):
        copies = []
        for p, order in enumerate(ORDERS):
            base = 0
            for s in range(step):
                base = base + place[order[s]] * (16 >> (2 * s))
            size = 16 >> (2 * step)
            axis = order[step]
            for k in (1, 2, 3):
                to = lax.rem(place[axis] + k, 4)
                n = sem0 + (step * 3 + p) * 3 + k - 1
                copies.append(pltpu.make_async_remote_copy(
                    src_ref=buf.at[p, pl.ds(base + to * size, size)],
                    dst_ref=recv.at[p, k - 1],
                    send_sem=R.rs_send.at[n],
                    recv_sem=R.rs_recv.at[n],
                    device_id=along(axis, k),
                    device_id_type=MESH))
        for c in copies:
            c.start()
        return copies

    def rs_add(buf, recv, step, copies):
        wait(copies)
        size = 16 >> (2 * step)
        for p, order in enumerate(ORDERS):
            base = 0
            for s in range(step + 1):
                base = base + place[order[s]] * (16 >> (2 * s))

            step_of = min(size, 65536 // (buf.shape[2] * buf.shape[3]))

            def add(n):
                at = pl.ds(base + n * step_of, step_of)
                near = pl.ds(n * step_of, step_of)
                t = buf[p, at].astype(F32) + recv[p, 0, near].astype(F32)
                t = t + recv[p, 1, near].astype(F32) + recv[p, 2, near].astype(F32)
                buf[p, at] = t.astype(BF)

            loop(size // step_of, add)

    def region(order, step):
        base = 0
        for k in range(step):
            base = base + place[order[k]] * (16 >> (2 * k))
        return base, 16 >> (2 * step)

    def ring(buf, via, recv, step):
        out = []
        for p, order in enumerate(ORDERS):
            base, size = region(order, step)
            half = size // 2
            axis = order[step]
            up, opposite, down = [base + lax.rem(place[axis] + k, 4) * size for k in (1, 2, 3)]
            ends = along(axis, 1), along(axis, 3)
            moves = (
                (opposite, via.at[p, 0], 0), (opposite + half, via.at[p, 1], 1),
                (up + half, recv.at[p, 0, pl.ds(half, half)], 0), (down, recv.at[p, 1, pl.ds(0, half)], 1),
                (up, recv.at[p, 0, pl.ds(0, half)], 0), (down + half, recv.at[p, 1, pl.ds(half, half)], 1))
            out.append([pltpu.make_async_remote_copy(
                src_ref=buf.at[p, pl.ds(start, half)], dst_ref=target,
                send_sem=R.ring_send.at[(step * 3 + p) * 6 + n], recv_sem=R.ring_recv.at[(step * 3 + p) * 6 + n],
                device_id=ends[way], device_id_type=MESH) for n, (start, target, way) in enumerate(moves)])
        return out

    def ring_start(*what):
        copies = ring(*what)
        for pair in (slice(0, 2), slice(2, 4)):
            for part in copies:
                for c in part[pair]:
                    c.start()

    def ring_relay(buf, via, recv, step):
        copies = ring(buf, via, recv, step)
        for p, order in enumerate(ORDERS):
            base, size = region(order, step)
            half = size // 2
            up, down = [base + lax.rem(place[order[step]] + k, 4) * size for k in (1, 3)]
            for way, start in ((0, up), (1, down + half)):
                copies[p][way].wait_recv()
                at = pl.ds(start, half)
                buf[p, at] = (buf[p, at].astype(F32) + via[p, way].astype(F32)).astype(BF)
                copies[p][4 + way].start()

    def ring_finish(buf, via, recv, step):
        copies = ring(buf, via, recv, step)
        for p, order in enumerate(ORDERS):
            for n, c in enumerate(copies[p]):
                c.wait_send()
                if n >= 2:
                    c.wait_recv()
            base, size = region(order, step + 1)[0], region(order, step)[1]
            at = pl.ds(base, size)
            t = buf[p, at].astype(F32) + recv[p, 0].astype(F32) + recv[p, 1].astype(F32)
            buf[p, at] = t.astype(BF)

    def rs_last(buf, recv, p, copies):
        order = ORDERS[p]
        base = (place[order[0]] * 4 + place[order[1]]) * 4 + place[order[2]]
        t = buf[p, base].astype(F32) + recv[p, 0, 0].astype(F32)
        return t + recv[p, 1, 0].astype(F32) + recv[p, 2, 0].astype(F32)

    first_ring = (R.b2, R.b2v0, R.b2r0, 0)
    second_ring = (R.b2, R.b2v1, R.b2r1, 1)
    ring_start(*first_ring)
    R.mats[...] = take("s4", 0, 608, 576)
    R.matr[...] = take("r3", 0, 576, 608)

    wait(halo2)
    R.g1[...] = nn(R.matr[...], R.xr[2]).astype(BF)

    def grad_mixed1(n):
        R.gm1[:, tile(n)] = nt(R.g1[...], R.p1[tile(n), :]).astype(BF)

    loop(2, grad_mixed1)

    def bwd1(pair):
        q2, k, v = four(pair)
        go = [stack(R.gm1[window(w), at(0, pair, 512)]) for w in range(4)]
        pb = [R.prob1[pair * 4 + w] for w in range(4)]
        back = attend_back(q2, k, v, [t.astype(F32) for t in pb], pb, go)
        for w in range(4):
            for part in range(3):
                R.dqkv1[window(w), at(part, pair, 512)] = back[part][w]
        pl.when(pair == 1)(lambda: ring_relay(*first_ring))

    loop(4, bwd1)

    def to_core(t):
        return pltpu.make_async_remote_copy(
            src_ref=R.b1h.at[t, 1 - core], dst_ref=R.b1c.at[t], send_sem=R.core_send.at[2 + t],
            recv_sem=R.core_recv.at[2 + t], device_id=other, device_id_type=MESH)

    def term1(t):
        c = pl.ds(pl.multiple_of(t * 384, 128), 384)
        g = nn(R.rolled1t[...], R.dqkv1[:, c])
        pick = is_left[0:16]
        for zz in range(4):
            for hh in range(2):
                for cc in range(2):
                    r = ((zz * 2 + hh) * 2 + cc) * 32
                    upper = g[r:r + 16, 128:256]
                    lower = pltpu.roll(g[r + 16:r + 32, 128:256], 64, 1)
                    mixes = (jnp.where(pick, upper, lower), jnp.where(pick, lower, upper))
                    for odd in range(2):
                        lanes = slice(odd * 256, odd * 256 + 128)
                        pieces = (g[r:r + 16, lanes], g[r + 16:r + 32, lanes], mixes[odd])
                        for p in range(3):
                            R.b1h[t, cc, p, zz * 4 + hh * 2 + odd] = pieces[p].astype(BF)
        to_core(t).start()

    loop(4, term1)
    ring_finish(*first_ring)
    ring_start(*second_ring)

    for t in range(4):
        to_core(t).wait()
        for p, order in enumerate(ORDERS):
            g = R.b1h[t, core, p].astype(F32) + R.b1c[t, p].astype(F32)
            for n in range(16):
                at = dict(z=n // 4, x=n % 4, y=t)
                block = (at[order[0]] * 4 + at[order[1]]) * 4 + at[order[2]]
                R.b1[p, block] = g[n].astype(BF)
    mine = R.b1
    small = rs_start(mine, R.b1r0, 27, 0)
    ring_relay(*second_ring)

    def grad_rolled1(n):
        R.gm1[:, tile(n)] = nt(R.dqkv1[...], R.w1[tile(n), :]).astype(BF)

    def tail1(w):
        r = window(w)
        R.out1[r, :] = norm_back(R.gm1[r, :], R.x1[r, :], gain1, R.g1[r, :])

    loop(2, grad_rolled1)
    loop(4, tail1)
    R.xs[3] = nn(R.mats[336:, :], R.out1[...]).astype(BF)
    halo3 = exchange(3, SEG1, R.xs.at[3], R.xr.at[3], ahead)
    R.xr[3, 0:336] = nn(R.mats[0:336, :], R.out1[...]).astype(BF)

    branch = nn(R.mixed2[...], R.p2[...]).astype(BF).astype(F32)
    R.res[...] = (R.second[...].astype(F32) + branch).astype(BF)
    R.cs[1] = nn(take("sr", 48, 144, CELLS), R.res[...]).astype(BF)
    halo_r = exchange(5, SEG2, R.cs.at[1], R.cr.at[1], ahead)
    R.cr[1, 0:48] = nn(take("sr", 0, 48, CELLS), R.res[...]).astype(BF)

    R.matr[...] = take("r4", 0, 576, 608)
    rs_add(mine, R.b1r0, 0, small)
    small = rs_start(mine, R.b1r1, 27, 1)
    ring_finish(*second_ring)
    big = rs_start(R.b2, R.b2r2, 0, 2)
    wait(halo_r)
    R.v_res[...] = nn(take("rr", 0, CELLS, 192), R.cr[1]).astype(BF).reshape(72, 2, 1024)
    puts = [put(0, "res")]
    rs_add(mine, R.b1r1, 1, small)
    small = rs_start(mine, R.b1r2, 27, 2)
    wait(halo3)
    R.v_tok[...] = jnp.where(present, nn(R.matr[...], R.xr[3]), 0.0).astype(BF)
    puts.append(put(1, "tok"))
    wait(big)
    for p in range(3):
        R.v_q2[:, p * 128:(p + 1) * 128] = rs_last(R.b2, R.b2r2, p, big)
    puts.append(put(3, "q2"))
    wait(small)
    a, b, m = [rs_last(mine, R.b1r2, p, small) for p in range(3)]
    turned = pltpu.roll(m, 64, 1)
    even = xl == 0
    a_turned = pltpu.roll(a, 64, 1)
    b_turned = pltpu.roll(b, 64, 1)
    pick = is_left[0:16]
    R.v_q1[0:16, 0:128] = jnp.where(even, a, jnp.where(pick, turned, a_turned))
    R.v_q1[16:32, 0:128] = jnp.where(even, b, jnp.where(pick, m, b_turned))
    R.v_q1[0:16, 128:192] = jnp.where(even, m, a_turned)[:, 0:64]
    R.v_q1[16:32, 128:192] = jnp.where(even, turned, b_turned)[:, 0:64]
    puts.append(put(2, "q1"))
    wait(puts)


def hand_on(*refs):
    given, out, held, sem = refs[0:4], refs[4:8], refs[8:12], refs[12]
    come = [pltpu.make_async_copy(given[n], held[n], sem.at[n]) for n in range(4)]
    leave = [pltpu.make_async_copy(held[n], out[n], sem.at[4 + n]) for n in range(4)]
    for c in come:
        c.start()
    for n in range(4):
        come[n].wait()
        leave[n].start()
    for c in leave:
        c.wait()


def shards(tokens, observed, mask_token, gain_one, qkv_one, table_one, proj_one, merge_weight, gain_two, qkv_two,
           table_two, proj_two, cotangent, sizes):
    first = tokens.transpose(0, 2, 1, 3).reshape(576, 512)
    cot = cotangent.transpose(1, 2, 0, 3).reshape(72, 2, 1024)
    seen = observed.transpose(2, 0, 1)
    given = dict(first=first, cot=cot, w1=qkv_one, p1=proj_one, wm=merge_weight, w2=qkv_two, p2=proj_two)
    args = [given[k] for k in LOADS]
    args += [jnp.asarray(TABLE_OF), seen, mask_token[None], table_one, table_two, gain_one[None], gain_two[None]]
    shapes = (
        jax.ShapeDtypeStruct((72, 2, 1024), BF),
        jax.ShapeDtypeStruct((576, 512), BF),
        jax.ShapeDtypeStruct((32, 192), F32),
        jax.ShapeDtypeStruct((64, 384), F32),
    )
    outs = pl.pallas_call(
        functools.partial(body, sizes),
        out_shape=shapes,
        in_specs=[pl.BlockSpec(memory_space=pl.ANY)] * len(LOADS) + [pl.BlockSpec(memory_space=pltpu.VMEM)] * len(SMALL),
        out_specs=[pl.BlockSpec(memory_space=pl.ANY)] * 4,
        scratch_shapes=list(SCRATCH.values()),
        compiler_params=pltpu.CompilerParams(
            collective_id=0, has_side_effects=True, vmem_limit_bytes=62 * 1024 * 1024),
        cost_estimate=pl.CostEstimate(flops=9 * 10 ** 9, bytes_accessed=24 * 10 ** 6, transcendentals=10 ** 6),
    )(*args)
    res, tok, q1, q2 = pl.pallas_call(
        hand_on,
        out_shape=shapes,
        in_specs=[pl.BlockSpec(memory_space=pl.ANY)] * 4,
        out_specs=[pl.BlockSpec(memory_space=pl.ANY)] * 4,
        scratch_shapes=[pltpu.VMEM(s.shape, s.dtype) for s in shapes] + [pltpu.SemaphoreType.DMA((8,))],
    )(*outs)
    result = res.reshape(12, 6, 2, 1024).transpose(2, 0, 1, 3)
    grad_tokens = tok.reshape(2, 12, 24, 512).transpose(0, 2, 1, 3)
    return (result, grad_tokens, q1, q2)


def solution(mesh):
    sizes = (mesh.shape["lon"], mesh.shape["lat"])
    split = P(None, "lon", "lat", None)

    def run(*args):
        return shards(*args, sizes)

    return jax.shard_map(
        run,
        mesh=mesh,
        in_specs=(split, P(None, "lon", "lat")) + (P(),) * 10 + (split,),
        out_specs=(split, split, P("lon", "lat"), P("lon", "lat")),
        check_vma=False,
    )
```

```python
import functools
from types import SimpleNamespace
import numpy as np
import jax
import jax.numpy as jnp
from jax import lax
from jax.experimental import pallas as pl
from jax.experimental.pallas import tpu as pltpu
from jax.sharding import PartitionSpec as P

BF = jnp.bfloat16
F32 = jnp.float32
EPS = 1e-05
NEG = -1000000000.0
MESH = pl.DeviceIdType.MESH
CELLS = 144
HALF = 72

SEG1 = ((0, 336), (336, 112), (448, 112), (560, 48))
HERE, AWAY, ALL = pl.ds(0, 336), pl.ds(336, 272), pl.ds(0, 576)
SEG2 = ((0, 48), (48, 48), (96, 48), (144, 48))


def _cells(along, across, half_lon, half_lat):
    out = [[], [], [], []]
    for v in range(2):
        for i in range(along):
            for j in range(across):
                seg = (1 if i < half_lon else 0) + (2 if j < half_lat else 0)
                moved = (v, (i - half_lon) % along, (j - half_lat) % across)
                out[seg].append(((v, i, j), moved))
    return out


def _send_index(segs, cells, row_of):
    out = [-1] * (segs[-1][0] + segs[-1][1])
    for (start, _), members in zip(segs, cells):
        for n, (cell, _) in enumerate(members):
            out[start + n] = row_of(*cell)
    return out


def _recv_index(segs, cells, row_of, rows):
    out = [-1] * rows
    for (start, _), members in zip(segs, cells):
        for n, (_, moved) in enumerate(members):
            out[row_of(*moved)] = start + n
    return out


def _inverse(index, rows):
    out = [-1] * rows
    for n, m in enumerate(index):
        if m >= 0:
            out[m] = n
    return out


def _nat1(v, i, j):
    return (v * 12 + j) * 24 + i


def _win1(v, i, j):
    return ((i // 12) * 2 + j // 6) * CELLS + (j % 6) * 24 + v * 12 + i % 12


def _merge(v, i, j):
    return ((i % 2) * 2 + j % 2) * CELLS + (j // 2) * 24 + v * 12 + i // 2


def _nat2(v, i, j):
    return (i * 6 + j) * 2 + v


def _win2(v, i, j):
    return j * 24 + v * 12 + i


def _indices():
    one = _cells(24, 12, 6, 3)
    two = _cells(12, 6, 6, 3)
    s1 = _send_index(SEG1, one, _nat1)
    r1 = _recv_index(SEG1, one, _win1, 576)
    s2 = _send_index(SEG1, one, _win1)
    r2 = _recv_index(SEG1, one, _merge, 576)
    sc = _send_index(SEG2, two, _nat2)
    rc = _recv_index(SEG2, two, _win2, CELLS)
    flip = [-1] * 768
    for x in range(3):
        for y in range(23):
            for z in range(11):
                flip[(x * 23 + y) * 11 + z] = z * 69 + x * 23 + y
    pick = [-1] * 768
    for z in range(11):
        for v in range(2):
            for l in range(12):
                pick[z * 69 + v * 23 + l] = z * 24 + v * 12 + l
    return dict(s1=s1, r1=r1, s2=s2, r2=r2, s3=_inverse(r2, 608), r3=_inverse(s2, 576), s4=_inverse(r1, 608),
                r4=_inverse(s1, 576), sc=sc, rc=rc, sr=_inverse(rc, 192), rr=_inverse(sc, CELLS), flip=flip, pick=pick)


INDEX = _indices()
TABLE_OF = np.full((768, len(INDEX)), -1, np.int32)
for _n, _rows in enumerate(INDEX.values()):
    TABLE_OF[:len(_rows), _n] = _rows

SHAPES = dict(first=(576, 512), cot=(72, 2, 1024), w1=(512, 1536), p1=(512, 512), p2=(1024, 1024),
              wm=(2048, 1024), w2=(1024, 3072))
LOADS = tuple(SHAPES)


def nn(a, b):
    return lax.dot_general(a, b, (((1,), (0,)), ((), ())), preferred_element_type=F32)


def nt(a, b):
    return lax.dot_general(a, b, (((1,), (1,)), ((), ())), preferred_element_type=F32)


def tn(a, b):
    return lax.dot_general(a, b, (((0,), (0,)), ((), ())), preferred_element_type=F32)


def norm_stats(x):
    centre = jnp.mean(x, axis=-1, keepdims=True)
    dev = x - centre
    spread = jnp.mean(dev * dev, axis=-1, keepdims=True)
    return dev, lax.rsqrt(spread + EPS)


def loop(n, body):
    lax.fori_loop(0, n, lambda i, c: (body(i), c)[1], 0)


SCRATCH = dict(
    {k: pltpu.VMEM(SHAPES[k], BF) for k in LOADS},
    mats=pltpu.VMEM((608, 576), BF),
    matr=pltpu.VMEM((576, 608), BF),
    tables=pltpu.VMEM((24, 768), F32),
    shifted=pltpu.VMEM((1152, 768), F32),
    ext=pltpu.VMEM((24, 24, 264), F32),
    bias=pltpu.VMEM((12, CELLS, 288), F32),
    seen=pltpu.VMEM((576, 1), F32),
    madd=pltpu.VMEM((CELLS, 288), F32),
    xr=pltpu.VMEM((4, 608, 512), BF),
    xs=pltpu.VMEM((4, 272, 512), BF),
    cr=pltpu.VMEM((2, 192, 1024), BF),
    cs=pltpu.VMEM((2, 144, 1024), BF),
    x1=pltpu.VMEM((576, 512), BF),
    rolled1=pltpu.VMEM((576, 512), BF),
    rolled1t=pltpu.VMEM((512, 576), BF),
    qkv1=pltpu.VMEM((576, 1536), BF),
    dqkv1=pltpu.VMEM((576, 1536), BF),
    prob1=pltpu.VMEM((16, CELLS, 288), BF),
    mixed1=pltpu.VMEM((576, 512), BF),
    out1=pltpu.VMEM((576, 512), BF),
    gm1=pltpu.VMEM((576, 512), BF),
    g1=pltpu.VMEM((576, 512), BF),
    merged=pltpu.VMEM((576, 512), BF),
    second=pltpu.VMEM((CELLS, 1024), BF),
    rolled2=pltpu.VMEM((CELLS, 1024), BF),
    qkv2=pltpu.VMEM((CELLS, 3072), BF),
    dqkv2=pltpu.VMEM((2, CELLS, 3072), BF),
    half2=pltpu.VMEM((2, CELLS, 512), BF),
    theirs2=pltpu.VMEM((CELLS, 512), BF),
    halft=pltpu.VMEM((2, 512, CELLS), BF),
    mixed2=pltpu.VMEM((CELLS, 1024), BF),
    ct=pltpu.VMEM((CELLS, 1024), BF),
    gm2=pltpu.VMEM((CELLS, 1024), BF),
    res=pltpu.VMEM((CELLS, 1024), BF),
    gs=pltpu.VMEM((CELLS, 1024), BF),
    v_res=pltpu.VMEM((72, 2, 1024), BF),
    v_tok=pltpu.VMEM((576, 512), BF),
    v_q1=pltpu.VMEM((32, 192), F32),
    v_q2=pltpu.VMEM((64, 384), F32),
    out_sem=pltpu.SemaphoreType.DMA((4,)),
    b2=pltpu.VMEM((3, 64, 64, 128), BF),
    b2v0=pltpu.VMEM((3, 2, 8, 64, 128), BF),
    b2r0=pltpu.VMEM((3, 2, 16, 64, 128), BF),
    b2v1=pltpu.VMEM((3, 2, 2, 64, 128), BF),
    b2r1=pltpu.VMEM((3, 2, 4, 64, 128), BF),
    b2r2=pltpu.VMEM((3, 3, 1, 64, 128), BF),
    b1=pltpu.VMEM((3, 64, 16, 128), BF),
    b1h=pltpu.VMEM((4, 2, 3, 16, 16, 128), BF),
    b1c=pltpu.VMEM((4, 3, 16, 16, 128), BF),
    b1r0=pltpu.VMEM((3, 3, 16, 16, 128), BF),
    b1r1=pltpu.VMEM((3, 3, 4, 16, 128), BF),
    b1r2=pltpu.VMEM((3, 3, 1, 16, 128), BF),
    load_sem=pltpu.SemaphoreType.DMA((4 * len(LOADS),)),
    halo_send=pltpu.SemaphoreType.DMA((18,)),
    halo_recv=pltpu.SemaphoreType.DMA((18,)),
    rs_send=pltpu.SemaphoreType.DMA((54,)),
    rs_recv=pltpu.SemaphoreType.DMA((54,)),
    ring_send=pltpu.SemaphoreType.DMA((36,)),
    ring_recv=pltpu.SemaphoreType.DMA((36,)),
    core_send=pltpu.SemaphoreType.DMA((6,)),
    core_recv=pltpu.SemaphoreType.DMA((6,)),
)
SMALL = ("index", "seen", "mask", "table1", "table2", "gain1", "gain2")
OUTPUTS = ("o_res", "o_tok", "o_q1", "o_q2")

ORDERS = (("z", "x", "y"), ("x", "y", "z"), ("y", "z", "x"))


def body(sizes, *refs):
    n_lon, n_lat = sizes
    names = ["in_" + n for n in LOADS + SMALL] + list(OUTPUTS) + list(SCRATCH)
    R = SimpleNamespace(**dict(zip(names, refs, strict=True)))

    e = lax.axis_index("lon")
    d = lax.axis_index("lat")
    core, xh, z = lax.rem(e, 2), lax.rem(e // 2, 2), e // 4
    xl, y = lax.rem(d, 2), d // 2
    x = xh * 2 + xl
    place = dict(x=x, y=y, z=z)
    e_up, e_dn = lax.rem(e + 1, n_lon), lax.rem(e + n_lon - 1, n_lon)
    d_up, d_dn = lax.rem(d + 1, n_lat), lax.rem(d + n_lat - 1, n_lat)
    last = d == n_lat - 1
    ahead = ((e_up, d), (e, d_up), (e_up, d_up))
    behind = ((e_dn, d), (e, d_dn), (e_dn, d_dn))
    other = (e + 1 - 2 * core, d)

    def device(x, y, z):
        return (z * 4 + (x // 2) * 2 + core, y * 2 + lax.rem(x, 2))

    def along(axis, k):
        at = dict(place)
        at[axis] = lax.rem(at[axis] + k, 4)
        return device(**at)

    def wait(copies):
        for c in copies:
            c.wait()

    loads = SimpleNamespace()
    for n, name in enumerate(LOADS):
        source, target = getattr(R, "in_" + name), getattr(R, name)
        cuts = 4 if source.shape[0] >= 1024 else 1
        size = source.shape[0] // cuts
        pieces = [pltpu.make_async_copy(source.at[pl.ds(c * size, size)], target.at[pl.ds(c * size, size)],
                                        R.load_sem.at[4 * n + c]) for c in range(cuts)]
        for copy in pieces:
            copy.start()
        setattr(loads, name, pieces)

    barrier = pltpu.get_barrier_semaphore()
    partners = list(ahead) + list(behind) + [other]
    for axis in place:
        for k in (1, 2, 3):
            partners.append(along(axis, k))
    for who in partners:
        pl.semaphore_signal(barrier, inc=1, device_id=who, device_id_type=MESH)

    def exchange(n, segs, source, target, to):
        copies = []
        for k in range(3):
            start, size = segs[k + 1]
            rows = pl.ds(start, size)
            copies.append(pltpu.make_async_remote_copy(
                src_ref=source.at[pl.ds(start - segs[0][1], size)],
                dst_ref=target.at[rows],
                send_sem=R.halo_send.at[3 * n + k],
                recv_sem=R.halo_recv.at[3 * n + k],
                device_id=to[k],
                device_id_type=MESH))
        for c in copies:
            c.start()
        return copies

    def take(key, start, size, columns):
        n = list(INDEX).index(key)
        col = R.in_index[pl.ds(start, size), n:n + 1]
        hit = col == lax.broadcasted_iota(jnp.int32, (size, columns), 1)
        return jnp.where(hit, 1.0, 0.0).astype(BF)

    def window(w):
        return pl.ds(pl.multiple_of(w * CELLS, 16), CELLS)

    def tile(n, size=256):
        return pl.ds(pl.multiple_of(n * size, size), size)

    def fill(ref, key, rows, columns):
        def some(n):
            at = tile(n, 32)
            ref[at, :] = take(key, pl.multiple_of(n * 32, 32), 32, columns)

        loop(rows // 32, some)

    def permute(out, rows, mat, source):
        def some(n):
            out[:, tile(n)] = nn(mat[rows, :], source[:, tile(n)]).astype(BF)

        loop(source.shape[1] // 256, some)

    def put(n, name):
        copy = pltpu.make_async_copy(getattr(R, "v_" + name), getattr(R, "o_" + name), R.out_sem.at[n])
        copy.start()
        return copy

    seen = R.in_seen[...]
    seen = jnp.concatenate([seen[:, 0, :], seen[:, 1, :]], axis=0).astype(F32).astype(BF)
    row = lax.broadcasted_iota(jnp.int32, (576, 24), 0)
    col = lax.broadcasted_iota(jnp.int32, (576, 24), 1)
    per = nn(jnp.where(row // 24 == col, 1.0, 0.0).astype(BF), seen)
    present = jnp.sum(jnp.where(lax.rem(row, 24) == col, per, 0.0), axis=-1, keepdims=True) > 0.5

    fill(R.mats, "s1", 608, 576)
    wait(loads.first)
    R.first[...] = jnp.where(present, R.first[...].astype(F32), R.in_mask[...].astype(BF).astype(F32)).astype(BF)
    permute(R.xs.at[0], AWAY, R.mats, R.first)

    R.tables[...] = jnp.zeros((24, 768), F32)
    R.tables[0:8, 0:759] = R.in_table1[...]
    R.tables[8:24, 0:759] = R.in_table2[...]
    table = R.tables[...]
    high = table.astype(BF).astype(F32)
    mid = (table - high).astype(BF).astype(F32)
    low = table - high - mid
    parts = jnp.concatenate([high, mid, low], axis=0).astype(BF)
    parts = nn(parts, take("flip", 0, 768, 768))
    picked = take("pick", 0, 768, 264)

    pl.semaphore_wait(barrier, len(partners))
    halo0 = exchange(0, SEG1, R.xs.at[0], R.xr.at[0], behind)
    permute(R.xr.at[0, pl.ds(0, 336)], HERE, R.mats, R.first)
    wait(loads.cot)
    cot = R.cot[...].reshape(CELLS, 1024)
    R.cs[0] = nn(take("sc", 48, 144, CELLS), cot).astype(BF)
    halo_c = exchange(4, SEG2, R.cs.at[0], R.cr.at[0], behind)
    R.cr[0, 0:48] = nn(take("sc", 0, 48, CELLS), cot).astype(BF)
    fill(R.matr, "r1", 576, 608)
    fill(R.mats, "s2", 608, 576)

    def extend(first, heads):
        part = jnp.concatenate([parts[24 * k + first:24 * k + first + heads] for k in range(3)], axis=0)
        for v in range(2):
            for l in range(12):
                shift = (1 - v) * 23 + 11 - l
                moved = pltpu.roll(part, (768 - shift) % 768, 1) if shift else part
                at = (v * 12 + l) * 3 * heads
                R.shifted[at:at + 3 * heads] = moved
        def some(v):
            got = nn(R.shifted[tile(v, 24 * heads)].astype(BF), picked)
            for n in range(8):
                at = n * 3 * heads
                R.ext[first:first + heads, v * 8 + n, :] = (
                    got[at:at + heads] + got[at + heads:at + 2 * heads] + got[at + 2 * heads:at + 3 * heads])

        loop(3, some)

    extend(0, 8)
    rows = lax.broadcasted_iota(jnp.int32, (CELLS, CELLS), 0)
    cols = lax.broadcasted_iota(jnp.int32, (CELLS, CELLS), 1)
    apart = jnp.where(jnp.logical_xor(rows < HALF, cols < HALF), NEG, 0.0).astype(F32)
    apart = apart * jnp.where(last, 1.0, 0.0).astype(F32)
    R.madd[...] = jnp.concatenate([apart, apart], axis=1)

    def expand(pair):
        one, two = R.ext[2 * pair], R.ext[2 * pair + 1]
        for a in range(6):
            at = slice((5 - a) * 24, (5 - a) * 24 + CELLS)
            R.bias[pair, a * 24:(a + 1) * 24, :] = jnp.concatenate([one[:, at], two[:, at]], axis=1)

    def expand_masked(pair):
        expand(4 + pair)
        R.bias[4 + pair] = R.bias[4 + pair] + R.madd[...]

    loop(4, expand)

    lane = lax.broadcasted_iota(jnp.int32, (1, 128), 1)
    left = jnp.where(lane < 64, 1.0, 0.0).astype(BF)
    right = jnp.where(lane < 64, 0.0, 1.0).astype(BF)
    is_left = lax.broadcasted_iota(jnp.int32, (CELLS, 128), 1) < 64

    def stack(t):
        return jnp.concatenate([t * left, t * right], axis=0)

    def at(part, pair, width):
        return pl.ds(pl.multiple_of(part * width + pair * 128, 128), 128)

    def heads_of(t):
        return jnp.where(is_left, t[:CELLS], t[CELLS:])

    def attend(q2, k, v, bias):
        score = [nt(b, a) + c for a, b, c in zip(q2, k, bias)]
        expo = [jnp.exp(t - jnp.max(t, axis=0, keepdims=True)) for t in score]
        p = [t * (1.0 / jnp.sum(t, axis=0, keepdims=True)) for t in expo]
        pb = [t.astype(BF) for t in p]
        o = [heads_of(tn(a, b)).astype(BF) for a, b in zip(pb, v)]
        return p, pb, o

    def attend_back(q2, k, v, p, pb, go):
        gw = [nt(a, b) for a, b in zip(v, go)]
        gs = [(a * (b - jnp.sum(a * b, axis=0, keepdims=True))).astype(BF) for a, b in zip(p, gw)]
        gv = [nn(a, b).astype(BF) for a, b in zip(pb, go)]
        gk = [nn(a, b).astype(BF) for a, b in zip(gs, q2)]
        gq = [(heads_of(tn(a, b)) * 0.125).astype(BF) for a, b in zip(gs, k)]
        return gq, gk, gv

    gain1 = R.in_gain1[...]
    wait(halo0)

    def norm1(w):
        dev, inv = norm_stats(R.x1[window(w), :].astype(F32))
        R.rolled1[window(w), :] = (dev * inv * gain1).astype(BF)

    permute(R.x1, ALL, R.matr, R.xr.at[0])
    loop(4, norm1)
    wait(loads.w1)

    def qkv1(n):
        c = pl.ds(pl.multiple_of(n * 256, 256), 256)
        R.qkv1[:, c] = nn(R.rolled1[...], R.w1[:, c]).astype(BF)

    loop(6, qkv1)

    def four(pair):
        q2 = [stack(R.qkv1[window(w), at(0, pair, 512)] * BF(0.125)) for w in range(4)]
        k = [R.qkv1[window(w), at(1, pair, 512)] for w in range(4)]
        v = [R.qkv1[window(w), at(2, pair, 512)] for w in range(4)]
        return q2, k, v

    def fwd1(pair):
        bias = R.bias[pair]
        masked = bias + R.madd[...]
        _, pb, o = attend(*four(pair), [bias, masked, bias, masked])
        for w in range(4):
            R.prob1[pair * 4 + w] = pb[w]
            R.mixed1[window(w), at(0, pair, 512)] = o[w]

    loop(4, fwd1)
    wait(loads.p1)

    def proj1(n):
        branch = nn(R.mixed1[...], R.p1[:, tile(n)]).astype(BF).astype(F32)
        R.out1[:, tile(n)] = (R.x1[:, tile(n)].astype(F32) + branch).astype(BF)

    loop(2, proj1)

    permute(R.xs.at[1], AWAY, R.mats, R.out1)
    halo1 = exchange(1, SEG1, R.xs.at[1], R.xr.at[1], behind)
    permute(R.xr.at[1, pl.ds(0, 336)], HERE, R.mats, R.out1)
    extend(8, 16)
    loop(8, expand_masked)
    fill(R.mats, "s3", 608, 576)
    fill(R.matr, "r2", 576, 608)
    wait(halo_c)
    R.ct[...] = nn(take("rc", 0, CELLS, 192), R.cr[0]).astype(BF)
    wait(loads.p2)

    def grad_mixed2(n):
        c = pl.ds(pl.multiple_of(n * 256, 256), 256)
        R.gm2[:, c] = nt(R.ct[...], R.p2[c, :]).astype(BF)

    loop(4, grad_mixed2)
    R.rolled1t[...] = R.rolled1[...].T
    wait(halo1)
    permute(R.merged, ALL, R.matr, R.xr.at[1])
    wait(loads.wm)
    def merge(n):
        acc = nn(R.merged[0:CELLS, :], R.wm[0:512, tile(n)])
        for s in range(1, 4):
            acc = acc + nn(R.merged[s * CELLS:(s + 1) * CELLS, :], R.wm[s * 512:(s + 1) * 512, tile(n)])
        R.second[:, tile(n)] = acc.astype(BF)

    loop(4, merge)
    second = R.second[...]
    gain2 = R.in_gain2[...]
    dev, inv = norm_stats(second.astype(F32))
    rolled2 = (dev * inv * gain2).astype(BF)
    R.rolled2[...] = rolled2
    wait(loads.w2)

    def qkv2(n):
        c = pl.ds(pl.multiple_of(n * 512, 512), 512)
        R.qkv2[:, c] = nn(R.rolled2[...], R.w2[:, c]).astype(BF)

    loop(6, qkv2)

    r2f = rolled2.astype(F32)
    for t in range(4):
        a = r2f[:, t * 256:t * 256 + 128]
        b = r2f[:, t * 256 + 128:t * 256 + 256]
        c = slice(t * 128, t * 128 + 128)
        R.half2[0, :, c] = jnp.where(is_left, a, pltpu.roll(b, 64, 1)).astype(BF)
        R.half2[1, :, c] = jnp.where(is_left, pltpu.roll(a, 64, 1), b).astype(BF)
    core0 = pltpu.make_async_remote_copy(
        src_ref=R.half2.at[1 - core], dst_ref=R.theirs2, send_sem=R.core_send.at[0],
        recv_sem=R.core_recv.at[0], device_id=other, device_id_type=MESH)
    core0.start()

    def both2(u):
        pairs = [u * 4 + n for n in range(4)]
        q2 = [stack(R.qkv2[:, at(0, c, 1024)] * BF(0.125)) for c in pairs]
        k = [R.qkv2[:, at(1, c, 1024)] for c in pairs]
        v = [R.qkv2[:, at(2, c, 1024)] for c in pairs]
        go = [stack(R.gm2[:, at(0, c, 1024)]) for c in pairs]
        p, pb, o = attend(q2, k, v, [R.bias[4 + c] for c in pairs])
        back = attend_back(q2, k, v, p, pb, go)
        for n, c in enumerate(pairs):
            R.mixed2[:, at(0, c, 1024)] = o[n]
            for part in range(3):
                R.dqkv2[0, :, at(part, c, 1024)] = back[part][n]

    loop(2, both2)
    core1 = pltpu.make_async_remote_copy(
        src_ref=R.dqkv2.at[0], dst_ref=R.dqkv2.at[1], send_sem=R.core_send.at[1],
        recv_sem=R.core_recv.at[1], device_id=other, device_id_type=MESH)
    core1.start()

    def grad_rolled2(n):
        R.gm2[:, tile(n)] = nt(R.dqkv2[0], R.w2[tile(n), :]).astype(BF)

    loop(4, grad_rolled2)

    def norm_back(grad, xin, gain, grad_out):
        grad = grad.astype(BF).astype(F32) * gain
        dev, inv = norm_stats(xin.astype(F32))
        hat = dev * inv
        inner = inv * (grad - jnp.mean(grad, axis=-1, keepdims=True)
                       - hat * jnp.mean(grad * hat, axis=-1, keepdims=True))
        return (grad_out.astype(F32) + inner.astype(BF).astype(F32)).astype(BF)

    R.gs[...] = norm_back(R.gm2[...], R.second[...], gain2, R.ct[...])

    def unmerge(s):
        R.merged[window(s), :] = nt(R.gs[...], R.wm[tile(s, 512), :]).astype(BF)

    loop(4, unmerge)
    permute(R.xs.at[2], AWAY, R.mats, R.merged)
    halo2 = exchange(2, SEG1, R.xs.at[2], R.xr.at[2], ahead)
    permute(R.xr.at[2, pl.ds(0, 336)], HERE, R.mats, R.merged)

    R.halft[0] = R.half2[core].T
    core0.wait()
    R.halft[1] = R.theirs2[...].T
    core1.wait()

    def term2(yy):
        c = tile(yy, 768)
        g = nn(R.halft[0], R.dqkv2[0, :, c]) + nn(R.halft[1], R.dqkv2[1, :, c])
        g = g.astype(BF)
        for zz in range(4):
            for hh in range(2):
                r = (zz * 2 + hh) * 64
                for xx in range(2):
                    at = dict(z=zz, x=hh * 2 + xx, y=yy)
                    for p, order in enumerate(ORDERS):
                        block = (at[order[0]] * 4 + at[order[1]]) * 4 + at[order[2]]
                        lanes = xx * 384 + p * 128
                        R.b2[p, block] = g[r:r + 64, lanes:lanes + 128]

    loop(4, term2)

    def rs_start(buf, recv, sem0, step):
        copies = []
        for p, order in enumerate(ORDERS):
            base = 0
            for s in range(step):
                base = base + place[order[s]] * (16 >> (2 * s))
            size = 16 >> (2 * step)
            axis = order[step]
            for k in (1, 2, 3):
                to = lax.rem(place[axis] + k, 4)
                n = sem0 + (step * 3 + p) * 3 + k - 1
                copies.append(pltpu.make_async_remote_copy(
                    src_ref=buf.at[p, pl.ds(base + to * size, size)],
                    dst_ref=recv.at[p, k - 1],
                    send_sem=R.rs_send.at[n],
                    recv_sem=R.rs_recv.at[n],
                    device_id=along(axis, k),
                    device_id_type=MESH))
        for c in copies:
            c.start()
        return copies

    def rs_add(buf, recv, step, copies):
        wait(copies)
        size = 16 >> (2 * step)
        for p, order in enumerate(ORDERS):
            base = 0
            for s in range(step + 1):
                base = base + place[order[s]] * (16 >> (2 * s))

            step_of = min(size, 65536 // (buf.shape[2] * buf.shape[3]))

            def add(n):
                at = pl.ds(base + n * step_of, step_of)
                near = pl.ds(n * step_of, step_of)
                t = buf[p, at].astype(F32) + recv[p, 0, near].astype(F32)
                t = t + recv[p, 1, near].astype(F32) + recv[p, 2, near].astype(F32)
                buf[p, at] = t.astype(BF)

            loop(size // step_of, add)

    def region(order, step):
        base = 0
        for k in range(step):
            base = base + place[order[k]] * (16 >> (2 * k))
        return base, 16 >> (2 * step)

    def ring(buf, via, recv, step):
        out = []
        for p, order in enumerate(ORDERS):
            base, size = region(order, step)
            half = size // 2
            axis = order[step]
            up, opposite, down = [base + lax.rem(place[axis] + k, 4) * size for k in (1, 2, 3)]
            ends = along(axis, 1), along(axis, 3)
            moves = (
                (opposite, via.at[p, 0], 0), (opposite + half, via.at[p, 1], 1),
                (up + half, recv.at[p, 0, pl.ds(half, half)], 0), (down, recv.at[p, 1, pl.ds(0, half)], 1),
                (up, recv.at[p, 0, pl.ds(0, half)], 0), (down + half, recv.at[p, 1, pl.ds(half, half)], 1))
            out.append([pltpu.make_async_remote_copy(
                src_ref=buf.at[p, pl.ds(start, half)], dst_ref=target,
                send_sem=R.ring_send.at[(step * 3 + p) * 6 + n], recv_sem=R.ring_recv.at[(step * 3 + p) * 6 + n],
                device_id=ends[way], device_id_type=MESH) for n, (start, target, way) in enumerate(moves)])
        return out

    def ring_start(*what):
        copies = ring(*what)
        for pair in (slice(0, 2), slice(2, 4)):
            for part in copies:
                for c in part[pair]:
                    c.start()

    def ring_relay(buf, via, recv, step):
        copies = ring(buf, via, recv, step)
        for p, order in enumerate(ORDERS):
            base, size = region(order, step)
            half = size // 2
            up, down = [base + lax.rem(place[order[step]] + k, 4) * size for k in (1, 3)]
            for way, start in ((0, up), (1, down + half)):
                copies[p][way].wait_recv()

                def add(n):
                    at = pl.ds(start + n * 2, 2)
                    buf[p, at] = (buf[p, at].astype(F32) + via[p, way, pl.ds(n * 2, 2)].astype(F32)).astype(BF)

                loop(half // 2, add)
                copies[p][4 + way].start()

    def ring_finish(buf, via, recv, step):
        copies = ring(buf, via, recv, step)
        for p, order in enumerate(ORDERS):
            for n, c in enumerate(copies[p]):
                c.wait_send()
                if n >= 2:
                    c.wait_recv()
            base, size = region(order, step + 1)[0], region(order, step)[1]

            def add(n):
                at, near = pl.ds(base + n * 2, 2), pl.ds(n * 2, 2)
                t = buf[p, at].astype(F32) + recv[p, 0, near].astype(F32) + recv[p, 1, near].astype(F32)
                buf[p, at] = t.astype(BF)

            loop(size // 2, add)

    def rs_last(buf, recv, p, copies):
        order = ORDERS[p]
        base = (place[order[0]] * 4 + place[order[1]]) * 4 + place[order[2]]
        t = buf[p, base].astype(F32) + recv[p, 0, 0].astype(F32)
        return t + recv[p, 1, 0].astype(F32) + recv[p, 2, 0].astype(F32)

    first_ring = (R.b2, R.b2v0, R.b2r0, 0)
    second_ring = (R.b2, R.b2v1, R.b2r1, 1)
    ring_start(*first_ring)
    fill(R.mats, "s4", 608, 576)
    fill(R.matr, "r3", 576, 608)

    wait(halo2)
    permute(R.g1, ALL, R.matr, R.xr.at[2])

    def grad_mixed1(n):
        R.gm1[:, tile(n)] = nt(R.g1[...], R.p1[tile(n), :]).astype(BF)

    loop(2, grad_mixed1)

    def bwd1(pair):
        q2, k, v = four(pair)
        go = [stack(R.gm1[window(w), at(0, pair, 512)]) for w in range(4)]
        pb = [R.prob1[pair * 4 + w] for w in range(4)]
        back = attend_back(q2, k, v, [t.astype(F32) for t in pb], pb, go)
        for w in range(4):
            for part in range(3):
                R.dqkv1[window(w), at(part, pair, 512)] = back[part][w]
        pl.when(pair == 1)(lambda: ring_relay(*first_ring))

    loop(4, bwd1)

    def to_core(t):
        return pltpu.make_async_remote_copy(
            src_ref=R.b1h.at[t, 1 - core], dst_ref=R.b1c.at[t], send_sem=R.core_send.at[2 + t],
            recv_sem=R.core_recv.at[2 + t], device_id=other, device_id_type=MESH)

    def term1(t):
        c = pl.ds(pl.multiple_of(t * 384, 128), 384)
        g = nn(R.rolled1t[...], R.dqkv1[:, c])
        pick = is_left[0:16]
        for zz in range(4):
            for hh in range(2):
                for cc in range(2):
                    r = ((zz * 2 + hh) * 2 + cc) * 32
                    upper = g[r:r + 16, 128:256]
                    lower = pltpu.roll(g[r + 16:r + 32, 128:256], 64, 1)
                    mixes = (jnp.where(pick, upper, lower), jnp.where(pick, lower, upper))
                    for odd in range(2):
                        lanes = slice(odd * 256, odd * 256 + 128)
                        pieces = (g[r:r + 16, lanes], g[r + 16:r + 32, lanes], mixes[odd])
                        for p in range(3):
                            R.b1h[t, cc, p, zz * 4 + hh * 2 + odd] = pieces[p].astype(BF)
        to_core(t).start()

    loop(4, term1)
    ring_finish(*first_ring)
    ring_start(*second_ring)

    def add_core(t):
        to_core(t).wait()
        for p, order in enumerate(ORDERS):
            g = R.b1h[t, core, p].astype(F32) + R.b1c[t, p].astype(F32)
            for n in range(16):
                at = dict(z=n // 4, x=n % 4, y=t)
                block = (at[order[0]] * 4 + at[order[1]]) * 4 + at[order[2]]
                R.b1[p, block] = g[n].astype(BF)

    loop(4, add_core)
    mine = R.b1
    small = rs_start(mine, R.b1r0, 27, 0)
    ring_relay(*second_ring)

    def grad_rolled1(n):
        R.gm1[:, tile(n)] = nt(R.dqkv1[...], R.w1[tile(n), :]).astype(BF)

    def tail1(w):
        r = window(w)
        R.out1[r, :] = norm_back(R.gm1[r, :], R.x1[r, :], gain1, R.g1[r, :])

    loop(2, grad_rolled1)
    loop(4, tail1)
    permute(R.xs.at[3], AWAY, R.mats, R.out1)
    halo3 = exchange(3, SEG1, R.xs.at[3], R.xr.at[3], ahead)
    permute(R.xr.at[3, pl.ds(0, 336)], HERE, R.mats, R.out1)

    def proj2(n):
        branch = nn(R.mixed2[...], R.p2[:, tile(n)]).astype(BF).astype(F32)
        R.res[:, tile(n)] = (R.second[:, tile(n)].astype(F32) + branch).astype(BF)

    loop(4, proj2)
    R.cs[1] = nn(take("sr", 48, 144, CELLS), R.res[...]).astype(BF)
    halo_r = exchange(5, SEG2, R.cs.at[1], R.cr.at[1], ahead)
    R.cr[1, 0:48] = nn(take("sr", 0, 48, CELLS), R.res[...]).astype(BF)

    fill(R.matr, "r4", 576, 608)
    rs_add(mine, R.b1r0, 0, small)
    small = rs_start(mine, R.b1r1, 27, 1)
    ring_finish(*second_ring)
    big = rs_start(R.b2, R.b2r2, 0, 2)
    wait(halo_r)
    R.v_res[...] = nn(take("rr", 0, CELLS, 192), R.cr[1]).astype(BF).reshape(72, 2, 1024)
    puts = [put(0, "res")]
    rs_add(mine, R.b1r1, 1, small)
    small = rs_start(mine, R.b1r2, 27, 2)
    wait(halo3)
    R.seen[...] = jnp.where(present, 1.0, 0.0).astype(F32)

    def final(n):
        R.v_tok[:, tile(n)] = (nn(R.matr[...], R.xr[3, :, tile(n)]) * R.seen[...]).astype(BF)

    loop(2, final)
    puts.append(put(1, "tok"))
    wait(big)
    for p in range(3):
        R.v_q2[:, p * 128:(p + 1) * 128] = rs_last(R.b2, R.b2r2, p, big)
    puts.append(put(3, "q2"))
    wait(small)
    a, b, m = [rs_last(mine, R.b1r2, p, small) for p in range(3)]
    turned = pltpu.roll(m, 64, 1)
    even = xl == 0
    a_turned = pltpu.roll(a, 64, 1)
    b_turned = pltpu.roll(b, 64, 1)
    pick = is_left[0:16]
    R.v_q1[0:16, 0:128] = jnp.where(even, a, jnp.where(pick, turned, a_turned))
    R.v_q1[16:32, 0:128] = jnp.where(even, b, jnp.where(pick, m, b_turned))
    R.v_q1[0:16, 128:192] = jnp.where(even, m, a_turned)[:, 0:64]
    R.v_q1[16:32, 128:192] = jnp.where(even, turned, b_turned)[:, 0:64]
    puts.append(put(2, "q1"))
    wait(puts)


def hand_on(*refs):
    given, out, held, sem = refs[0:4], refs[4:8], refs[8:12], refs[12]
    come = [pltpu.make_async_copy(given[n], held[n], sem.at[n]) for n in range(4)]
    leave = [pltpu.make_async_copy(held[n], out[n], sem.at[4 + n]) for n in range(4)]
    for c in come:
        c.start()
    for n in range(4):
        come[n].wait()
        leave[n].start()
    for c in leave:
        c.wait()


def shards(tokens, observed, mask_token, gain_one, qkv_one, table_one, proj_one, merge_weight, gain_two, qkv_two,
           table_two, proj_two, cotangent, sizes):
    first = tokens.transpose(0, 2, 1, 3).reshape(576, 512)
    cot = cotangent.transpose(1, 2, 0, 3).reshape(72, 2, 1024)
    seen = observed.transpose(2, 0, 1)
    given = dict(first=first, cot=cot, w1=qkv_one, p1=proj_one, wm=merge_weight, w2=qkv_two, p2=proj_two)
    args = [given[k] for k in LOADS]
    args += [jnp.asarray(TABLE_OF), seen, mask_token[None], table_one, table_two, gain_one[None], gain_two[None]]
    shapes = (
        jax.ShapeDtypeStruct((72, 2, 1024), BF),
        jax.ShapeDtypeStruct((576, 512), BF),
        jax.ShapeDtypeStruct((32, 192), F32),
        jax.ShapeDtypeStruct((64, 384), F32),
    )
    outs = pl.pallas_call(
        functools.partial(body, sizes),
        out_shape=shapes,
        in_specs=[pl.BlockSpec(memory_space=pl.ANY)] * len(LOADS) + [pl.BlockSpec(memory_space=pltpu.VMEM)] * len(SMALL),
        out_specs=[pl.BlockSpec(memory_space=pl.ANY)] * 4,
        scratch_shapes=list(SCRATCH.values()),
        compiler_params=pltpu.CompilerParams(
            collective_id=0, has_side_effects=True, vmem_limit_bytes=62 * 1024 * 1024),
        cost_estimate=pl.CostEstimate(flops=9 * 10 ** 9, bytes_accessed=24 * 10 ** 6, transcendentals=10 ** 6),
    )(*args)
    res, tok, q1, q2 = pl.pallas_call(
        hand_on,
        out_shape=shapes,
        in_specs=[pl.BlockSpec(memory_space=pl.ANY)] * 4,
        out_specs=[pl.BlockSpec(memory_space=pl.ANY)] * 4,
        scratch_shapes=[pltpu.VMEM(s.shape, s.dtype) for s in shapes] + [pltpu.SemaphoreType.DMA((8,))],
    )(*outs)
    result = res.reshape(12, 6, 2, 1024).transpose(2, 0, 1, 3)
    grad_tokens = tok.reshape(2, 12, 24, 512).transpose(0, 2, 1, 3)
    return (result, grad_tokens, q1, q2)


def solution(mesh):
    sizes = (mesh.shape["lon"], mesh.shape["lat"])
    split = P(None, "lon", "lat", None)

    def run(*args):
        return shards(*args, sizes)

    return jax.shard_map(
        run,
        mesh=mesh,
        in_specs=(split, P(None, "lon", "lat")) + (P(),) * 10 + (split,),
        out_specs=(split, split, P("lon", "lat"), P("lon", "lat")),
        check_vma=False,
    )
```

```python
import functools
from types import SimpleNamespace
import numpy as np
import jax
import jax.numpy as jnp
from jax import lax
from jax.experimental import pallas as pl
from jax.experimental.pallas import tpu as pltpu
from jax.sharding import PartitionSpec as P

BF = jnp.bfloat16
F32 = jnp.float32
EPS = 1e-05
NEG = -1000000000.0
MESH = pl.DeviceIdType.MESH
CELLS = 144
HALF = 72

SEG1 = ((0, 336), (336, 112), (448, 112), (560, 48))
SEG2 = ((0, 48), (48, 48), (96, 48), (144, 48))


def _cells(along, across, half_lon, half_lat):
    out = [[], [], [], []]
    for v in range(2):
        for i in range(along):
            for j in range(across):
                seg = (1 if i < half_lon else 0) + (2 if j < half_lat else 0)
                moved = (v, (i - half_lon) % along, (j - half_lat) % across)
                out[seg].append(((v, i, j), moved))
    return out


def _send_index(segs, cells, row_of):
    out = [-1] * (segs[-1][0] + segs[-1][1])
    for (start, _), members in zip(segs, cells):
        for n, (cell, _) in enumerate(members):
            out[start + n] = row_of(*cell)
    return out


def _recv_index(segs, cells, row_of, rows):
    out = [-1] * rows
    for (start, _), members in zip(segs, cells):
        for n, (_, moved) in enumerate(members):
            out[row_of(*moved)] = start + n
    return out


def _inverse(index, rows):
    out = [-1] * rows
    for n, m in enumerate(index):
        if m >= 0:
            out[m] = n
    return out


def _nat1(v, i, j):
    return (v * 12 + j) * 24 + i


def _win1(v, i, j):
    return ((i // 12) * 2 + j // 6) * CELLS + (j % 6) * 24 + v * 12 + i % 12


def _merge(v, i, j):
    return ((i % 2) * 2 + j % 2) * CELLS + (j // 2) * 24 + v * 12 + i // 2


def _nat2(v, i, j):
    return (i * 6 + j) * 2 + v


def _win2(v, i, j):
    return j * 24 + v * 12 + i


def _indices():
    one = _cells(24, 12, 6, 3)
    two = _cells(12, 6, 6, 3)
    s1 = _send_index(SEG1, one, _nat1)
    r1 = _recv_index(SEG1, one, _win1, 576)
    s2 = _send_index(SEG1, one, _win1)
    r2 = _recv_index(SEG1, one, _merge, 576)
    sc = _send_index(SEG2, two, _nat2)
    rc = _recv_index(SEG2, two, _win2, CELLS)
    flip = [-1] * 768
    for x in range(3):
        for y in range(23):
            for z in range(11):
                flip[(x * 23 + y) * 11 + z] = z * 69 + x * 23 + y
    pick = [-1] * 768
    for z in range(11):
        for v in range(2):
            for l in range(12):
                pick[z * 69 + v * 23 + l] = z * 24 + v * 12 + l
    return dict(s1=s1, r1=r1, s2=s2, r2=r2, s3=_inverse(r2, 608), r3=_inverse(s2, 576), s4=_inverse(r1, 608),
                r4=_inverse(s1, 576), sc=sc, rc=rc, sr=_inverse(rc, 192), rr=_inverse(sc, CELLS), flip=flip, pick=pick)


INDEX = _indices()
TABLE_OF = np.full((768, len(INDEX)), -1, np.int32)
for _n, _rows in enumerate(INDEX.values()):
    TABLE_OF[:len(_rows), _n] = _rows

SHAPES = dict(first=(576, 512), cot=(72, 2, 1024), w1=(512, 1536), p1=(512, 512), p2=(1024, 1024),
              wm=(2048, 1024), w2=(1024, 3072))
LOADS = tuple(SHAPES)


def nn(a, b):
    return lax.dot_general(a, b, (((1,), (0,)), ((), ())), preferred_element_type=F32)


def nt(a, b):
    return lax.dot_general(a, b, (((1,), (1,)), ((), ())), preferred_element_type=F32)


def tn(a, b):
    return lax.dot_general(a, b, (((0,), (0,)), ((), ())), preferred_element_type=F32)


def norm_stats(x):
    centre = jnp.mean(x, axis=-1, keepdims=True)
    dev = x - centre
    spread = jnp.mean(dev * dev, axis=-1, keepdims=True)
    return dev, lax.rsqrt(spread + EPS)


def aligned(start, multiple):
    return start if isinstance(start, int) else pl.multiple_of(start, multiple)


def loop(n, body):
    for i in range(n):
        body(i)


SCRATCH = dict(
    {k: pltpu.VMEM(SHAPES[k], BF) for k in LOADS},
    mats=pltpu.VMEM((608, 576), BF),
    matr=pltpu.VMEM((576, 608), BF),
    tables=pltpu.VMEM((24, 768), F32),
    shifted=pltpu.VMEM((1152, 768), F32),
    ext=pltpu.VMEM((24, 24, 264), F32),
    bias=pltpu.VMEM((12, CELLS, 288), F32),
    madd=pltpu.VMEM((CELLS, 288), F32),
    xr=pltpu.VMEM((4, 608, 512), BF),
    xs=pltpu.VMEM((4, 272, 512), BF),
    cr=pltpu.VMEM((2, 192, 1024), BF),
    cs=pltpu.VMEM((2, 144, 1024), BF),
    x1=pltpu.VMEM((576, 512), BF),
    rolled1=pltpu.VMEM((576, 512), BF),
    rolled1t=pltpu.VMEM((512, 576), BF),
    qkv1=pltpu.VMEM((576, 1536), BF),
    dqkv1=pltpu.VMEM((576, 1536), BF),
    prob1=pltpu.VMEM((16, CELLS, 288), BF),
    mixed1=pltpu.VMEM((576, 512), BF),
    out1=pltpu.VMEM((576, 512), BF),
    gm1=pltpu.VMEM((576, 512), BF),
    g1=pltpu.VMEM((576, 512), BF),
    merged=pltpu.VMEM((576, 512), BF),
    second=pltpu.VMEM((CELLS, 1024), BF),
    rolled2=pltpu.VMEM((CELLS, 1024), BF),
    qkv2=pltpu.VMEM((CELLS, 3072), BF),
    dqkv2=pltpu.VMEM((2, CELLS, 3072), BF),
    half2=pltpu.VMEM((2, CELLS, 512), BF),
    theirs2=pltpu.VMEM((CELLS, 512), BF),
    halft=pltpu.VMEM((2, 512, CELLS), BF),
    mixed2=pltpu.VMEM((CELLS, 1024), BF),
    ct=pltpu.VMEM((CELLS, 1024), BF),
    gm2=pltpu.VMEM((CELLS, 1024), BF),
    res=pltpu.VMEM((CELLS, 1024), BF),
    gs=pltpu.VMEM((CELLS, 1024), BF),
    v_res=pltpu.VMEM((72, 2, 1024), BF),
    v_tok=pltpu.VMEM((576, 512), BF),
    v_q1=pltpu.VMEM((32, 192), F32),
    v_q2=pltpu.VMEM((64, 384), F32),
    out_sem=pltpu.SemaphoreType.DMA((4,)),
    b2=pltpu.VMEM((3, 64, 64, 128), BF),
    b2v0=pltpu.VMEM((3, 2, 8, 64, 128), BF),
    b2r0=pltpu.VMEM((3, 2, 16, 64, 128), BF),
    b2v1=pltpu.VMEM((3, 2, 2, 64, 128), BF),
    b2r1=pltpu.VMEM((3, 2, 4, 64, 128), BF),
    b2r2=pltpu.VMEM((3, 3, 1, 64, 128), BF),
    b1=pltpu.VMEM((3, 64, 16, 128), BF),
    b1h=pltpu.VMEM((4, 2, 3, 16, 16, 128), BF),
    b1c=pltpu.VMEM((4, 3, 16, 16, 128), BF),
    b1r0=pltpu.VMEM((3, 3, 16, 16, 128), BF),
    b1r1=pltpu.VMEM((3, 3, 4, 16, 128), BF),
    b1r2=pltpu.VMEM((3, 3, 1, 16, 128), BF),
    load_sem=pltpu.SemaphoreType.DMA((len(LOADS),)),
    halo_send=pltpu.SemaphoreType.DMA((18,)),
    halo_recv=pltpu.SemaphoreType.DMA((18,)),
    rs_send=pltpu.SemaphoreType.DMA((54,)),
    rs_recv=pltpu.SemaphoreType.DMA((54,)),
    ring_send=pltpu.SemaphoreType.DMA((36,)),
    ring_recv=pltpu.SemaphoreType.DMA((36,)),
    core_send=pltpu.SemaphoreType.DMA((6,)),
    core_recv=pltpu.SemaphoreType.DMA((6,)),
)
SMALL = ("index", "seen", "mask", "table1", "table2", "gain1", "gain2")
OUTPUTS = ("o_res", "o_tok", "o_q1", "o_q2")

ORDERS = (("z", "x", "y"), ("x", "y", "z"), ("y", "z", "x"))


def body(sizes, *refs):
    n_lon, n_lat = sizes
    names = ["in_" + n for n in LOADS + SMALL] + list(OUTPUTS) + list(SCRATCH)
    R = SimpleNamespace(**dict(zip(names, refs, strict=True)))

    e = lax.axis_index("lon")
    d = lax.axis_index("lat")
    core, xh, z = lax.rem(e, 2), lax.rem(e // 2, 2), e // 4
    xl, y = lax.rem(d, 2), d // 2
    x = xh * 2 + xl
    place = dict(x=x, y=y, z=z)
    e_up, e_dn = lax.rem(e + 1, n_lon), lax.rem(e + n_lon - 1, n_lon)
    d_up, d_dn = lax.rem(d + 1, n_lat), lax.rem(d + n_lat - 1, n_lat)
    last = d == n_lat - 1
    ahead = ((e_up, d), (e, d_up), (e_up, d_up))
    behind = ((e_dn, d), (e, d_dn), (e_dn, d_dn))
    other = (e + 1 - 2 * core, d)

    def device(x, y, z):
        return (z * 4 + (x // 2) * 2 + core, y * 2 + lax.rem(x, 2))

    def along(axis, k):
        at = dict(place)
        at[axis] = lax.rem(at[axis] + k, 4)
        return device(**at)

    loads = SimpleNamespace()
    for n, name in enumerate(LOADS):
        copy = pltpu.make_async_copy(getattr(R, "in_" + name), getattr(R, name), R.load_sem.at[n])
        copy.start()
        setattr(loads, name, copy)

    barrier = pltpu.get_barrier_semaphore()
    partners = list(ahead) + list(behind) + [other]
    for axis in place:
        for k in (1, 2, 3):
            partners.append(along(axis, k))
    for who in partners:
        pl.semaphore_signal(barrier, inc=1, device_id=who, device_id_type=MESH)

    def exchange(n, segs, source, target, to):
        copies = []
        for k in range(3):
            start, size = segs[k + 1]
            rows = pl.ds(start, size)
            copies.append(pltpu.make_async_remote_copy(
                src_ref=source.at[pl.ds(start - segs[0][1], size)],
                dst_ref=target.at[rows],
                send_sem=R.halo_send.at[3 * n + k],
                recv_sem=R.halo_recv.at[3 * n + k],
                device_id=to[k],
                device_id_type=MESH))
        for c in copies:
            c.start()
        return copies

    def wait(copies):
        for c in copies:
            c.wait()

    def take(key, start, size, columns):
        n = list(INDEX).index(key)
        col = R.in_index[pl.ds(start, size), n:n + 1]
        hit = col == lax.broadcasted_iota(jnp.int32, (size, columns), 1)
        return jnp.where(hit, 1.0, 0.0).astype(BF)

    def put(n, name):
        copy = pltpu.make_async_copy(getattr(R, "v_" + name), getattr(R, "o_" + name), R.out_sem.at[n])
        copy.start()
        return copy

    seen = R.in_seen[...]
    seen = jnp.concatenate([seen[:, 0, :], seen[:, 1, :]], axis=0).astype(F32).astype(BF)
    row = lax.broadcasted_iota(jnp.int32, (576, 24), 0)
    col = lax.broadcasted_iota(jnp.int32, (576, 24), 1)
    per = nn(jnp.where(row // 24 == col, 1.0, 0.0).astype(BF), seen)
    present = jnp.sum(jnp.where(lax.rem(row, 24) == col, per, 0.0), axis=-1, keepdims=True) > 0.5

    R.mats[...] = take("s1", 0, 608, 576)
    loads.first.wait()
    R.first[...] = jnp.where(present, R.first[...].astype(F32), R.in_mask[...].astype(BF).astype(F32)).astype(BF)
    R.xs[0] = nn(R.mats[336:, :], R.first[...]).astype(BF)

    R.tables[...] = jnp.zeros((24, 768), F32)
    R.tables[0:8, 0:759] = R.in_table1[...]
    R.tables[8:24, 0:759] = R.in_table2[...]
    table = R.tables[...]
    high = table.astype(BF).astype(F32)
    mid = (table - high).astype(BF).astype(F32)
    low = table - high - mid
    parts = jnp.concatenate([high, mid, low], axis=0).astype(BF)
    parts = nn(parts, take("flip", 0, 768, 768))
    picked = take("pick", 0, 768, 264)

    pl.semaphore_wait(barrier, len(partners))
    halo0 = exchange(0, SEG1, R.xs.at[0], R.xr.at[0], behind)
    R.xr[0, 0:336] = nn(R.mats[0:336, :], R.first[...]).astype(BF)
    loads.cot.wait()
    cot = R.cot[...].reshape(CELLS, 1024)
    R.cs[0] = nn(take("sc", 48, 144, CELLS), cot).astype(BF)
    halo_c = exchange(4, SEG2, R.cs.at[0], R.cr.at[0], behind)
    R.cr[0, 0:48] = nn(take("sc", 0, 48, CELLS), cot).astype(BF)
    R.matr[...] = take("r1", 0, 576, 608)
    R.mats[...] = take("s2", 0, 608, 576)

    def extend(first, heads):
        part = jnp.concatenate([parts[24 * k + first:24 * k + first + heads] for k in range(3)], axis=0)
        for v in range(2):
            for l in range(12):
                shift = (1 - v) * 23 + 11 - l
                moved = pltpu.roll(part, (768 - shift) % 768, 1) if shift else part
                at = (v * 12 + l) * 3 * heads
                R.shifted[at:at + 3 * heads] = moved
        got = nn(R.shifted[0:72 * heads].astype(BF), picked)
        for n in range(24):
            at = n * 3 * heads
            R.ext[first:first + heads, n, :] = (
                got[at:at + heads] + got[at + heads:at + 2 * heads] + got[at + 2 * heads:at + 3 * heads])

    extend(0, 8)
    rows = lax.broadcasted_iota(jnp.int32, (CELLS, CELLS), 0)
    cols = lax.broadcasted_iota(jnp.int32, (CELLS, CELLS), 1)
    apart = jnp.where(jnp.logical_xor(rows < HALF, cols < HALF), NEG, 0.0).astype(F32)
    apart = apart * jnp.where(last, 1.0, 0.0).astype(F32)
    R.madd[...] = jnp.concatenate([apart, apart], axis=1)

    def expand(pair):
        one, two = R.ext[2 * pair], R.ext[2 * pair + 1]
        for a in range(6):
            at = slice((5 - a) * 24, (5 - a) * 24 + CELLS)
            R.bias[pair, a * 24:(a + 1) * 24, :] = jnp.concatenate([one[:, at], two[:, at]], axis=1)

    def expand_masked(pair):
        expand(4 + pair)
        R.bias[4 + pair] = R.bias[4 + pair] + R.madd[...]

    loop(4, expand)

    lane = lax.broadcasted_iota(jnp.int32, (1, 128), 1)
    left = jnp.where(lane < 64, 1.0, 0.0).astype(BF)
    right = jnp.where(lane < 64, 0.0, 1.0).astype(BF)
    is_left = lax.broadcasted_iota(jnp.int32, (CELLS, 128), 1) < 64

    def stack(t):
        return jnp.concatenate([t * left, t * right], axis=0)

    def at(part, pair, width):
        return pl.ds(aligned(part * width + pair * 128, 128), 128)

    def heads_of(t):
        return jnp.where(is_left, t[:CELLS], t[CELLS:])

    def attend(q2, k, v, bias):
        score = [nt(b, a) + c for a, b, c in zip(q2, k, bias)]
        expo = [jnp.exp(t - jnp.max(t, axis=0, keepdims=True)) for t in score]
        p = [t * (1.0 / jnp.sum(t, axis=0, keepdims=True)) for t in expo]
        pb = [t.astype(BF) for t in p]
        o = [heads_of(tn(a, b)).astype(BF) for a, b in zip(pb, v)]
        return p, pb, o

    def attend_back(q2, k, v, p, pb, go):
        gw = [nt(a, b) for a, b in zip(v, go)]
        gs = [(a * (b - jnp.sum(a * b, axis=0, keepdims=True))).astype(BF) for a, b in zip(p, gw)]
        gv = [nn(a, b).astype(BF) for a, b in zip(pb, go)]
        gk = [nn(a, b).astype(BF) for a, b in zip(gs, q2)]
        gq = [(heads_of(tn(a, b)) * 0.125).astype(BF) for a, b in zip(gs, k)]
        return gq, gk, gv

    gain1 = R.in_gain1[...]
    wait(halo0)

    def window(w):
        return pl.ds(aligned(w * CELLS, 16), CELLS)

    def tile(n, size=256):
        return pl.ds(aligned(n * size, size), size)

    def place1(n):
        R.x1[:, tile(n)] = nn(R.matr[...], R.xr[0, :, tile(n)]).astype(BF)

    def norm1(w):
        dev, inv = norm_stats(R.x1[window(w), :].astype(F32))
        R.rolled1[window(w), :] = (dev * inv * gain1).astype(BF)

    loop(2, place1)
    loop(4, norm1)
    loads.w1.wait()

    def qkv1(n):
        c = pl.ds(aligned(n * 256, 256), 256)
        R.qkv1[:, c] = nn(R.rolled1[...], R.w1[:, c]).astype(BF)

    loop(6, qkv1)

    def four(pair):
        q2 = [stack(R.qkv1[window(w), at(0, pair, 512)] * BF(0.125)) for w in range(4)]
        k = [R.qkv1[window(w), at(1, pair, 512)] for w in range(4)]
        v = [R.qkv1[window(w), at(2, pair, 512)] for w in range(4)]
        return q2, k, v

    def fwd1(pair):
        bias = R.bias[pair]
        masked = bias + R.madd[...]
        _, pb, o = attend(*four(pair), [bias, masked, bias, masked])
        for w in range(4):
            R.prob1[pair * 4 + w] = pb[w]
            R.mixed1[window(w), at(0, pair, 512)] = o[w]

    loop(4, fwd1)
    loads.p1.wait()

    def proj1(n):
        branch = nn(R.mixed1[...], R.p1[:, tile(n)]).astype(BF).astype(F32)
        R.out1[:, tile(n)] = (R.x1[:, tile(n)].astype(F32) + branch).astype(BF)

    loop(2, proj1)

    R.xs[1] = nn(R.mats[336:, :], R.out1[...]).astype(BF)
    halo1 = exchange(1, SEG1, R.xs.at[1], R.xr.at[1], behind)
    R.xr[1, 0:336] = nn(R.mats[0:336, :], R.out1[...]).astype(BF)
    extend(8, 16)
    loop(8, expand_masked)
    R.mats[...] = take("s3", 0, 608, 576)
    R.matr[...] = take("r2", 0, 576, 608)
    wait(halo_c)
    R.ct[...] = nn(take("rc", 0, CELLS, 192), R.cr[0]).astype(BF)
    loads.p2.wait()

    def grad_mixed2(n):
        c = pl.ds(aligned(n * 256, 256), 256)
        R.gm2[:, c] = nt(R.ct[...], R.p2[c, :]).astype(BF)

    loop(4, grad_mixed2)
    R.rolled1t[...] = R.rolled1[...].T
    wait(halo1)
    R.merged[...] = nn(R.matr[...], R.xr[1]).astype(BF)
    loads.wm.wait()
    acc = nn(R.merged[0:CELLS, :], R.wm[0:512, :])
    for s in range(1, 4):
        acc = acc + nn(R.merged[s * CELLS:(s + 1) * CELLS, :], R.wm[s * 512:(s + 1) * 512, :])
    second = acc.astype(BF)
    R.second[...] = second
    gain2 = R.in_gain2[...]
    dev, inv = norm_stats(second.astype(F32))
    rolled2 = (dev * inv * gain2).astype(BF)
    R.rolled2[...] = rolled2
    loads.w2.wait()

    def qkv2(n):
        c = pl.ds(aligned(n * 512, 512), 512)
        R.qkv2[:, c] = nn(R.rolled2[...], R.w2[:, c]).astype(BF)

    loop(6, qkv2)

    r2f = rolled2.astype(F32)
    for t in range(4):
        a = r2f[:, t * 256:t * 256 + 128]
        b = r2f[:, t * 256 + 128:t * 256 + 256]
        c = slice(t * 128, t * 128 + 128)
        R.half2[0, :, c] = jnp.where(is_left, a, pltpu.roll(b, 64, 1)).astype(BF)
        R.half2[1, :, c] = jnp.where(is_left, pltpu.roll(a, 64, 1), b).astype(BF)
    core0 = pltpu.make_async_remote_copy(
        src_ref=R.half2.at[1 - core], dst_ref=R.theirs2, send_sem=R.core_send.at[0],
        recv_sem=R.core_recv.at[0], device_id=other, device_id_type=MESH)
    core0.start()

    def both2(u):
        pairs = [u * 4 + n for n in range(4)]
        q2 = [stack(R.qkv2[:, at(0, c, 1024)] * BF(0.125)) for c in pairs]
        k = [R.qkv2[:, at(1, c, 1024)] for c in pairs]
        v = [R.qkv2[:, at(2, c, 1024)] for c in pairs]
        go = [stack(R.gm2[:, at(0, c, 1024)]) for c in pairs]
        p, pb, o = attend(q2, k, v, [R.bias[4 + c] for c in pairs])
        back = attend_back(q2, k, v, p, pb, go)
        for n, c in enumerate(pairs):
            R.mixed2[:, at(0, c, 1024)] = o[n]
            for part in range(3):
                R.dqkv2[0, :, at(part, c, 1024)] = back[part][n]

    loop(2, both2)
    core1 = pltpu.make_async_remote_copy(
        src_ref=R.dqkv2.at[0], dst_ref=R.dqkv2.at[1], send_sem=R.core_send.at[1],
        recv_sem=R.core_recv.at[1], device_id=other, device_id_type=MESH)
    core1.start()

    grad_rolled = nt(R.dqkv2[0, :, 0:1024], R.w2[:, 0:1024])
    grad_rolled = grad_rolled + nt(R.dqkv2[0, :, 1024:2048], R.w2[:, 1024:2048])
    grad_rolled = grad_rolled + nt(R.dqkv2[0, :, 2048:3072], R.w2[:, 2048:3072])

    def norm_back(grad, xin, gain, grad_out):
        grad = grad.astype(BF).astype(F32) * gain
        dev, inv = norm_stats(xin.astype(F32))
        hat = dev * inv
        inner = inv * (grad - jnp.mean(grad, axis=-1, keepdims=True)
                       - hat * jnp.mean(grad * hat, axis=-1, keepdims=True))
        return (grad_out.astype(F32) + inner.astype(BF).astype(F32)).astype(BF)

    R.gs[...] = norm_back(grad_rolled, R.second[...], gain2, R.ct[...])
    for s in range(4):
        R.merged[s * CELLS:(s + 1) * CELLS, :] = nt(R.gs[...], R.wm[s * 512:(s + 1) * 512, :]).astype(BF)
    R.xs[2] = nn(R.mats[336:, :], R.merged[...]).astype(BF)
    halo2 = exchange(2, SEG1, R.xs.at[2], R.xr.at[2], ahead)
    R.xr[2, 0:336] = nn(R.mats[0:336, :], R.merged[...]).astype(BF)

    R.halft[0] = R.half2[core].T
    core0.wait()
    R.halft[1] = R.theirs2[...].T
    core1.wait()

    def term2(yy):
        c = tile(yy, 768)
        g = nn(R.halft[0], R.dqkv2[0, :, c]) + nn(R.halft[1], R.dqkv2[1, :, c])
        g = g.astype(BF)
        for zz in range(4):
            for hh in range(2):
                r = (zz * 2 + hh) * 64
                for xx in range(2):
                    at = dict(z=zz, x=hh * 2 + xx, y=yy)
                    for p, order in enumerate(ORDERS):
                        block = (at[order[0]] * 4 + at[order[1]]) * 4 + at[order[2]]
                        lanes = xx * 384 + p * 128
                        R.b2[p, block] = g[r:r + 64, lanes:lanes + 128]

    loop(4, term2)

    def rs_start(buf, recv, sem0, step):
        copies = []
        for p, order in enumerate(ORDERS):
            base = 0
            for s in range(step):
                base = base + place[order[s]] * (16 >> (2 * s))
            size = 16 >> (2 * step)
            axis = order[step]
            for k in (1, 2, 3):
                to = lax.rem(place[axis] + k, 4)
                n = sem0 + (step * 3 + p) * 3 + k - 1
                copies.append(pltpu.make_async_remote_copy(
                    src_ref=buf.at[p, pl.ds(base + to * size, size)],
                    dst_ref=recv.at[p, k - 1],
                    send_sem=R.rs_send.at[n],
                    recv_sem=R.rs_recv.at[n],
                    device_id=along(axis, k),
                    device_id_type=MESH))
        for c in copies:
            c.start()
        return copies

    def rs_add(buf, recv, step, copies):
        wait(copies)
        size = 16 >> (2 * step)
        for p, order in enumerate(ORDERS):
            base = 0
            for s in range(step + 1):
                base = base + place[order[s]] * (16 >> (2 * s))

            step_of = min(size, 65536 // (buf.shape[2] * buf.shape[3]))

            def add(n):
                at = pl.ds(base + n * step_of, step_of)
                near = pl.ds(n * step_of, step_of)
                t = buf[p, at].astype(F32) + recv[p, 0, near].astype(F32)
                t = t + recv[p, 1, near].astype(F32) + recv[p, 2, near].astype(F32)
                buf[p, at] = t.astype(BF)

            loop(size // step_of, add)

    def region(order, step):
        base = 0
        for k in range(step):
            base = base + place[order[k]] * (16 >> (2 * k))
        return base, 16 >> (2 * step)

    def ring(buf, via, recv, step):
        out = []
        for p, order in enumerate(ORDERS):
            base, size = region(order, step)
            half = size // 2
            axis = order[step]
            up, opposite, down = [base + lax.rem(place[axis] + k, 4) * size for k in (1, 2, 3)]
            ends = along(axis, 1), along(axis, 3)
            moves = (
                (opposite, via.at[p, 0], 0), (opposite + half, via.at[p, 1], 1),
                (up + half, recv.at[p, 0, pl.ds(half, half)], 0), (down, recv.at[p, 1, pl.ds(0, half)], 1),
                (up, recv.at[p, 0, pl.ds(0, half)], 0), (down + half, recv.at[p, 1, pl.ds(half, half)], 1))
            out.append([pltpu.make_async_remote_copy(
                src_ref=buf.at[p, pl.ds(start, half)], dst_ref=target,
                send_sem=R.ring_send.at[(step * 3 + p) * 6 + n], recv_sem=R.ring_recv.at[(step * 3 + p) * 6 + n],
                device_id=ends[way], device_id_type=MESH) for n, (start, target, way) in enumerate(moves)])
        return out

    def ring_start(*what):
        copies = ring(*what)
        for pair in (slice(0, 2), slice(2, 4)):
            for part in copies:
                for c in part[pair]:
                    c.start()

    def ring_relay(buf, via, recv, step):
        copies = ring(buf, via, recv, step)
        for p, order in enumerate(ORDERS):
            base, size = region(order, step)
            half = size // 2
            up, down = [base + lax.rem(place[order[step]] + k, 4) * size for k in (1, 3)]
            for way, start in ((0, up), (1, down + half)):
                copies[p][way].wait_recv()
                at = pl.ds(start, half)
                buf[p, at] = (buf[p, at].astype(F32) + via[p, way].astype(F32)).astype(BF)
                copies[p][4 + way].start()

    def ring_finish(buf, via, recv, step):
        copies = ring(buf, via, recv, step)
        for p, order in enumerate(ORDERS):
            for n, c in enumerate(copies[p]):
                c.wait_send()
                if n >= 2:
                    c.wait_recv()
            base, size = region(order, step + 1)[0], region(order, step)[1]
            at = pl.ds(base, size)
            t = buf[p, at].astype(F32) + recv[p, 0].astype(F32) + recv[p, 1].astype(F32)
            buf[p, at] = t.astype(BF)

    def rs_last(buf, recv, p, copies):
        order = ORDERS[p]
        base = (place[order[0]] * 4 + place[order[1]]) * 4 + place[order[2]]
        t = buf[p, base].astype(F32) + recv[p, 0, 0].astype(F32)
        return t + recv[p, 1, 0].astype(F32) + recv[p, 2, 0].astype(F32)

    first_ring = (R.b2, R.b2v0, R.b2r0, 0)
    second_ring = (R.b2, R.b2v1, R.b2r1, 1)
    ring_start(*first_ring)
    R.mats[...] = take("s4", 0, 608, 576)
    R.matr[...] = take("r3", 0, 576, 608)

    wait(halo2)
    R.g1[...] = nn(R.matr[...], R.xr[2]).astype(BF)

    def grad_mixed1(n):
        R.gm1[:, tile(n)] = nt(R.g1[...], R.p1[tile(n), :]).astype(BF)

    loop(2, grad_mixed1)

    def bwd1(pair):
        q2, k, v = four(pair)
        go = [stack(R.gm1[window(w), at(0, pair, 512)]) for w in range(4)]
        pb = [R.prob1[pair * 4 + w] for w in range(4)]
        back = attend_back(q2, k, v, [t.astype(F32) for t in pb], pb, go)
        for w in range(4):
            for part in range(3):
                R.dqkv1[window(w), at(part, pair, 512)] = back[part][w]
        if pair == 1:
            ring_relay(*first_ring)

    loop(4, bwd1)

    def to_core(t):
        return pltpu.make_async_remote_copy(
            src_ref=R.b1h.at[t, 1 - core], dst_ref=R.b1c.at[t], send_sem=R.core_send.at[2 + t],
            recv_sem=R.core_recv.at[2 + t], device_id=other, device_id_type=MESH)

    def term1(t):
        c = pl.ds(aligned(t * 384, 128), 384)
        g = nn(R.rolled1t[...], R.dqkv1[:, c])
        pick = is_left[0:16]
        for zz in range(4):
            for hh in range(2):
                for cc in range(2):
                    r = ((zz * 2 + hh) * 2 + cc) * 32
                    upper = g[r:r + 16, 128:256]
                    lower = pltpu.roll(g[r + 16:r + 32, 128:256], 64, 1)
                    mixes = (jnp.where(pick, upper, lower), jnp.where(pick, lower, upper))
                    for odd in range(2):
                        lanes = slice(odd * 256, odd * 256 + 128)
                        pieces = (g[r:r + 16, lanes], g[r + 16:r + 32, lanes], mixes[odd])
                        for p in range(3):
                            R.b1h[t, cc, p, zz * 4 + hh * 2 + odd] = pieces[p].astype(BF)
        to_core(t).start()

    loop(4, term1)
    ring_finish(*first_ring)
    ring_start(*second_ring)

    for t in range(4):
        to_core(t).wait()
        for p, order in enumerate(ORDERS):
            g = R.b1h[t, core, p].astype(F32) + R.b1c[t, p].astype(F32)
            for n in range(16):
                at = dict(z=n // 4, x=n % 4, y=t)
                block = (at[order[0]] * 4 + at[order[1]]) * 4 + at[order[2]]
                R.b1[p, block] = g[n].astype(BF)
    mine = R.b1
    small = rs_start(mine, R.b1r0, 27, 0)
    ring_relay(*second_ring)

    def grad_rolled1(n):
        R.gm1[:, tile(n)] = nt(R.dqkv1[...], R.w1[tile(n), :]).astype(BF)

    def tail1(w):
        r = window(w)
        R.out1[r, :] = norm_back(R.gm1[r, :], R.x1[r, :], gain1, R.g1[r, :])

    loop(2, grad_rolled1)
    loop(4, tail1)
    R.xs[3] = nn(R.mats[336:, :], R.out1[...]).astype(BF)
    halo3 = exchange(3, SEG1, R.xs.at[3], R.xr.at[3], ahead)
    R.xr[3, 0:336] = nn(R.mats[0:336, :], R.out1[...]).astype(BF)

    branch = nn(R.mixed2[...], R.p2[...]).astype(BF).astype(F32)
    R.res[...] = (R.second[...].astype(F32) + branch).astype(BF)
    R.cs[1] = nn(take("sr", 48, 144, CELLS), R.res[...]).astype(BF)
    halo_r = exchange(5, SEG2, R.cs.at[1], R.cr.at[1], ahead)
    R.cr[1, 0:48] = nn(take("sr", 0, 48, CELLS), R.res[...]).astype(BF)

    R.matr[...] = take("r4", 0, 576, 608)
    rs_add(mine, R.b1r0, 0, small)
    small = rs_start(mine, R.b1r1, 27, 1)
    ring_finish(*second_ring)
    big = rs_start(R.b2, R.b2r2, 0, 2)
    wait(halo_r)
    R.v_res[...] = nn(take("rr", 0, CELLS, 192), R.cr[1]).astype(BF).reshape(72, 2, 1024)
    puts = [put(0, "res")]
    rs_add(mine, R.b1r1, 1, small)
    small = rs_start(mine, R.b1r2, 27, 2)
    wait(halo3)
    R.v_tok[...] = jnp.where(present, nn(R.matr[...], R.xr[3]), 0.0).astype(BF)
    puts.append(put(1, "tok"))
    wait(big)
    for p in range(3):
        R.v_q2[:, p * 128:(p + 1) * 128] = rs_last(R.b2, R.b2r2, p, big)
    puts.append(put(3, "q2"))
    wait(small)
    a, b, m = [rs_last(mine, R.b1r2, p, small) for p in range(3)]
    turned = pltpu.roll(m, 64, 1)
    even = xl == 0
    a_turned = pltpu.roll(a, 64, 1)
    b_turned = pltpu.roll(b, 64, 1)
    pick = is_left[0:16]
    R.v_q1[0:16, 0:128] = jnp.where(even, a, jnp.where(pick, turned, a_turned))
    R.v_q1[16:32, 0:128] = jnp.where(even, b, jnp.where(pick, m, b_turned))
    R.v_q1[0:16, 128:192] = jnp.where(even, m, a_turned)[:, 0:64]
    R.v_q1[16:32, 128:192] = jnp.where(even, turned, b_turned)[:, 0:64]
    puts.append(put(2, "q1"))
    wait(puts)


def hand_on(*refs):
    given, out, held, sem = refs[0:4], refs[4:8], refs[8:12], refs[12]
    come = [pltpu.make_async_copy(given[n], held[n], sem.at[n]) for n in range(4)]
    leave = [pltpu.make_async_copy(held[n], out[n], sem.at[4 + n]) for n in range(4)]
    for c in come:
        c.start()
    for n in range(4):
        come[n].wait()
        leave[n].start()
    for c in leave:
        c.wait()


def shards(tokens, observed, mask_token, gain_one, qkv_one, table_one, proj_one, merge_weight, gain_two, qkv_two,
           table_two, proj_two, cotangent, sizes):
    first = tokens.transpose(0, 2, 1, 3).reshape(576, 512)
    cot = cotangent.transpose(1, 2, 0, 3).reshape(72, 2, 1024)
    seen = observed.transpose(2, 0, 1)
    given = dict(first=first, cot=cot, w1=qkv_one, p1=proj_one, wm=merge_weight, w2=qkv_two, p2=proj_two)
    args = [given[k] for k in LOADS]
    args += [jnp.asarray(TABLE_OF), seen, mask_token[None], table_one, table_two, gain_one[None], gain_two[None]]
    shapes = (
        jax.ShapeDtypeStruct((72, 2, 1024), BF),
        jax.ShapeDtypeStruct((576, 512), BF),
        jax.ShapeDtypeStruct((32, 192), F32),
        jax.ShapeDtypeStruct((64, 384), F32),
    )
    outs = pl.pallas_call(
        functools.partial(body, sizes),
        out_shape=shapes,
        in_specs=[pl.BlockSpec(memory_space=pl.ANY)] * len(LOADS) + [pl.BlockSpec(memory_space=pltpu.VMEM)] * len(SMALL),
        out_specs=[pl.BlockSpec(memory_space=pl.ANY)] * 4,
        scratch_shapes=list(SCRATCH.values()),
        compiler_params=pltpu.CompilerParams(
            collective_id=0, has_side_effects=True, vmem_limit_bytes=62 * 1024 * 1024),
        cost_estimate=pl.CostEstimate(flops=9 * 10 ** 9, bytes_accessed=24 * 10 ** 6, transcendentals=10 ** 6),
    )(*args)
    res, tok, q1, q2 = pl.pallas_call(
        hand_on,
        out_shape=shapes,
        in_specs=[pl.BlockSpec(memory_space=pl.ANY)] * 4,
        out_specs=[pl.BlockSpec(memory_space=pl.ANY)] * 4,
        scratch_shapes=[pltpu.VMEM(s.shape, s.dtype) for s in shapes] + [pltpu.SemaphoreType.DMA((8,))],
    )(*outs)
    result = res.reshape(12, 6, 2, 1024).transpose(2, 0, 1, 3)
    grad_tokens = tok.reshape(2, 12, 24, 512).transpose(0, 2, 1, 3)
    return (result, grad_tokens, q1, q2)


def solution(mesh):
    sizes = (mesh.shape["lon"], mesh.shape["lat"])
    split = P(None, "lon", "lat", None)

    def run(*args):
        return shards(*args, sizes)

    return jax.shard_map(
        run,
        mesh=mesh,
        in_specs=(split, P(None, "lon", "lat")) + (P(),) * 10 + (split,),
        out_specs=(split, split, P("lon", "lat"), P("lon", "lat")),
        check_vma=False,
    )
```

```python
import functools
from types import SimpleNamespace
import numpy as np
import jax
import jax.numpy as jnp
from jax import lax
from jax.experimental import pallas as pl
from jax.experimental.pallas import tpu as pltpu
from jax.sharding import PartitionSpec as P

BF = jnp.bfloat16
F32 = jnp.float32
EPS = 1e-05
NEG = -1000000000.0
MESH = pl.DeviceIdType.MESH
CELLS = 144
HALF = 72

SEG1 = ((0, 336), (336, 112), (448, 112), (560, 48))
SEG2 = ((0, 48), (48, 48), (96, 48), (144, 48))


def _cells(along, across, half_lon, half_lat):
    out = [[], [], [], []]
    for v in range(2):
        for i in range(along):
            for j in range(across):
                seg = (1 if i < half_lon else 0) + (2 if j < half_lat else 0)
                moved = (v, (i - half_lon) % along, (j - half_lat) % across)
                out[seg].append(((v, i, j), moved))
    return out


def _send_index(segs, cells, row_of):
    out = [-1] * (segs[-1][0] + segs[-1][1])
    for (start, _), members in zip(segs, cells):
        for n, (cell, _) in enumerate(members):
            out[start + n] = row_of(*cell)
    return out


def _recv_index(segs, cells, row_of, rows):
    out = [-1] * rows
    for (start, _), members in zip(segs, cells):
        for n, (_, moved) in enumerate(members):
            out[row_of(*moved)] = start + n
    return out


def _inverse(index, rows):
    out = [-1] * rows
    for n, m in enumerate(index):
        if m >= 0:
            out[m] = n
    return out


def _nat1(v, i, j):
    return (v * 12 + j) * 24 + i


def _win1(v, i, j):
    return ((i // 12) * 2 + j // 6) * CELLS + (j % 6) * 24 + v * 12 + i % 12


def _merge(v, i, j):
    return ((i % 2) * 2 + j % 2) * CELLS + (j // 2) * 24 + v * 12 + i // 2


def _nat2(v, i, j):
    return (i * 6 + j) * 2 + v


def _win2(v, i, j):
    return j * 24 + v * 12 + i


def _indices():
    one = _cells(24, 12, 6, 3)
    two = _cells(12, 6, 6, 3)
    s1 = _send_index(SEG1, one, _nat1)
    r1 = _recv_index(SEG1, one, _win1, 576)
    s2 = _send_index(SEG1, one, _win1)
    r2 = _recv_index(SEG1, one, _merge, 576)
    sc = _send_index(SEG2, two, _nat2)
    rc = _recv_index(SEG2, two, _win2, CELLS)
    flip = [-1] * 768
    for x in range(3):
        for y in range(23):
            for z in range(11):
                flip[(x * 23 + y) * 11 + z] = z * 69 + x * 23 + y
    pick = [-1] * 768
    for z in range(11):
        for v in range(2):
            for l in range(12):
                pick[z * 69 + v * 23 + l] = z * 24 + v * 12 + l
    return dict(s1=s1, r1=r1, s2=s2, r2=r2, s3=_inverse(r2, 608), r3=_inverse(s2, 576), s4=_inverse(r1, 608),
                r4=_inverse(s1, 576), sc=sc, rc=rc, sr=_inverse(rc, 192), rr=_inverse(sc, CELLS), flip=flip, pick=pick)


INDEX = _indices()
COLUMNS = dict(s1=576, r1=608, s2=576, r2=608, s3=576, r3=608, s4=576, r4=608, sc=CELLS, rc=192, sr=CELLS, rr=192,
               flip=768, pick=264)


def _matrix(key):
    index = np.asarray(INDEX[key])
    m = np.zeros((len(index), COLUMNS[key]), np.float32)
    rows = np.nonzero(index >= 0)[0]
    m[rows, index[rows]] = 1
    return m.astype(jnp.bfloat16)


MATRICES = {k: _matrix(k) for k in INDEX}

SHAPES = dict(first=(576, 512), s1=(608, 576), cot=(72, 2, 1024), sc=(192, CELLS), flip=(768, 768), pick=(768, 264),
              r1=(576, 608), w1=(512, 1536), p1=(512, 512), rc=(CELLS, 192), p2=(1024, 1024), wm=(2048, 1024),
              w2=(1024, 3072), sr=(192, CELLS), rr=(CELLS, 192), s2=(608, 576), r2=(576, 608), s3=(608, 576),
              r3=(576, 608), s4=(608, 576), r4=(576, 608))
LOADS = tuple(SHAPES)
LATER = dict(s2="s1", s3="s1", s4="s1", r2="r1", r3="r1", r4="r1")


def nn(a, b):
    return lax.dot_general(a, b, (((1,), (0,)), ((), ())), preferred_element_type=F32)


def nt(a, b):
    return lax.dot_general(a, b, (((1,), (1,)), ((), ())), preferred_element_type=F32)


def tn(a, b):
    return lax.dot_general(a, b, (((0,), (0,)), ((), ())), preferred_element_type=F32)


def norm_stats(x):
    centre = jnp.mean(x, axis=-1, keepdims=True)
    dev = x - centre
    spread = jnp.mean(dev * dev, axis=-1, keepdims=True)
    return dev, lax.rsqrt(spread + EPS)


def aligned(start, multiple):
    return start if isinstance(start, int) else pl.multiple_of(start, multiple)


def loop(n, body):
    for i in range(n):
        body(i)


SCRATCH = dict(
    {k: pltpu.VMEM(SHAPES[k], BF) for k in LOADS if k not in LATER},
    tables=pltpu.VMEM((24, 768), F32),
    shifted=pltpu.VMEM((1152, 768), F32),
    ext=pltpu.VMEM((24, 24, 264), F32),
    bias=pltpu.VMEM((12, CELLS, 288), F32),
    inv1=pltpu.VMEM((576, 1), F32),
    hat1=pltpu.VMEM((576, 512), F32),
    madd=pltpu.VMEM((CELLS, 288), F32),
    xr=pltpu.VMEM((4, 608, 512), BF),
    xs=pltpu.VMEM((4, 272, 512), BF),
    cr=pltpu.VMEM((2, 192, 1024), BF),
    cs=pltpu.VMEM((2, 144, 1024), BF),
    x1=pltpu.VMEM((576, 512), BF),
    rolled1=pltpu.VMEM((576, 512), BF),
    rolled1t=pltpu.VMEM((512, 576), BF),
    qkv1=pltpu.VMEM((576, 1536), BF),
    dqkv1=pltpu.VMEM((576, 1536), BF),
    prob1=pltpu.VMEM((16, CELLS, 288), BF),
    mixed1=pltpu.VMEM((576, 512), BF),
    out1=pltpu.VMEM((576, 512), BF),
    gm1=pltpu.VMEM((576, 512), BF),
    g1=pltpu.VMEM((576, 512), BF),
    merged=pltpu.VMEM((576, 512), BF),
    second=pltpu.VMEM((CELLS, 1024), BF),
    rolled2=pltpu.VMEM((CELLS, 1024), BF),
    qkv2=pltpu.VMEM((CELLS, 3072), BF),
    dqkv2=pltpu.VMEM((2, CELLS, 3072), BF),
    half2=pltpu.VMEM((2, CELLS, 512), BF),
    theirs2=pltpu.VMEM((CELLS, 512), BF),
    halft=pltpu.VMEM((2, 512, CELLS), BF),
    mixed2=pltpu.VMEM((CELLS, 1024), BF),
    ct=pltpu.VMEM((CELLS, 1024), BF),
    gm2=pltpu.VMEM((CELLS, 1024), BF),
    res=pltpu.VMEM((CELLS, 1024), BF),
    gs=pltpu.VMEM((CELLS, 1024), BF),
    v_res=pltpu.VMEM((72, 2, 1024), BF),
    v_tok=pltpu.VMEM((576, 512), BF),
    v_q1=pltpu.VMEM((32, 192), F32),
    v_q2=pltpu.VMEM((64, 384), F32),
    out_sem=pltpu.SemaphoreType.DMA((4,)),
    b2=pltpu.VMEM((3, 64, 64, 128), BF),
    b2v0=pltpu.VMEM((3, 2, 8, 64, 128), BF),
    b2r0=pltpu.VMEM((3, 2, 16, 64, 128), BF),
    b2v1=pltpu.VMEM((3, 2, 2, 64, 128), BF),
    b2r1=pltpu.VMEM((3, 2, 4, 64, 128), BF),
    b2r2=pltpu.VMEM((3, 3, 1, 64, 128), BF),
    b1=pltpu.VMEM((3, 64, 16, 128), BF),
    b1h=pltpu.VMEM((4, 2, 3, 16, 16, 128), BF),
    b1c=pltpu.VMEM((4, 3, 16, 16, 128), BF),
    b1r0=pltpu.VMEM((3, 3, 16, 16, 128), BF),
    b1r1=pltpu.VMEM((3, 3, 4, 16, 128), BF),
    b1r2=pltpu.VMEM((3, 3, 1, 16, 128), BF),
    load_sem=pltpu.SemaphoreType.DMA((len(LOADS),)),
    halo_send=pltpu.SemaphoreType.DMA((18,)),
    halo_recv=pltpu.SemaphoreType.DMA((18,)),
    rs_send=pltpu.SemaphoreType.DMA((54,)),
    rs_recv=pltpu.SemaphoreType.DMA((54,)),
    ring_send=pltpu.SemaphoreType.DMA((36,)),
    ring_recv=pltpu.SemaphoreType.DMA((36,)),
    core_send=pltpu.SemaphoreType.DMA((6,)),
    core_recv=pltpu.SemaphoreType.DMA((6,)),
)
SMALL = ("seen", "mask", "table1", "table2", "gain1", "gain2")
OUTPUTS = ("o_res", "o_tok", "o_q1", "o_q2")

ORDERS = (("z", "x", "y"), ("x", "y", "z"), ("y", "z", "x"))


def body(sizes, *refs):
    n_lon, n_lat = sizes
    names = ["in_" + n for n in LOADS + SMALL] + list(OUTPUTS) + list(SCRATCH)
    R = SimpleNamespace(**dict(zip(names, refs, strict=True)))

    e = lax.axis_index("lon")
    d = lax.axis_index("lat")
    core, xh, z = lax.rem(e, 2), lax.rem(e // 2, 2), e // 4
    xl, y = lax.rem(d, 2), d // 2
    x = xh * 2 + xl
    place = dict(x=x, y=y, z=z)
    e_up, e_dn = lax.rem(e + 1, n_lon), lax.rem(e + n_lon - 1, n_lon)
    d_up, d_dn = lax.rem(d + 1, n_lat), lax.rem(d + n_lat - 1, n_lat)
    last = d == n_lat - 1
    ahead = ((e_up, d), (e, d_up), (e_up, d_up))
    behind = ((e_dn, d), (e, d_dn), (e_dn, d_dn))
    other = (e + 1 - 2 * core, d)

    def device(x, y, z):
        return (z * 4 + (x // 2) * 2 + core, y * 2 + lax.rem(x, 2))

    def along(axis, k):
        at = dict(place)
        at[axis] = lax.rem(at[axis] + k, 4)
        return device(**at)

    loads = SimpleNamespace()
    for n, name in enumerate(LOADS):
        target = getattr(R, LATER.get(name, name))
        copy = pltpu.make_async_copy(getattr(R, "in_" + name), target, R.load_sem.at[n])
        if name not in LATER:
            copy.start()
        setattr(loads, name, copy)

    barrier = pltpu.get_barrier_semaphore()
    partners = list(ahead) + list(behind) + [other]
    for axis in place:
        for k in (1, 2, 3):
            partners.append(along(axis, k))
    for who in partners:
        pl.semaphore_signal(barrier, inc=1, device_id=who, device_id_type=MESH)

    def exchange(n, segs, source, target, to):
        copies = []
        for k in range(3):
            start, size = segs[k + 1]
            rows = pl.ds(start, size)
            copies.append(pltpu.make_async_remote_copy(
                src_ref=source.at[pl.ds(start - segs[0][1], size)],
                dst_ref=target.at[rows],
                send_sem=R.halo_send.at[3 * n + k],
                recv_sem=R.halo_recv.at[3 * n + k],
                device_id=to[k],
                device_id_type=MESH))
        for c in copies:
            c.start()
        return copies

    def wait(copies):
        for c in copies:
            c.wait()

    def put(n, name):
        copy = pltpu.make_async_copy(getattr(R, "v_" + name), getattr(R, "o_" + name), R.out_sem.at[n])
        copy.start()
        return copy

    seen = R.in_seen[...]
    seen = jnp.concatenate([seen[:, 0, :], seen[:, 1, :]], axis=0).astype(F32).astype(BF)
    row = lax.broadcasted_iota(jnp.int32, (576, 24), 0)
    col = lax.broadcasted_iota(jnp.int32, (576, 24), 1)
    per = nn(jnp.where(row // 24 == col, 1.0, 0.0).astype(BF), seen)
    present = jnp.sum(jnp.where(lax.rem(row, 24) == col, per, 0.0), axis=-1, keepdims=True) > 0.5

    loads.first.wait()
    R.first[...] = jnp.where(present, R.first[...].astype(F32), R.in_mask[...].astype(BF).astype(F32)).astype(BF)
    loads.s1.wait()
    R.xs[0] = nn(R.s1[336:, :], R.first[...]).astype(BF)

    pl.semaphore_wait(barrier, len(partners))
    halo0 = exchange(0, SEG1, R.xs.at[0], R.xr.at[0], behind)
    R.xr[0, 0:336] = nn(R.s1[0:336, :], R.first[...]).astype(BF)
    loads.s2.start()
    loads.sc.wait()
    loads.cot.wait()
    cot = R.cot[...].reshape(CELLS, 1024)
    R.cs[0] = nn(R.sc[48:, :], cot).astype(BF)
    halo_c = exchange(4, SEG2, R.cs.at[0], R.cr.at[0], behind)
    R.cr[0, 0:48] = nn(R.sc[0:48, :], cot).astype(BF)

    R.tables[...] = jnp.zeros((24, 768), F32)
    R.tables[0:8, 0:759] = R.in_table1[...]
    R.tables[8:24, 0:759] = R.in_table2[...]
    table = R.tables[...]
    high = table.astype(BF).astype(F32)
    mid = (table - high).astype(BF).astype(F32)
    low = table - high - mid
    parts = jnp.concatenate([high, mid, low], axis=0).astype(BF)
    loads.flip.wait()
    parts = nn(parts, R.flip[...])
    loads.pick.wait()
    picked = R.pick[...]

    def extend(first, heads):
        part = jnp.concatenate([parts[24 * k + first:24 * k + first + heads] for k in range(3)], axis=0)
        for v in range(2):
            for l in range(12):
                shift = (1 - v) * 23 + 11 - l
                moved = pltpu.roll(part, (768 - shift) % 768, 1) if shift else part
                at = (v * 12 + l) * 3 * heads
                R.shifted[at:at + 3 * heads] = moved
        got = nn(R.shifted[0:72 * heads].astype(BF), picked)
        for n in range(24):
            at = n * 3 * heads
            R.ext[first:first + heads, n, :] = (
                got[at:at + heads] + got[at + heads:at + 2 * heads] + got[at + 2 * heads:at + 3 * heads])

    extend(0, 8)
    rows = lax.broadcasted_iota(jnp.int32, (CELLS, CELLS), 0)
    cols = lax.broadcasted_iota(jnp.int32, (CELLS, CELLS), 1)
    apart = jnp.where(jnp.logical_xor(rows < HALF, cols < HALF), NEG, 0.0).astype(F32)
    apart = apart * jnp.where(last, 1.0, 0.0).astype(F32)
    R.madd[...] = jnp.concatenate([apart, apart], axis=1)

    def expand(pair):
        one, two = R.ext[2 * pair], R.ext[2 * pair + 1]
        for a in range(6):
            at = slice((5 - a) * 24, (5 - a) * 24 + CELLS)
            R.bias[pair, a * 24:(a + 1) * 24, :] = jnp.concatenate([one[:, at], two[:, at]], axis=1)

    def expand_masked(pair):
        expand(4 + pair)
        R.bias[4 + pair] = R.bias[4 + pair] + R.madd[...]

    loop(4, expand)

    lane = lax.broadcasted_iota(jnp.int32, (1, 128), 1)
    left = jnp.where(lane < 64, 1.0, 0.0).astype(BF)
    right = jnp.where(lane < 64, 0.0, 1.0).astype(BF)
    is_left = lax.broadcasted_iota(jnp.int32, (CELLS, 128), 1) < 64

    def stack(t):
        return jnp.concatenate([t * left, t * right], axis=0)

    def at(part, pair, width):
        return pl.ds(aligned(part * width + pair * 128, 128), 128)

    def heads_of(t):
        return jnp.where(is_left, t[:CELLS], t[CELLS:])

    def attend(q2, k, v, bias):
        score = [nt(b, a) + c for a, b, c in zip(q2, k, bias)]
        expo = [jnp.exp(t - jnp.max(t, axis=0, keepdims=True)) for t in score]
        p = [t * (1.0 / jnp.sum(t, axis=0, keepdims=True)) for t in expo]
        pb = [t.astype(BF) for t in p]
        o = [heads_of(tn(a, b)).astype(BF) for a, b in zip(pb, v)]
        return p, pb, o

    def attend_back(q2, k, v, p, pb, go):
        gw = [nt(a, b) for a, b in zip(v, go)]
        gs = [(a * (b - jnp.sum(a * b, axis=0, keepdims=True))).astype(BF) for a, b in zip(p, gw)]
        gv = [nn(a, b).astype(BF) for a, b in zip(pb, go)]
        gk = [nn(a, b).astype(BF) for a, b in zip(gs, q2)]
        gq = [(heads_of(tn(a, b)) * 0.125).astype(BF) for a, b in zip(gs, k)]
        return gq, gk, gv

    gain1 = R.in_gain1[...]
    loads.r1.wait()
    wait(halo0)

    def window(w):
        return pl.ds(aligned(w * CELLS, 16), CELLS)

    def tile(n, size=256):
        return pl.ds(aligned(n * size, size), size)

    def place1(n):
        R.x1[:, tile(n)] = nn(R.r1[...], R.xr[0, :, tile(n)]).astype(BF)

    def norm1(w):
        dev, inv = norm_stats(R.x1[window(w), :].astype(F32))
        R.inv1[window(w), :] = inv
        R.hat1[window(w), :] = dev * inv
        R.rolled1[window(w), :] = (dev * inv * gain1).astype(BF)

    loop(2, place1)
    loop(4, norm1)
    loads.r2.start()
    loads.w1.wait()

    def qkv1(n):
        c = pl.ds(aligned(n * 256, 256), 256)
        R.qkv1[:, c] = nn(R.rolled1[...], R.w1[:, c]).astype(BF)

    loop(6, qkv1)

    def four(pair):
        q2 = [stack(R.qkv1[window(w), at(0, pair, 512)] * BF(0.125)) for w in range(4)]
        k = [R.qkv1[window(w), at(1, pair, 512)] for w in range(4)]
        v = [R.qkv1[window(w), at(2, pair, 512)] for w in range(4)]
        return q2, k, v

    def fwd1(pair):
        bias = R.bias[pair]
        masked = bias + R.madd[...]
        _, pb, o = attend(*four(pair), [bias, masked, bias, masked])
        for w in range(4):
            R.prob1[pair * 4 + w] = pb[w]
            R.mixed1[window(w), at(0, pair, 512)] = o[w]

    loop(4, fwd1)
    loads.p1.wait()

    def proj1(n):
        branch = nn(R.mixed1[...], R.p1[:, tile(n)]).astype(BF).astype(F32)
        R.out1[:, tile(n)] = (R.x1[:, tile(n)].astype(F32) + branch).astype(BF)

    loop(2, proj1)

    loads.s2.wait()
    R.xs[1] = nn(R.s1[336:, :], R.out1[...]).astype(BF)
    halo1 = exchange(1, SEG1, R.xs.at[1], R.xr.at[1], behind)
    R.xr[1, 0:336] = nn(R.s1[0:336, :], R.out1[...]).astype(BF)
    loads.s3.start()
    extend(8, 16)
    loop(8, expand_masked)
    wait(halo_c)
    loads.rc.wait()
    R.ct[...] = nn(R.rc[...], R.cr[0]).astype(BF)
    loads.p2.wait()

    def grad_mixed2(n):
        c = pl.ds(aligned(n * 256, 256), 256)
        R.gm2[:, c] = nt(R.ct[...], R.p2[c, :]).astype(BF)

    loop(4, grad_mixed2)
    R.rolled1t[...] = R.rolled1[...].T
    loads.r2.wait()
    wait(halo1)
    R.merged[...] = nn(R.r1[...], R.xr[1]).astype(BF)
    loads.r3.start()
    loads.wm.wait()
    acc = nn(R.merged[0:CELLS, :], R.wm[0:512, :])
    for s in range(1, 4):
        acc = acc + nn(R.merged[s * CELLS:(s + 1) * CELLS, :], R.wm[s * 512:(s + 1) * 512, :])
    second = acc.astype(BF)
    R.second[...] = second
    gain2 = R.in_gain2[...]
    dev2, inv2 = norm_stats(second.astype(F32))
    hat2 = dev2 * inv2
    rolled2 = (hat2 * gain2).astype(BF)
    R.rolled2[...] = rolled2
    loads.w2.wait()

    def qkv2(n):
        c = pl.ds(aligned(n * 512, 512), 512)
        R.qkv2[:, c] = nn(R.rolled2[...], R.w2[:, c]).astype(BF)

    loop(6, qkv2)

    r2f = rolled2.astype(F32)
    for t in range(4):
        a = r2f[:, t * 256:t * 256 + 128]
        b = r2f[:, t * 256 + 128:t * 256 + 256]
        c = slice(t * 128, t * 128 + 128)
        R.half2[0, :, c] = jnp.where(is_left, a, pltpu.roll(b, 64, 1)).astype(BF)
        R.half2[1, :, c] = jnp.where(is_left, pltpu.roll(a, 64, 1), b).astype(BF)
    core0 = pltpu.make_async_remote_copy(
        src_ref=R.half2.at[1 - core], dst_ref=R.theirs2, send_sem=R.core_send.at[0],
        recv_sem=R.core_recv.at[0], device_id=other, device_id_type=MESH)
    core0.start()

    def both2(u):
        pairs = [u * 4 + n for n in range(4)]
        q2 = [stack(R.qkv2[:, at(0, c, 1024)] * BF(0.125)) for c in pairs]
        k = [R.qkv2[:, at(1, c, 1024)] for c in pairs]
        v = [R.qkv2[:, at(2, c, 1024)] for c in pairs]
        go = [stack(R.gm2[:, at(0, c, 1024)]) for c in pairs]
        p, pb, o = attend(q2, k, v, [R.bias[4 + c] for c in pairs])
        back = attend_back(q2, k, v, p, pb, go)
        for n, c in enumerate(pairs):
            R.mixed2[:, at(0, c, 1024)] = o[n]
            for part in range(3):
                R.dqkv2[0, :, at(part, c, 1024)] = back[part][n]

    loop(2, both2)
    core1 = pltpu.make_async_remote_copy(
        src_ref=R.dqkv2.at[0], dst_ref=R.dqkv2.at[1], send_sem=R.core_send.at[1],
        recv_sem=R.core_recv.at[1], device_id=other, device_id_type=MESH)
    core1.start()

    grad_rolled = nt(R.dqkv2[0, :, 0:1024], R.w2[:, 0:1024])
    grad_rolled = grad_rolled + nt(R.dqkv2[0, :, 1024:2048], R.w2[:, 1024:2048])
    grad_rolled = grad_rolled + nt(R.dqkv2[0, :, 2048:3072], R.w2[:, 2048:3072])

    def norm_back(grad, hat, inv, gain, grad_out):
        grad = grad.astype(BF).astype(F32) * gain
        inner = inv * (grad - jnp.mean(grad, axis=-1, keepdims=True)
                       - hat * jnp.mean(grad * hat, axis=-1, keepdims=True))
        return (grad_out.astype(F32) + inner.astype(BF).astype(F32)).astype(BF)

    R.gs[...] = norm_back(grad_rolled, hat2, inv2, gain2, R.ct[...])
    for s in range(4):
        R.merged[s * CELLS:(s + 1) * CELLS, :] = nt(R.gs[...], R.wm[s * 512:(s + 1) * 512, :]).astype(BF)
    loads.s3.wait()
    R.xs[2] = nn(R.s1[336:, :], R.merged[...]).astype(BF)
    halo2 = exchange(2, SEG1, R.xs.at[2], R.xr.at[2], ahead)
    R.xr[2, 0:336] = nn(R.s1[0:336, :], R.merged[...]).astype(BF)
    loads.s4.start()

    R.halft[0] = R.half2[core].T
    core0.wait()
    R.halft[1] = R.theirs2[...].T
    core1.wait()

    def term2(yy):
        c = tile(yy, 768)
        g = nn(R.halft[0], R.dqkv2[0, :, c]) + nn(R.halft[1], R.dqkv2[1, :, c])
        g = g.astype(BF)
        for zz in range(4):
            for hh in range(2):
                r = (zz * 2 + hh) * 64
                for xx in range(2):
                    at = dict(z=zz, x=hh * 2 + xx, y=yy)
                    for p, order in enumerate(ORDERS):
                        block = (at[order[0]] * 4 + at[order[1]]) * 4 + at[order[2]]
                        lanes = xx * 384 + p * 128
                        R.b2[p, block] = g[r:r + 64, lanes:lanes + 128]

    loop(4, term2)

    def rs_start(buf, recv, sem0, step):
        copies = []
        for p, order in enumerate(ORDERS):
            base = 0
            for s in range(step):
                base = base + place[order[s]] * (16 >> (2 * s))
            size = 16 >> (2 * step)
            axis = order[step]
            for k in (1, 2, 3):
                to = lax.rem(place[axis] + k, 4)
                n = sem0 + (step * 3 + p) * 3 + k - 1
                copies.append(pltpu.make_async_remote_copy(
                    src_ref=buf.at[p, pl.ds(base + to * size, size)],
                    dst_ref=recv.at[p, k - 1],
                    send_sem=R.rs_send.at[n],
                    recv_sem=R.rs_recv.at[n],
                    device_id=along(axis, k),
                    device_id_type=MESH))
        for c in copies:
            c.start()
        return copies

    def rs_add(buf, recv, step, copies):
        wait(copies)
        size = 16 >> (2 * step)
        for p, order in enumerate(ORDERS):
            base = 0
            for s in range(step + 1):
                base = base + place[order[s]] * (16 >> (2 * s))

            step_of = min(size, 65536 // (buf.shape[2] * buf.shape[3]))

            def add(n):
                at = pl.ds(base + n * step_of, step_of)
                near = pl.ds(n * step_of, step_of)
                t = buf[p, at].astype(F32) + recv[p, 0, near].astype(F32)
                t = t + recv[p, 1, near].astype(F32) + recv[p, 2, near].astype(F32)
                buf[p, at] = t.astype(BF)

            loop(size // step_of, add)

    def region(order, step):
        base = 0
        for k in range(step):
            base = base + place[order[k]] * (16 >> (2 * k))
        return base, 16 >> (2 * step)

    def ring(buf, via, recv, step):
        out = []
        for p, order in enumerate(ORDERS):
            base, size = region(order, step)
            half = size // 2
            axis = order[step]
            up, opposite, down = [base + lax.rem(place[axis] + k, 4) * size for k in (1, 2, 3)]
            ends = along(axis, 1), along(axis, 3)
            moves = (
                (opposite, via.at[p, 0], 0), (opposite + half, via.at[p, 1], 1),
                (up + half, recv.at[p, 0, pl.ds(half, half)], 0), (down, recv.at[p, 1, pl.ds(0, half)], 1),
                (up, recv.at[p, 0, pl.ds(0, half)], 0), (down + half, recv.at[p, 1, pl.ds(half, half)], 1))
            out.append([pltpu.make_async_remote_copy(
                src_ref=buf.at[p, pl.ds(start, half)], dst_ref=target,
                send_sem=R.ring_send.at[(step * 3 + p) * 6 + n], recv_sem=R.ring_recv.at[(step * 3 + p) * 6 + n],
                device_id=ends[way], device_id_type=MESH) for n, (start, target, way) in enumerate(moves)])
        return out

    def ring_start(*what):
        copies = ring(*what)
        for pair in (slice(0, 2), slice(2, 4)):
            for part in copies:
                for c in part[pair]:
                    c.start()

    def ring_relay(buf, via, recv, step):
        copies = ring(buf, via, recv, step)
        for p, order in enumerate(ORDERS):
            base, size = region(order, step)
            half = size // 2
            up, down = [base + lax.rem(place[order[step]] + k, 4) * size for k in (1, 3)]
            for way, start in ((0, up), (1, down + half)):
                copies[p][way].wait_recv()
                at = pl.ds(start, half)
                buf[p, at] = (buf[p, at].astype(F32) + via[p, way].astype(F32)).astype(BF)
                copies[p][4 + way].start()

    def ring_finish(buf, via, recv, step):
        copies = ring(buf, via, recv, step)
        for p, order in enumerate(ORDERS):
            for n, c in enumerate(copies[p]):
                c.wait_send()
                if n >= 2:
                    c.wait_recv()
            base, size = region(order, step + 1)[0], region(order, step)[1]
            at = pl.ds(base, size)
            t = buf[p, at].astype(F32) + recv[p, 0].astype(F32) + recv[p, 1].astype(F32)
            buf[p, at] = t.astype(BF)

    def rs_last(buf, recv, p, copies):
        order = ORDERS[p]
        base = (place[order[0]] * 4 + place[order[1]]) * 4 + place[order[2]]
        t = buf[p, base].astype(F32) + recv[p, 0, 0].astype(F32)
        return t + recv[p, 1, 0].astype(F32) + recv[p, 2, 0].astype(F32)

    first_ring = (R.b2, R.b2v0, R.b2r0, 0)
    second_ring = (R.b2, R.b2v1, R.b2r1, 1)
    ring_start(*first_ring)

    loads.r3.wait()
    wait(halo2)
    R.g1[...] = nn(R.r1[...], R.xr[2]).astype(BF)
    loads.r4.start()

    def grad_mixed1(n):
        R.gm1[:, tile(n)] = nt(R.g1[...], R.p1[tile(n), :]).astype(BF)

    loop(2, grad_mixed1)

    def bwd1(pair):
        q2, k, v = four(pair)
        go = [stack(R.gm1[window(w), at(0, pair, 512)]) for w in range(4)]
        pb = [R.prob1[pair * 4 + w] for w in range(4)]
        back = attend_back(q2, k, v, [t.astype(F32) for t in pb], pb, go)
        for w in range(4):
            for part in range(3):
                R.dqkv1[window(w), at(part, pair, 512)] = back[part][w]
        if pair == 1:
            ring_relay(*first_ring)

    loop(4, bwd1)

    def to_core(t):
        return pltpu.make_async_remote_copy(
            src_ref=R.b1h.at[t, 1 - core], dst_ref=R.b1c.at[t], send_sem=R.core_send.at[2 + t],
            recv_sem=R.core_recv.at[2 + t], device_id=other, device_id_type=MESH)

    wide = []

    def term1(t):
        if t % 2 == 0:
            wide.append(nn(R.rolled1t[...], R.dqkv1[:, tile(t // 2, 768)]))
        g = wide[-1][:, t % 2 * 384:t % 2 * 384 + 384]
        pick = is_left[0:16]
        for zz in range(4):
            for hh in range(2):
                for cc in range(2):
                    r = ((zz * 2 + hh) * 2 + cc) * 32
                    upper = g[r:r + 16, 128:256]
                    lower = pltpu.roll(g[r + 16:r + 32, 128:256], 64, 1)
                    mixes = (jnp.where(pick, upper, lower), jnp.where(pick, lower, upper))
                    for odd in range(2):
                        lanes = slice(odd * 256, odd * 256 + 128)
                        pieces = (g[r:r + 16, lanes], g[r + 16:r + 32, lanes], mixes[odd])
                        for p in range(3):
                            R.b1h[t, cc, p, zz * 4 + hh * 2 + odd] = pieces[p].astype(BF)
        to_core(t).start()

    loop(4, term1)
    ring_finish(*first_ring)
    ring_start(*second_ring)

    for t in range(4):
        to_core(t).wait()
        for p, order in enumerate(ORDERS):
            g = R.b1h[t, core, p].astype(F32) + R.b1c[t, p].astype(F32)
            for n in range(16):
                at = dict(z=n // 4, x=n % 4, y=t)
                block = (at[order[0]] * 4 + at[order[1]]) * 4 + at[order[2]]
                R.b1[p, block] = g[n].astype(BF)
    mine = R.b1
    small = rs_start(mine, R.b1r0, 27, 0)
    ring_relay(*second_ring)

    def grad_rolled1(n):
        R.gm1[:, tile(n)] = nt(R.dqkv1[...], R.w1[tile(n), :]).astype(BF)

    def tail1(w):
        r = window(w)
        R.out1[r, :] = norm_back(R.gm1[r, :], R.hat1[r, :], R.inv1[r, :], gain1, R.g1[r, :])

    loop(2, grad_rolled1)
    loop(4, tail1)
    loads.s4.wait()
    R.xs[3] = nn(R.s1[336:, :], R.out1[...]).astype(BF)
    halo3 = exchange(3, SEG1, R.xs.at[3], R.xr.at[3], ahead)
    R.xr[3, 0:336] = nn(R.s1[0:336, :], R.out1[...]).astype(BF)

    branch = nn(R.mixed2[...], R.p2[...]).astype(BF).astype(F32)
    R.res[...] = (R.second[...].astype(F32) + branch).astype(BF)
    loads.sr.wait()
    R.cs[1] = nn(R.sr[48:, :], R.res[...]).astype(BF)
    halo_r = exchange(5, SEG2, R.cs.at[1], R.cr.at[1], ahead)
    R.cr[1, 0:48] = nn(R.sr[0:48, :], R.res[...]).astype(BF)

    rs_add(mine, R.b1r0, 0, small)
    small = rs_start(mine, R.b1r1, 27, 1)
    ring_finish(*second_ring)
    big = rs_start(R.b2, R.b2r2, 0, 2)
    wait(halo_r)
    loads.rr.wait()
    R.v_res[...] = nn(R.rr[...], R.cr[1]).astype(BF).reshape(72, 2, 1024)
    puts = [put(0, "res")]
    rs_add(mine, R.b1r1, 1, small)
    small = rs_start(mine, R.b1r2, 27, 2)
    loads.r4.wait()
    wait(halo3)
    R.v_tok[...] = jnp.where(present, nn(R.r1[...], R.xr[3]), 0.0).astype(BF)
    puts.append(put(1, "tok"))
    wait(big)
    for p in range(3):
        R.v_q2[:, p * 128:(p + 1) * 128] = rs_last(R.b2, R.b2r2, p, big)
    puts.append(put(3, "q2"))
    wait(small)
    a, b, m = [rs_last(mine, R.b1r2, p, small) for p in range(3)]
    turned = pltpu.roll(m, 64, 1)
    even = xl == 0
    a_turned = pltpu.roll(a, 64, 1)
    b_turned = pltpu.roll(b, 64, 1)
    pick = is_left[0:16]
    R.v_q1[0:16, 0:128] = jnp.where(even, a, jnp.where(pick, turned, a_turned))
    R.v_q1[16:32, 0:128] = jnp.where(even, b, jnp.where(pick, m, b_turned))
    R.v_q1[0:16, 128:192] = jnp.where(even, m, a_turned)[:, 0:64]
    R.v_q1[16:32, 128:192] = jnp.where(even, turned, b_turned)[:, 0:64]
    puts.append(put(2, "q1"))
    wait(puts)


def hand_on(*refs):
    given, out, held, sem = refs[0:4], refs[4:8], refs[8:12], refs[12]
    come = [pltpu.make_async_copy(given[n], held[n], sem.at[n]) for n in range(4)]
    leave = [pltpu.make_async_copy(held[n], out[n], sem.at[4 + n]) for n in range(4)]
    for c in come:
        c.start()
    for n in range(4):
        come[n].wait()
        leave[n].start()
    for c in leave:
        c.wait()


def shards(tokens, observed, mask_token, gain_one, qkv_one, table_one, proj_one, merge_weight, gain_two, qkv_two,
           table_two, proj_two, cotangent, sizes):
    first = tokens.transpose(0, 2, 1, 3).reshape(576, 512)
    cot = cotangent.transpose(1, 2, 0, 3).reshape(72, 2, 1024)
    seen = observed.transpose(2, 0, 1)
    given = dict(first=first, cot=cot, w1=qkv_one, p1=proj_one, wm=merge_weight, w2=qkv_two, p2=proj_two)
    for k, m in MATRICES.items():
        given[k] = jnp.asarray(m)
    args = [given[k] for k in LOADS]
    args += [seen, mask_token[None], table_one, table_two, gain_one[None], gain_two[None]]
    shapes = (
        jax.ShapeDtypeStruct((72, 2, 1024), BF),
        jax.ShapeDtypeStruct((576, 512), BF),
        jax.ShapeDtypeStruct((32, 192), F32),
        jax.ShapeDtypeStruct((64, 384), F32),
    )
    outs = pl.pallas_call(
        functools.partial(body, sizes),
        out_shape=shapes,
        in_specs=[pl.BlockSpec(memory_space=pl.ANY)] * len(LOADS) + [pl.BlockSpec(memory_space=pltpu.VMEM)] * len(SMALL),
        out_specs=[pl.BlockSpec(memory_space=pl.ANY)] * 4,
        scratch_shapes=list(SCRATCH.values()),
        compiler_params=pltpu.CompilerParams(
            collective_id=0, has_side_effects=True, vmem_limit_bytes=62 * 1024 * 1024),
        cost_estimate=pl.CostEstimate(flops=9 * 10 ** 9, bytes_accessed=24 * 10 ** 6, transcendentals=10 ** 6),
    )(*args)
    res, tok, q1, q2 = pl.pallas_call(
        hand_on,
        out_shape=shapes,
        in_specs=[pl.BlockSpec(memory_space=pl.ANY)] * 4,
        out_specs=[pl.BlockSpec(memory_space=pl.ANY)] * 4,
        scratch_shapes=[pltpu.VMEM(s.shape, s.dtype) for s in shapes] + [pltpu.SemaphoreType.DMA((8,))],
    )(*outs)
    result = res.reshape(12, 6, 2, 1024).transpose(2, 0, 1, 3)
    grad_tokens = tok.reshape(2, 12, 24, 512).transpose(0, 2, 1, 3)
    return (result, grad_tokens, q1, q2)


def solution(mesh):
    sizes = (mesh.shape["lon"], mesh.shape["lat"])
    split = P(None, "lon", "lat", None)

    def run(*args):
        return shards(*args, sizes)

    return jax.shard_map(
        run,
        mesh=mesh,
        in_specs=(split, P(None, "lon", "lat")) + (P(),) * 10 + (split,),
        out_specs=(split, split, P("lon", "lat"), P("lon", "lat")),
        check_vma=False,
    )
```

```python
import functools
from types import SimpleNamespace
import numpy as np
import jax
import jax.numpy as jnp
from jax import lax
from jax.experimental import pallas as pl
from jax.experimental.pallas import tpu as pltpu
from jax.sharding import PartitionSpec as P

BF = jnp.bfloat16
F32 = jnp.float32
EPS = 1e-05
NEG = -1000000000.0
MESH = pl.DeviceIdType.MESH
CELLS = 144
HALF = 72

SEG1 = ((0, 336), (336, 112), (448, 112), (560, 48))
SEG2 = ((0, 48), (48, 48), (96, 48), (144, 48))


def _cells(along, across, half_lon, half_lat):
    out = [[], [], [], []]
    for v in range(2):
        for i in range(along):
            for j in range(across):
                seg = (1 if i < half_lon else 0) + (2 if j < half_lat else 0)
                moved = (v, (i - half_lon) % along, (j - half_lat) % across)
                out[seg].append(((v, i, j), moved))
    return out


def _send_index(segs, cells, row_of):
    out = [-1] * (segs[-1][0] + segs[-1][1])
    for (start, _), members in zip(segs, cells):
        for n, (cell, _) in enumerate(members):
            out[start + n] = row_of(*cell)
    return out


def _recv_index(segs, cells, row_of, rows):
    out = [-1] * rows
    for (start, _), members in zip(segs, cells):
        for n, (_, moved) in enumerate(members):
            out[row_of(*moved)] = start + n
    return out


def _inverse(index, rows):
    out = [-1] * rows
    for n, m in enumerate(index):
        if m >= 0:
            out[m] = n
    return out


def _nat1(v, i, j):
    return (v * 12 + j) * 24 + i


def _win1(v, i, j):
    return ((i // 12) * 2 + j // 6) * CELLS + (j % 6) * 24 + v * 12 + i % 12


def _merge(v, i, j):
    return ((i % 2) * 2 + j % 2) * CELLS + (j // 2) * 24 + v * 12 + i // 2


def _nat2(v, i, j):
    return (i * 6 + j) * 2 + v


def _win2(v, i, j):
    return j * 24 + v * 12 + i


def _indices():
    one = _cells(24, 12, 6, 3)
    two = _cells(12, 6, 6, 3)
    s1 = _send_index(SEG1, one, _nat1)
    r1 = _recv_index(SEG1, one, _win1, 576)
    s2 = _send_index(SEG1, one, _win1)
    r2 = _recv_index(SEG1, one, _merge, 576)
    sc = _send_index(SEG2, two, _nat2)
    rc = _recv_index(SEG2, two, _win2, CELLS)
    flip = [-1] * 768
    for x in range(3):
        for y in range(23):
            for z in range(11):
                flip[(x * 23 + y) * 11 + z] = z * 69 + x * 23 + y
    pick = [-1] * 768
    for z in range(11):
        for v in range(2):
            for l in range(12):
                pick[z * 69 + v * 23 + l] = z * 24 + v * 12 + l
    return dict(s1=s1, r1=r1, s2=s2, r2=r2, s3=_inverse(r2, 608), r3=_inverse(s2, 576), s4=_inverse(r1, 608),
                r4=_inverse(s1, 576), sc=sc, rc=rc, sr=_inverse(rc, 192), rr=_inverse(sc, CELLS), flip=flip, pick=pick)


INDEX = _indices()
COLUMNS = dict(s1=576, r1=608, s2=576, r2=608, s3=576, r3=608, s4=576, r4=608, sc=CELLS, rc=192, sr=CELLS, rr=192,
               flip=768, pick=264)


def _matrix(key):
    index = np.asarray(INDEX[key])
    m = np.zeros((len(index), COLUMNS[key]), np.float32)
    rows = np.nonzero(index >= 0)[0]
    m[rows, index[rows]] = 1
    return m.astype(jnp.bfloat16)


MATRICES = {k: _matrix(k) for k in INDEX}

SHAPES = dict(first=(576, 512), s1=(608, 576), cot=(72, 2, 1024), sc=(192, CELLS), flip=(768, 768), pick=(768, 264),
              r1=(576, 608), w1=(512, 1536), p1=(512, 512), rc=(CELLS, 192), p2=(1024, 1024), wm=(2048, 1024),
              w2=(1024, 3072), sr=(192, CELLS), rr=(CELLS, 192), s2=(608, 576), r2=(576, 608), s3=(608, 576),
              r3=(576, 608), s4=(608, 576), r4=(576, 608))
LOADS = tuple(SHAPES)
LATER = dict(s2="s1", s3="s1", s4="s1", r2="r1", r3="r1", r4="r1")


def nn(a, b):
    return lax.dot_general(a, b, (((1,), (0,)), ((), ())), preferred_element_type=F32)


def nt(a, b):
    return lax.dot_general(a, b, (((1,), (1,)), ((), ())), preferred_element_type=F32)


def tn(a, b):
    return lax.dot_general(a, b, (((0,), (0,)), ((), ())), preferred_element_type=F32)


def norm_stats(x):
    centre = jnp.mean(x, axis=-1, keepdims=True)
    dev = x - centre
    spread = jnp.mean(dev * dev, axis=-1, keepdims=True)
    return dev, lax.rsqrt(spread + EPS)


def aligned(start, multiple):
    return start if isinstance(start, int) else pl.multiple_of(start, multiple)


def loop(n, body):
    for i in range(n):
        body(i)


SCRATCH = dict(
    {k: pltpu.VMEM(SHAPES[k], BF) for k in LOADS if k not in LATER},
    tables=pltpu.VMEM((24, 768), F32),
    shifted=pltpu.VMEM((1152, 768), F32),
    ext=pltpu.VMEM((24, 24, 264), F32),
    bias=pltpu.VMEM((12, CELLS, 288), F32),
    inv1=pltpu.VMEM((576, 1), F32),
    hat1=pltpu.VMEM((576, 512), F32),
    madd=pltpu.VMEM((CELLS, 288), F32),
    xr=pltpu.VMEM((4, 608, 512), BF),
    xs=pltpu.VMEM((4, 272, 512), BF),
    cr=pltpu.VMEM((2, 192, 1024), BF),
    cs=pltpu.VMEM((2, 144, 1024), BF),
    x1=pltpu.VMEM((576, 512), BF),
    rolled1=pltpu.VMEM((576, 512), BF),
    rolled1t=pltpu.VMEM((512, 576), BF),
    qkv1=pltpu.VMEM((576, 1536), BF),
    dqkv1=pltpu.VMEM((576, 1536), BF),
    prob1=pltpu.VMEM((16, CELLS, 288), BF),
    mixed1=pltpu.VMEM((576, 512), BF),
    out1=pltpu.VMEM((576, 512), BF),
    gm1=pltpu.VMEM((576, 512), BF),
    g1=pltpu.VMEM((576, 512), BF),
    merged=pltpu.VMEM((576, 512), BF),
    second=pltpu.VMEM((CELLS, 1024), BF),
    rolled2=pltpu.VMEM((CELLS, 1024), BF),
    qkv2=pltpu.VMEM((CELLS, 3072), BF),
    dqkv2=pltpu.VMEM((2, CELLS, 3072), BF),
    half2=pltpu.VMEM((2, CELLS, 512), BF),
    theirs2=pltpu.VMEM((CELLS, 512), BF),
    halft=pltpu.VMEM((2, 512, CELLS), BF),
    mixed2=pltpu.VMEM((CELLS, 1024), BF),
    ct=pltpu.VMEM((CELLS, 1024), BF),
    gm2=pltpu.VMEM((CELLS, 1024), BF),
    res=pltpu.VMEM((CELLS, 1024), BF),
    gs=pltpu.VMEM((CELLS, 1024), BF),
    v_res=pltpu.VMEM((72, 2, 1024), BF),
    v_tok=pltpu.VMEM((576, 512), BF),
    v_q1=pltpu.VMEM((32, 192), F32),
    v_q2=pltpu.VMEM((64, 384), F32),
    out_sem=pltpu.SemaphoreType.DMA((4,)),
    b2=pltpu.VMEM((3, 64, 64, 128), BF),
    b2v0=pltpu.VMEM((3, 2, 8, 64, 128), BF),
    b2r0=pltpu.VMEM((3, 2, 16, 64, 128), BF),
    b2v1=pltpu.VMEM((3, 2, 2, 64, 128), BF),
    b2r1=pltpu.VMEM((3, 2, 4, 64, 128), BF),
    b2r2=pltpu.VMEM((3, 3, 1, 64, 128), BF),
    b1=pltpu.VMEM((3, 64, 16, 128), BF),
    b1h=pltpu.VMEM((4, 2, 3, 16, 16, 128), BF),
    b1c=pltpu.VMEM((4, 3, 16, 16, 128), BF),
    b1r0=pltpu.VMEM((3, 3, 16, 16, 128), BF),
    b1r1=pltpu.VMEM((3, 3, 4, 16, 128), BF),
    b1r2=pltpu.VMEM((3, 3, 1, 16, 128), BF),
    load_sem=pltpu.SemaphoreType.DMA((len(LOADS),)),
    halo_send=pltpu.SemaphoreType.DMA((18,)),
    halo_recv=pltpu.SemaphoreType.DMA((18,)),
    rs_send=pltpu.SemaphoreType.DMA((54,)),
    rs_recv=pltpu.SemaphoreType.DMA((54,)),
    ring_send=pltpu.SemaphoreType.DMA((36,)),
    ring_recv=pltpu.SemaphoreType.DMA((36,)),
    core_send=pltpu.SemaphoreType.DMA((6,)),
    core_recv=pltpu.SemaphoreType.DMA((6,)),
)
SMALL = ("seen", "mask", "table1", "table2", "gain1", "gain2")
OUTPUTS = ("o_res", "o_tok", "o_q1", "o_q2")

ORDERS = (("z", "x", "y"), ("x", "y", "z"), ("y", "z", "x"))


def body(sizes, *refs):
    n_lon, n_lat = sizes
    names = ["in_" + n for n in LOADS + SMALL] + list(OUTPUTS) + list(SCRATCH)
    R = SimpleNamespace(**dict(zip(names, refs, strict=True)))

    e = lax.axis_index("lon")
    d = lax.axis_index("lat")
    core, xh, z = lax.rem(e, 2), lax.rem(e // 2, 2), e // 4
    xl, y = lax.rem(d, 2), d // 2
    x = xh * 2 + xl
    place = dict(x=x, y=y, z=z)
    e_up, e_dn = lax.rem(e + 1, n_lon), lax.rem(e + n_lon - 1, n_lon)
    d_up, d_dn = lax.rem(d + 1, n_lat), lax.rem(d + n_lat - 1, n_lat)
    last = d == n_lat - 1
    ahead = ((e_up, d), (e, d_up), (e_up, d_up))
    behind = ((e_dn, d), (e, d_dn), (e_dn, d_dn))
    other = (e + 1 - 2 * core, d)

    def device(x, y, z):
        return (z * 4 + (x // 2) * 2 + core, y * 2 + lax.rem(x, 2))

    def along(axis, k):
        at = dict(place)
        at[axis] = lax.rem(at[axis] + k, 4)
        return device(**at)

    loads = SimpleNamespace()
    for n, name in enumerate(LOADS):
        target = getattr(R, LATER.get(name, name))
        copy = pltpu.make_async_copy(getattr(R, "in_" + name), target, R.load_sem.at[n])
        if name not in LATER:
            copy.start()
        setattr(loads, name, copy)

    barrier = pltpu.get_barrier_semaphore()
    partners = list(ahead) + list(behind) + [other]
    for axis in place:
        for k in (1, 2, 3):
            partners.append(along(axis, k))
    for who in partners:
        pl.semaphore_signal(barrier, inc=1, device_id=who, device_id_type=MESH)

    def exchange(n, segs, source, target, to):
        copies = []
        for k in range(3):
            start, size = segs[k + 1]
            rows = pl.ds(start, size)
            copies.append(pltpu.make_async_remote_copy(
                src_ref=source.at[pl.ds(start - segs[0][1], size)],
                dst_ref=target.at[rows],
                send_sem=R.halo_send.at[3 * n + k],
                recv_sem=R.halo_recv.at[3 * n + k],
                device_id=to[k],
                device_id_type=MESH))
        for c in copies:
            c.start()
        return copies

    def wait(copies):
        for c in copies:
            c.wait()

    def put(n, name):
        copy = pltpu.make_async_copy(getattr(R, "v_" + name), getattr(R, "o_" + name), R.out_sem.at[n])
        copy.start()
        return copy

    seen = R.in_seen[...]
    seen = jnp.concatenate([seen[:, 0, :], seen[:, 1, :]], axis=0).astype(F32).astype(BF)
    row = lax.broadcasted_iota(jnp.int32, (576, 24), 0)
    col = lax.broadcasted_iota(jnp.int32, (576, 24), 1)
    per = nn(jnp.where(row // 24 == col, 1.0, 0.0).astype(BF), seen)
    present = jnp.sum(jnp.where(lax.rem(row, 24) == col, per, 0.0), axis=-1, keepdims=True) > 0.5

    loads.first.wait()
    R.first[...] = jnp.where(present, R.first[...].astype(F32), R.in_mask[...].astype(BF).astype(F32)).astype(BF)
    loads.s1.wait()
    R.xs[0] = nn(R.s1[336:, :], R.first[...]).astype(BF)

    pl.semaphore_wait(barrier, len(partners))
    halo0 = exchange(0, SEG1, R.xs.at[0], R.xr.at[0], behind)
    R.xr[0, 0:336] = nn(R.s1[0:336, :], R.first[...]).astype(BF)
    loads.s2.start()
    loads.sc.wait()
    loads.cot.wait()
    cot = R.cot[...].reshape(CELLS, 1024)
    R.cs[0] = nn(R.sc[48:, :], cot).astype(BF)
    halo_c = exchange(4, SEG2, R.cs.at[0], R.cr.at[0], behind)
    R.cr[0, 0:48] = nn(R.sc[0:48, :], cot).astype(BF)

    R.tables[...] = jnp.zeros((24, 768), F32)
    R.tables[0:8, 0:759] = R.in_table1[...]
    R.tables[8:24, 0:759] = R.in_table2[...]
    table = R.tables[...]
    high = table.astype(BF).astype(F32)
    mid = (table - high).astype(BF).astype(F32)
    low = table - high - mid
    parts = jnp.concatenate([high, mid, low], axis=0).astype(BF)
    loads.flip.wait()
    parts = nn(parts, R.flip[...])
    loads.pick.wait()
    picked = R.pick[...]

    def extend(first, heads):
        part = jnp.concatenate([parts[24 * k + first:24 * k + first + heads] for k in range(3)], axis=0)
        for v in range(2):
            for l in range(12):
                shift = (1 - v) * 23 + 11 - l
                moved = pltpu.roll(part, (768 - shift) % 768, 1) if shift else part
                at = (v * 12 + l) * 3 * heads
                R.shifted[at:at + 3 * heads] = moved
        got = nn(R.shifted[0:72 * heads].astype(BF), picked)
        for n in range(24):
            at = n * 3 * heads
            R.ext[first:first + heads, n, :] = (
                got[at:at + heads] + got[at + heads:at + 2 * heads] + got[at + 2 * heads:at + 3 * heads])

    extend(0, 8)
    rows = lax.broadcasted_iota(jnp.int32, (CELLS, CELLS), 0)
    cols = lax.broadcasted_iota(jnp.int32, (CELLS, CELLS), 1)
    apart = jnp.where(jnp.logical_xor(rows < HALF, cols < HALF), NEG, 0.0).astype(F32)
    apart = apart * jnp.where(last, 1.0, 0.0).astype(F32)
    R.madd[...] = jnp.concatenate([apart, apart], axis=1)

    def expand(pair):
        one, two = R.ext[2 * pair], R.ext[2 * pair + 1]
        for a in range(6):
            at = slice((5 - a) * 24, (5 - a) * 24 + CELLS)
            R.bias[pair, a * 24:(a + 1) * 24, :] = jnp.concatenate([one[:, at], two[:, at]], axis=1)

    def expand_masked(pair):
        expand(4 + pair)
        R.bias[4 + pair] = R.bias[4 + pair] + R.madd[...]

    loop(4, expand)

    lane = lax.broadcasted_iota(jnp.int32, (1, 128), 1)
    left = jnp.where(lane < 64, 1.0, 0.0).astype(BF)
    right = jnp.where(lane < 64, 0.0, 1.0).astype(BF)
    is_left = lax.broadcasted_iota(jnp.int32, (CELLS, 128), 1) < 64

    def stack(t):
        return jnp.concatenate([t * left, t * right], axis=0)

    def at(part, pair, width):
        return pl.ds(aligned(part * width + pair * 128, 128), 128)

    def heads_of(t):
        return jnp.where(is_left, t[:CELLS], t[CELLS:])

    def attend(q2, k, v, bias):
        score = [nt(b, a) + c for a, b, c in zip(q2, k, bias)]
        expo = [jnp.exp(t - jnp.max(t, axis=0, keepdims=True)) for t in score]
        p = [t * (1.0 / jnp.sum(t, axis=0, keepdims=True)) for t in expo]
        pb = [t.astype(BF) for t in p]
        o = [heads_of(tn(a, b)).astype(BF) for a, b in zip(pb, v)]
        return p, pb, o

    def attend_back(q2, k, v, p, pb, go):
        gw = [nt(a, b) for a, b in zip(v, go)]
        gs = [(a * (b - jnp.sum(a * b, axis=0, keepdims=True))).astype(BF) for a, b in zip(p, gw)]
        gv = [nn(a, b).astype(BF) for a, b in zip(pb, go)]
        gk = [nn(a, b).astype(BF) for a, b in zip(gs, q2)]
        gq = [(heads_of(tn(a, b)) * 0.125).astype(BF) for a, b in zip(gs, k)]
        return gq, gk, gv

    gain1 = R.in_gain1[...]

    def window(w):
        return pl.ds(aligned(w * CELLS, 16), CELLS)

    def tile(n, size=256):
        return pl.ds(aligned(n * size, size), size)

    def span(first, last):
        return slice(first * CELLS, last * CELLS)

    def norm1(w):
        rows = span(w, w + 1)
        dev, inv = norm_stats(R.x1[rows, :].astype(F32))
        R.inv1[rows, :] = inv
        R.hat1[rows, :] = dev * inv
        R.rolled1[rows, :] = (dev * inv * gain1).astype(BF)

    def qkv1(first, last):
        rows = span(first, last)
        for n in range(6):
            R.qkv1[rows, tile(n)] = nn(R.rolled1[rows, :], R.w1[:, tile(n)]).astype(BF)

    def units(which):
        q2 = [stack(R.qkv1[window(w), at(0, pair, 512)] * BF(0.125)) for pair, w in which]
        k = [R.qkv1[window(w), at(1, pair, 512)] for pair, w in which]
        v = [R.qkv1[window(w), at(2, pair, 512)] for pair, w in which]
        return q2, k, v

    def fwd1(which):
        bias = [R.bias[pair] + R.madd[...] if w % 2 else R.bias[pair] for pair, w in which]
        _, pb, o = attend(*units(which), bias)
        for n, (pair, w) in enumerate(which):
            R.prob1[pair * 4 + w] = pb[n]
            R.mixed1[window(w), at(0, pair, 512)] = o[n]

    def proj1(first, last):
        rows = span(first, last)
        for n in range(2):
            branch = nn(R.mixed1[rows, :], R.p1[:, tile(n)]).astype(BF).astype(F32)
            R.out1[rows, tile(n)] = (R.x1[rows, tile(n)].astype(F32) + branch).astype(BF)

    loads.r1.wait()
    R.x1[0:CELLS, :] = nn(R.r1[0:CELLS, 0:336], R.xr[0, 0:336, :]).astype(BF)
    norm1(0)
    loads.w1.wait()
    qkv1(0, 1)
    fwd1([(pair, 0) for pair in range(4)])
    wait(halo0)
    R.x1[span(1, 4), :] = nn(R.r1[span(1, 4), :], R.xr[0]).astype(BF)
    loads.r2.start()
    for w in (1, 2, 3):
        norm1(w)
    qkv1(1, 4)
    fwd1([(0, 1), (0, 2), (1, 1), (1, 2)])
    fwd1([(2, 1), (2, 2), (3, 1), (3, 2)])
    loads.p1.wait()
    proj1(0, 3)
    R.out1[span(3, 4), :] = jnp.zeros((CELLS, 512), BF)

    loads.s2.wait()
    R.xs[1] = nn(R.s1[336:, :], R.out1[...]).astype(BF)
    halo1 = exchange(1, SEG1, R.xs.at[1], R.xr.at[1], behind)
    fwd1([(pair, 3) for pair in range(4)])
    proj1(3, 4)
    R.xr[1, 0:336] = nn(R.s1[0:336, :], R.out1[...]).astype(BF)
    loads.s3.start()
    extend(8, 16)
    loop(8, expand_masked)
    wait(halo_c)
    loads.rc.wait()
    R.ct[...] = nn(R.rc[...], R.cr[0]).astype(BF)
    loads.p2.wait()

    def grad_mixed2(n):
        c = pl.ds(aligned(n * 256, 256), 256)
        R.gm2[:, c] = nt(R.ct[...], R.p2[c, :]).astype(BF)

    loop(4, grad_mixed2)
    R.rolled1t[...] = R.rolled1[...].T
    loads.r2.wait()
    wait(halo1)
    R.merged[...] = nn(R.r1[...], R.xr[1]).astype(BF)
    loads.r3.start()
    loads.wm.wait()
    acc = nn(R.merged[0:CELLS, :], R.wm[0:512, :])
    for s in range(1, 4):
        acc = acc + nn(R.merged[s * CELLS:(s + 1) * CELLS, :], R.wm[s * 512:(s + 1) * 512, :])
    second = acc.astype(BF)
    R.second[...] = second
    gain2 = R.in_gain2[...]
    dev2, inv2 = norm_stats(second.astype(F32))
    hat2 = dev2 * inv2
    rolled2 = (hat2 * gain2).astype(BF)
    R.rolled2[...] = rolled2
    loads.w2.wait()

    def qkv2(n):
        c = pl.ds(aligned(n * 512, 512), 512)
        R.qkv2[:, c] = nn(R.rolled2[...], R.w2[:, c]).astype(BF)

    loop(6, qkv2)

    r2f = rolled2.astype(F32)
    for t in range(4):
        a = r2f[:, t * 256:t * 256 + 128]
        b = r2f[:, t * 256 + 128:t * 256 + 256]
        c = slice(t * 128, t * 128 + 128)
        R.half2[0, :, c] = jnp.where(is_left, a, pltpu.roll(b, 64, 1)).astype(BF)
        R.half2[1, :, c] = jnp.where(is_left, pltpu.roll(a, 64, 1), b).astype(BF)
    core0 = pltpu.make_async_remote_copy(
        src_ref=R.half2.at[1 - core], dst_ref=R.theirs2, send_sem=R.core_send.at[0],
        recv_sem=R.core_recv.at[0], device_id=other, device_id_type=MESH)
    core0.start()

    def both2(u):
        pairs = [u * 4 + n for n in range(4)]
        q2 = [stack(R.qkv2[:, at(0, c, 1024)] * BF(0.125)) for c in pairs]
        k = [R.qkv2[:, at(1, c, 1024)] for c in pairs]
        v = [R.qkv2[:, at(2, c, 1024)] for c in pairs]
        go = [stack(R.gm2[:, at(0, c, 1024)]) for c in pairs]
        p, pb, o = attend(q2, k, v, [R.bias[4 + c] for c in pairs])
        back = attend_back(q2, k, v, p, pb, go)
        for n, c in enumerate(pairs):
            R.mixed2[:, at(0, c, 1024)] = o[n]
            for part in range(3):
                R.dqkv2[0, :, at(part, c, 1024)] = back[part][n]

    loop(2, both2)
    core1 = pltpu.make_async_remote_copy(
        src_ref=R.dqkv2.at[0], dst_ref=R.dqkv2.at[1], send_sem=R.core_send.at[1],
        recv_sem=R.core_recv.at[1], device_id=other, device_id_type=MESH)
    core1.start()

    grad_rolled = nt(R.dqkv2[0, :, 0:1024], R.w2[:, 0:1024])
    grad_rolled = grad_rolled + nt(R.dqkv2[0, :, 1024:2048], R.w2[:, 1024:2048])
    grad_rolled = grad_rolled + nt(R.dqkv2[0, :, 2048:3072], R.w2[:, 2048:3072])

    def norm_back(grad, hat, inv, gain, grad_out):
        grad = grad.astype(BF).astype(F32) * gain
        inner = inv * (grad - jnp.mean(grad, axis=-1, keepdims=True)
                       - hat * jnp.mean(grad * hat, axis=-1, keepdims=True))
        return (grad_out.astype(F32) + inner.astype(BF).astype(F32)).astype(BF)

    R.gs[...] = norm_back(grad_rolled, hat2, inv2, gain2, R.ct[...])
    for s in range(4):
        R.merged[s * CELLS:(s + 1) * CELLS, :] = nt(R.gs[...], R.wm[s * 512:(s + 1) * 512, :]).astype(BF)
    loads.s3.wait()
    R.xs[2] = nn(R.s1[336:, :], R.merged[...]).astype(BF)
    halo2 = exchange(2, SEG1, R.xs.at[2], R.xr.at[2], ahead)
    R.xr[2, 0:336] = nn(R.s1[0:336, :], R.merged[...]).astype(BF)
    loads.s4.start()

    R.halft[0] = R.half2[core].T
    core0.wait()
    R.halft[1] = R.theirs2[...].T
    core1.wait()

    def term2(yy):
        c = tile(yy, 768)
        g = nn(R.halft[0], R.dqkv2[0, :, c]) + nn(R.halft[1], R.dqkv2[1, :, c])
        g = g.astype(BF)
        for zz in range(4):
            for hh in range(2):
                r = (zz * 2 + hh) * 64
                for xx in range(2):
                    at = dict(z=zz, x=hh * 2 + xx, y=yy)
                    for p, order in enumerate(ORDERS):
                        block = (at[order[0]] * 4 + at[order[1]]) * 4 + at[order[2]]
                        lanes = xx * 384 + p * 128
                        R.b2[p, block] = g[r:r + 64, lanes:lanes + 128]

    loop(4, term2)

    def rs_start(buf, recv, sem0, step):
        copies = []
        for p, order in enumerate(ORDERS):
            base = 0
            for s in range(step):
                base = base + place[order[s]] * (16 >> (2 * s))
            size = 16 >> (2 * step)
            axis = order[step]
            for k in (1, 2, 3):
                to = lax.rem(place[axis] + k, 4)
                n = sem0 + (step * 3 + p) * 3 + k - 1
                copies.append(pltpu.make_async_remote_copy(
                    src_ref=buf.at[p, pl.ds(base + to * size, size)],
                    dst_ref=recv.at[p, k - 1],
                    send_sem=R.rs_send.at[n],
                    recv_sem=R.rs_recv.at[n],
                    device_id=along(axis, k),
                    device_id_type=MESH))
        for c in copies:
            c.start()
        return copies

    def rs_add(buf, recv, step, copies):
        wait(copies)
        size = 16 >> (2 * step)
        for p, order in enumerate(ORDERS):
            base = 0
            for s in range(step + 1):
                base = base + place[order[s]] * (16 >> (2 * s))

            step_of = min(size, 65536 // (buf.shape[2] * buf.shape[3]))

            def add(n):
                at = pl.ds(base + n * step_of, step_of)
                near = pl.ds(n * step_of, step_of)
                t = buf[p, at].astype(F32) + recv[p, 0, near].astype(F32)
                t = t + recv[p, 1, near].astype(F32) + recv[p, 2, near].astype(F32)
                buf[p, at] = t.astype(BF)

            loop(size // step_of, add)

    def region(order, step):
        base = 0
        for k in range(step):
            base = base + place[order[k]] * (16 >> (2 * k))
        return base, 16 >> (2 * step)

    def ring(buf, via, recv, step):
        out = []
        for p, order in enumerate(ORDERS):
            base, size = region(order, step)
            half = size // 2
            axis = order[step]
            up, opposite, down = [base + lax.rem(place[axis] + k, 4) * size for k in (1, 2, 3)]
            ends = along(axis, 1), along(axis, 3)
            moves = (
                (opposite, via.at[p, 0], 0), (opposite + half, via.at[p, 1], 1),
                (up + half, recv.at[p, 0, pl.ds(half, half)], 0), (down, recv.at[p, 1, pl.ds(0, half)], 1),
                (up, recv.at[p, 0, pl.ds(0, half)], 0), (down + half, recv.at[p, 1, pl.ds(half, half)], 1))
            out.append([pltpu.make_async_remote_copy(
                src_ref=buf.at[p, pl.ds(start, half)], dst_ref=target,
                send_sem=R.ring_send.at[(step * 3 + p) * 6 + n], recv_sem=R.ring_recv.at[(step * 3 + p) * 6 + n],
                device_id=ends[way], device_id_type=MESH) for n, (start, target, way) in enumerate(moves)])
        return out

    def ring_start(*what):
        copies = ring(*what)
        for pair in (slice(0, 2), slice(2, 4)):
            for part in copies:
                for c in part[pair]:
                    c.start()

    def ring_relay(buf, via, recv, step):
        copies = ring(buf, via, recv, step)
        for p, order in enumerate(ORDERS):
            base, size = region(order, step)
            half = size // 2
            up, down = [base + lax.rem(place[order[step]] + k, 4) * size for k in (1, 3)]
            for way, start in ((0, up), (1, down + half)):
                copies[p][way].wait_recv()
                at = pl.ds(start, half)
                buf[p, at] = (buf[p, at].astype(F32) + via[p, way].astype(F32)).astype(BF)
                copies[p][4 + way].start()

    def ring_finish(buf, via, recv, step):
        copies = ring(buf, via, recv, step)
        for p, order in enumerate(ORDERS):
            for n, c in enumerate(copies[p]):
                c.wait_send()
                if n >= 2:
                    c.wait_recv()
            base, size = region(order, step + 1)[0], region(order, step)[1]
            at = pl.ds(base, size)
            t = buf[p, at].astype(F32) + recv[p, 0].astype(F32) + recv[p, 1].astype(F32)
            buf[p, at] = t.astype(BF)

    def rs_last(buf, recv, p, copies):
        order = ORDERS[p]
        base = (place[order[0]] * 4 + place[order[1]]) * 4 + place[order[2]]
        t = buf[p, base].astype(F32) + recv[p, 0, 0].astype(F32)
        return t + recv[p, 1, 0].astype(F32) + recv[p, 2, 0].astype(F32)

    first_ring = (R.b2, R.b2v0, R.b2r0, 0)
    second_ring = (R.b2, R.b2v1, R.b2r1, 1)
    ring_start(*first_ring)

    def back1(which):
        q2, k, v = units(which)
        go = [stack(R.gm1[window(w), at(0, pair, 512)]) for pair, w in which]
        pb = [R.prob1[pair * 4 + w] for pair, w in which]
        back = attend_back(q2, k, v, [t.astype(F32) for t in pb], pb, go)
        for n, (pair, w) in enumerate(which):
            for part in range(3):
                R.dqkv1[window(w), at(part, pair, 512)] = back[part][n]

    loads.r3.wait()
    R.g1[span(3, 4), :] = nn(R.r1[span(3, 4), 0:336], R.xr[2, 0:336, :]).astype(BF)
    R.gm1[span(3, 4), :] = nt(R.g1[span(3, 4), :], R.p1[...]).astype(BF)
    back1([(pair, 3) for pair in range(4)])
    wait(halo2)
    R.g1[span(0, 3), :] = nn(R.r1[span(0, 3), :], R.xr[2]).astype(BF)
    loads.r4.start()
    for n in range(2):
        R.gm1[span(0, 3), tile(n)] = nt(R.g1[span(0, 3), :], R.p1[tile(n), :]).astype(BF)
    for pair in range(4):
        back1([(pair, w) for w in range(3)])
        if pair == 1:
            ring_relay(*first_ring)

    def to_core(t):
        return pltpu.make_async_remote_copy(
            src_ref=R.b1h.at[t, 1 - core], dst_ref=R.b1c.at[t], send_sem=R.core_send.at[2 + t],
            recv_sem=R.core_recv.at[2 + t], device_id=other, device_id_type=MESH)

    wide = []

    def term1(t):
        if t % 2 == 0:
            wide.append(nn(R.rolled1t[...], R.dqkv1[:, tile(t // 2, 768)]))
        g = wide[-1][:, t % 2 * 384:t % 2 * 384 + 384]
        pick = is_left[0:16]
        for zz in range(4):
            for hh in range(2):
                for cc in range(2):
                    r = ((zz * 2 + hh) * 2 + cc) * 32
                    upper = g[r:r + 16, 128:256]
                    lower = pltpu.roll(g[r + 16:r + 32, 128:256], 64, 1)
                    mixes = (jnp.where(pick, upper, lower), jnp.where(pick, lower, upper))
                    for odd in range(2):
                        lanes = slice(odd * 256, odd * 256 + 128)
                        pieces = (g[r:r + 16, lanes], g[r + 16:r + 32, lanes], mixes[odd])
                        for p in range(3):
                            R.b1h[t, cc, p, zz * 4 + hh * 2 + odd] = pieces[p].astype(BF)
        to_core(t).start()

    loop(4, term1)
    ring_finish(*first_ring)
    ring_start(*second_ring)

    for t in range(4):
        to_core(t).wait()
        for p, order in enumerate(ORDERS):
            g = R.b1h[t, core, p].astype(F32) + R.b1c[t, p].astype(F32)
            for n in range(16):
                at = dict(z=n // 4, x=n % 4, y=t)
                block = (at[order[0]] * 4 + at[order[1]]) * 4 + at[order[2]]
                R.b1[p, block] = g[n].astype(BF)
    mine = R.b1
    small = rs_start(mine, R.b1r0, 27, 0)
    ring_relay(*second_ring)

    def grad_rolled1(n):
        R.gm1[:, tile(n)] = nt(R.dqkv1[...], R.w1[tile(n), :]).astype(BF)

    def tail1(w):
        r = window(w)
        R.out1[r, :] = norm_back(R.gm1[r, :], R.hat1[r, :], R.inv1[r, :], gain1, R.g1[r, :])

    loop(2, grad_rolled1)
    loop(4, tail1)
    loads.s4.wait()
    R.xs[3] = nn(R.s1[336:, :], R.out1[...]).astype(BF)
    halo3 = exchange(3, SEG1, R.xs.at[3], R.xr.at[3], ahead)
    R.xr[3, 0:336] = nn(R.s1[0:336, :], R.out1[...]).astype(BF)

    branch = nn(R.mixed2[...], R.p2[...]).astype(BF).astype(F32)
    R.res[...] = (R.second[...].astype(F32) + branch).astype(BF)
    loads.sr.wait()
    R.cs[1] = nn(R.sr[48:, :], R.res[...]).astype(BF)
    halo_r = exchange(5, SEG2, R.cs.at[1], R.cr.at[1], ahead)
    R.cr[1, 0:48] = nn(R.sr[0:48, :], R.res[...]).astype(BF)

    rs_add(mine, R.b1r0, 0, small)
    small = rs_start(mine, R.b1r1, 27, 1)
    ring_finish(*second_ring)
    big = rs_start(R.b2, R.b2r2, 0, 2)
    wait(halo_r)
    loads.rr.wait()
    R.v_res[...] = nn(R.rr[...], R.cr[1]).astype(BF).reshape(72, 2, 1024)
    puts = [put(0, "res")]
    rs_add(mine, R.b1r1, 1, small)
    small = rs_start(mine, R.b1r2, 27, 2)
    loads.r4.wait()
    wait(halo3)
    R.v_tok[...] = jnp.where(present, nn(R.r1[...], R.xr[3]), 0.0).astype(BF)
    puts.append(put(1, "tok"))
    wait(big)
    for p in range(3):
        R.v_q2[:, p * 128:(p + 1) * 128] = rs_last(R.b2, R.b2r2, p, big)
    puts.append(put(3, "q2"))
    wait(small)
    a, b, m = [rs_last(mine, R.b1r2, p, small) for p in range(3)]
    turned = pltpu.roll(m, 64, 1)
    even = xl == 0
    a_turned = pltpu.roll(a, 64, 1)
    b_turned = pltpu.roll(b, 64, 1)
    pick = is_left[0:16]
    R.v_q1[0:16, 0:128] = jnp.where(even, a, jnp.where(pick, turned, a_turned))
    R.v_q1[16:32, 0:128] = jnp.where(even, b, jnp.where(pick, m, b_turned))
    R.v_q1[0:16, 128:192] = jnp.where(even, m, a_turned)[:, 0:64]
    R.v_q1[16:32, 128:192] = jnp.where(even, turned, b_turned)[:, 0:64]
    puts.append(put(2, "q1"))
    wait(puts)


def hand_on(*refs):
    given, out, held, sem = refs[0:4], refs[4:8], refs[8:12], refs[12]
    come = [pltpu.make_async_copy(given[n], held[n], sem.at[n]) for n in range(4)]
    leave = [pltpu.make_async_copy(held[n], out[n], sem.at[4 + n]) for n in range(4)]
    for c in come:
        c.start()
    for n in range(4):
        come[n].wait()
        leave[n].start()
    for c in leave:
        c.wait()


def shards(tokens, observed, mask_token, gain_one, qkv_one, table_one, proj_one, merge_weight, gain_two, qkv_two,
           table_two, proj_two, cotangent, sizes):
    first = tokens.transpose(0, 2, 1, 3).reshape(576, 512)
    cot = cotangent.transpose(1, 2, 0, 3).reshape(72, 2, 1024)
    seen = observed.transpose(2, 0, 1)
    given = dict(first=first, cot=cot, w1=qkv_one, p1=proj_one, wm=merge_weight, w2=qkv_two, p2=proj_two)
    for k, m in MATRICES.items():
        given[k] = jnp.asarray(m)
    args = [given[k] for k in LOADS]
    args += [seen, mask_token[None], table_one, table_two, gain_one[None], gain_two[None]]
    shapes = (
        jax.ShapeDtypeStruct((72, 2, 1024), BF),
        jax.ShapeDtypeStruct((576, 512), BF),
        jax.ShapeDtypeStruct((32, 192), F32),
        jax.ShapeDtypeStruct((64, 384), F32),
    )
    outs = pl.pallas_call(
        functools.partial(body, sizes),
        out_shape=shapes,
        in_specs=[pl.BlockSpec(memory_space=pl.ANY)] * len(LOADS) + [pl.BlockSpec(memory_space=pltpu.VMEM)] * len(SMALL),
        out_specs=[pl.BlockSpec(memory_space=pl.ANY)] * 4,
        scratch_shapes=list(SCRATCH.values()),
        compiler_params=pltpu.CompilerParams(
            collective_id=0, has_side_effects=True, vmem_limit_bytes=62 * 1024 * 1024),
        cost_estimate=pl.CostEstimate(flops=9 * 10 ** 9, bytes_accessed=24 * 10 ** 6, transcendentals=10 ** 6),
    )(*args)
    res, tok, q1, q2 = pl.pallas_call(
        hand_on,
        out_shape=shapes,
        in_specs=[pl.BlockSpec(memory_space=pl.ANY)] * 4,
        out_specs=[pl.BlockSpec(memory_space=pl.ANY)] * 4,
        scratch_shapes=[pltpu.VMEM(s.shape, s.dtype) for s in shapes] + [pltpu.SemaphoreType.DMA((8,))],
    )(*outs)
    result = res.reshape(12, 6, 2, 1024).transpose(2, 0, 1, 3)
    grad_tokens = tok.reshape(2, 12, 24, 512).transpose(0, 2, 1, 3)
    return (result, grad_tokens, q1, q2)


def solution(mesh):
    sizes = (mesh.shape["lon"], mesh.shape["lat"])
    split = P(None, "lon", "lat", None)

    def run(*args):
        return shards(*args, sizes)

    return jax.shard_map(
        run,
        mesh=mesh,
        in_specs=(split, P(None, "lon", "lat")) + (P(),) * 10 + (split,),
        out_specs=(split, split, P("lon", "lat"), P("lon", "lat")),
        check_vma=False,
    )
```

```python
import functools
from types import SimpleNamespace
import numpy as np
import jax
import jax.numpy as jnp
from jax import lax
from jax.experimental import pallas as pl
from jax.experimental.pallas import tpu as pltpu
from jax.sharding import PartitionSpec as P

BF = jnp.bfloat16
F32 = jnp.float32
EPS = 1e-05
NEG = -1000000000.0
MESH = pl.DeviceIdType.MESH
CELLS = 144
HALF = 72

SEG1 = ((0, 336), (336, 112), (448, 112), (560, 48))
SEG2 = ((0, 48), (48, 48), (96, 48), (144, 48))


def _cells(along, across, half_lon, half_lat):
    out = [[], [], [], []]
    for v in range(2):
        for i in range(along):
            for j in range(across):
                seg = (1 if i < half_lon else 0) + (2 if j < half_lat else 0)
                moved = (v, (i - half_lon) % along, (j - half_lat) % across)
                out[seg].append(((v, i, j), moved))
    return out


def _send_index(segs, cells, row_of):
    out = [-1] * (segs[-1][0] + segs[-1][1])
    for (start, _), members in zip(segs, cells):
        for n, (cell, _) in enumerate(members):
            out[start + n] = row_of(*cell)
    return out


def _recv_index(segs, cells, row_of, rows):
    out = [-1] * rows
    for (start, _), members in zip(segs, cells):
        for n, (_, moved) in enumerate(members):
            out[row_of(*moved)] = start + n
    return out


def _inverse(index, rows):
    out = [-1] * rows
    for n, m in enumerate(index):
        if m >= 0:
            out[m] = n
    return out


def _nat1(v, i, j):
    return (v * 12 + j) * 24 + i


def _win1(v, i, j):
    return ((i // 12) * 2 + j // 6) * CELLS + (j % 6) * 24 + v * 12 + i % 12


def _merge(v, i, j):
    return ((i % 2) * 2 + j % 2) * CELLS + (j // 2) * 24 + v * 12 + i // 2


def _nat2(v, i, j):
    return (i * 6 + j) * 2 + v


def _win2(v, i, j):
    return j * 24 + v * 12 + i


def _indices():
    one = _cells(24, 12, 6, 3)
    two = _cells(12, 6, 6, 3)
    s1 = _send_index(SEG1, one, _nat1)
    r1 = _recv_index(SEG1, one, _win1, 576)
    s2 = _send_index(SEG1, one, _win1)
    r2 = _recv_index(SEG1, one, _merge, 576)
    sc = _send_index(SEG2, two, _nat2)
    rc = _recv_index(SEG2, two, _win2, CELLS)
    flip = [-1] * 768
    for x in range(3):
        for y in range(23):
            for z in range(11):
                flip[(x * 23 + y) * 11 + z] = z * 69 + x * 23 + y
    pick = [-1] * 768
    for z in range(11):
        for v in range(2):
            for l in range(12):
                pick[z * 69 + v * 23 + l] = z * 24 + v * 12 + l
    return dict(s1=s1, r1=r1, s2=s2, r2=r2, s3=_inverse(r2, 608), r3=_inverse(s2, 576), s4=_inverse(r1, 608),
                r4=_inverse(s1, 576), sc=sc, rc=rc, sr=_inverse(rc, 192), rr=_inverse(sc, CELLS), flip=flip, pick=pick)


INDEX = _indices()
COLUMNS = dict(s1=576, r1=608, s2=576, r2=608, s3=576, r3=608, s4=576, r4=608, sc=CELLS, rc=192, sr=CELLS, rr=192,
               flip=768, pick=264)


def _matrix(key):
    index = np.asarray(INDEX[key])
    m = np.zeros((len(index), COLUMNS[key]), np.float32)
    rows = np.nonzero(index >= 0)[0]
    m[rows, index[rows]] = 1
    return m.astype(jnp.bfloat16)


MATRICES = {k: _matrix(k) for k in INDEX}

SHAPES = dict(first=(576, 512), s1=(608, 576), cot=(72, 2, 1024), sc=(192, CELLS), flip=(768, 768), pick=(768, 264),
              r1=(576, 608), w1=(512, 1536), p1=(512, 512), rc=(CELLS, 192), p2=(1024, 1024), wm=(2048, 1024),
              w2=(1024, 3072), sr=(192, CELLS), rr=(CELLS, 192), s2=(608, 576), r2=(576, 608), s3=(608, 576),
              r3=(576, 608), s4=(608, 576), r4=(576, 608))
LOADS = tuple(SHAPES)
LATER = dict(s2="s1", s3="s1", s4="s1", r2="r1", r3="r1", r4="r1")


def nn(a, b):
    return lax.dot_general(a, b, (((1,), (0,)), ((), ())), preferred_element_type=F32)


def nt(a, b):
    return lax.dot_general(a, b, (((1,), (1,)), ((), ())), preferred_element_type=F32)


def tn(a, b):
    return lax.dot_general(a, b, (((0,), (0,)), ((), ())), preferred_element_type=F32)


def norm_stats(x):
    centre = jnp.mean(x, axis=-1, keepdims=True)
    dev = x - centre
    spread = jnp.mean(dev * dev, axis=-1, keepdims=True)
    return dev, lax.rsqrt(spread + EPS)


def aligned(start, multiple):
    return start if isinstance(start, int) else pl.multiple_of(start, multiple)


def loop(n, body):
    for i in range(n):
        body(i)


SCRATCH = dict(
    {k: pltpu.VMEM(SHAPES[k], BF) for k in LOADS if k not in LATER},
    tables=pltpu.VMEM((24, 768), F32),
    shifted=pltpu.VMEM((1152, 768), F32),
    ext=pltpu.VMEM((24, 24, 264), F32),
    bias=pltpu.VMEM((12, CELLS, 288), F32),
    inv1=pltpu.VMEM((576, 1), F32),
    hat1=pltpu.VMEM((576, 512), F32),
    madd=pltpu.VMEM((CELLS, 288), F32),
    xr=pltpu.VMEM((4, 608, 512), BF),
    xs=pltpu.VMEM((4, 272, 512), BF),
    cr=pltpu.VMEM((2, 192, 1024), BF),
    cs=pltpu.VMEM((2, 144, 1024), BF),
    x1=pltpu.VMEM((576, 512), BF),
    rolled1=pltpu.VMEM((576, 512), BF),
    rolled1t=pltpu.VMEM((512, 576), BF),
    qkv1=pltpu.VMEM((576, 1536), BF),
    dqkv1=pltpu.VMEM((576, 1536), BF),
    prob1=pltpu.VMEM((16, CELLS, 288), BF),
    mixed1=pltpu.VMEM((576, 512), BF),
    out1=pltpu.VMEM((576, 512), BF),
    gm1=pltpu.VMEM((576, 512), BF),
    g1=pltpu.VMEM((576, 512), BF),
    merged=pltpu.VMEM((576, 512), BF),
    second=pltpu.VMEM((CELLS, 1024), BF),
    rolled2=pltpu.VMEM((CELLS, 1024), BF),
    qkv2=pltpu.VMEM((CELLS, 3072), BF),
    dqkv2=pltpu.VMEM((2, CELLS, 3072), BF),
    half2=pltpu.VMEM((2, CELLS, 512), BF),
    theirs2=pltpu.VMEM((CELLS, 512), BF),
    halft=pltpu.VMEM((2, 512, CELLS), BF),
    mixed2=pltpu.VMEM((CELLS, 1024), BF),
    ct=pltpu.VMEM((CELLS, 1024), BF),
    gm2=pltpu.VMEM((CELLS, 1024), BF),
    res=pltpu.VMEM((CELLS, 1024), BF),
    gs=pltpu.VMEM((CELLS, 1024), BF),
    v_res=pltpu.VMEM((72, 2, 1024), BF),
    v_tok=pltpu.VMEM((576, 512), BF),
    v_q1=pltpu.VMEM((32, 192), F32),
    v_q2=pltpu.VMEM((64, 384), F32),
    out_sem=pltpu.SemaphoreType.DMA((4,)),
    b2=pltpu.VMEM((3, 64, 64, 128), BF),
    b2v0=pltpu.VMEM((3, 2, 8, 64, 128), BF),
    b2r0=pltpu.VMEM((3, 2, 16, 64, 128), BF),
    b2v1=pltpu.VMEM((3, 2, 2, 64, 128), BF),
    b2r1=pltpu.VMEM((3, 2, 4, 64, 128), BF),
    b2r2=pltpu.VMEM((3, 3, 1, 64, 128), BF),
    b1=pltpu.VMEM((3, 64, 16, 128), BF),
    b1h=pltpu.VMEM((4, 2, 3, 16, 16, 128), BF),
    b1c=pltpu.VMEM((4, 3, 16, 16, 128), BF),
    b1r0=pltpu.VMEM((3, 3, 16, 16, 128), BF),
    b1r1=pltpu.VMEM((3, 3, 4, 16, 128), BF),
    b1r2=pltpu.VMEM((3, 3, 1, 16, 128), BF),
    load_sem=pltpu.SemaphoreType.DMA((len(LOADS),)),
    halo_send=pltpu.SemaphoreType.DMA((18,)),
    halo_recv=pltpu.SemaphoreType.DMA((18,)),
    rs_send=pltpu.SemaphoreType.DMA((54,)),
    rs_recv=pltpu.SemaphoreType.DMA((54,)),
    ring_send=pltpu.SemaphoreType.DMA((36,)),
    ring_recv=pltpu.SemaphoreType.DMA((36,)),
    core_send=pltpu.SemaphoreType.DMA((6,)),
    core_recv=pltpu.SemaphoreType.DMA((6,)),
)
SMALL = ("seen", "mask", "table1", "table2", "gain1", "gain2")
OUTPUTS = ("o_res", "o_tok", "o_q1", "o_q2")

ORDERS = (("z", "x", "y"), ("x", "y", "z"), ("y", "z", "x"))


def body(sizes, *refs):
    n_lon, n_lat = sizes
    names = ["in_" + n for n in LOADS + SMALL] + list(OUTPUTS) + list(SCRATCH)
    R = SimpleNamespace(**dict(zip(names, refs, strict=True)))

    e = lax.axis_index("lon")
    d = lax.axis_index("lat")
    core, xh, z = lax.rem(e, 2), lax.rem(e // 2, 2), e // 4
    xl, y = lax.rem(d, 2), d // 2
    x = xh * 2 + xl
    place = dict(x=x, y=y, z=z)
    e_up, e_dn = lax.rem(e + 1, n_lon), lax.rem(e + n_lon - 1, n_lon)
    d_up, d_dn = lax.rem(d + 1, n_lat), lax.rem(d + n_lat - 1, n_lat)
    last = d == n_lat - 1
    ahead = ((e_up, d), (e, d_up), (e_up, d_up))
    behind = ((e_dn, d), (e, d_dn), (e_dn, d_dn))
    other = (e + 1 - 2 * core, d)

    def device(x, y, z):
        return (z * 4 + (x // 2) * 2 + core, y * 2 + lax.rem(x, 2))

    def along(axis, k):
        at = dict(place)
        at[axis] = lax.rem(at[axis] + k, 4)
        return device(**at)

    loads = SimpleNamespace()
    for n, name in enumerate(LOADS):
        target = getattr(R, LATER.get(name, name))
        copy = pltpu.make_async_copy(getattr(R, "in_" + name), target, R.load_sem.at[n])
        if name not in LATER:
            copy.start()
        setattr(loads, name, copy)

    barrier = pltpu.get_barrier_semaphore()
    partners = list(ahead) + list(behind) + [other]
    for axis in place:
        for k in (1, 2, 3):
            partners.append(along(axis, k))
    for who in partners:
        pl.semaphore_signal(barrier, inc=1, device_id=who, device_id_type=MESH)

    def exchange(n, segs, source, target, to):
        copies = []
        for k in range(3):
            start, size = segs[k + 1]
            rows = pl.ds(start, size)
            copies.append(pltpu.make_async_remote_copy(
                src_ref=source.at[pl.ds(start - segs[0][1], size)],
                dst_ref=target.at[rows],
                send_sem=R.halo_send.at[3 * n + k],
                recv_sem=R.halo_recv.at[3 * n + k],
                device_id=to[k],
                device_id_type=MESH))
        for c in copies:
            c.start()
        return copies

    def wait(copies):
        for c in copies:
            c.wait()

    def put(n, name):
        copy = pltpu.make_async_copy(getattr(R, "v_" + name), getattr(R, "o_" + name), R.out_sem.at[n])
        copy.start()
        return copy

    seen = R.in_seen[...]
    seen = jnp.concatenate([seen[:, 0, :], seen[:, 1, :]], axis=0).astype(F32).astype(BF)
    row = lax.broadcasted_iota(jnp.int32, (576, 24), 0)
    col = lax.broadcasted_iota(jnp.int32, (576, 24), 1)
    per = nn(jnp.where(row // 24 == col, 1.0, 0.0).astype(BF), seen)
    present = jnp.sum(jnp.where(lax.rem(row, 24) == col, per, 0.0), axis=-1, keepdims=True) > 0.5

    loads.first.wait()
    R.first[...] = jnp.where(present, R.first[...].astype(F32), R.in_mask[...].astype(BF).astype(F32)).astype(BF)
    loads.s1.wait()
    R.xs[0] = nn(R.s1[336:, :], R.first[...]).astype(BF)

    pl.semaphore_wait(barrier, len(partners))
    halo0 = exchange(0, SEG1, R.xs.at[0], R.xr.at[0], behind)
    R.xr[0, 0:336] = nn(R.s1[0:336, :], R.first[...]).astype(BF)
    loads.s2.start()
    loads.sc.wait()
    loads.cot.wait()
    cot = R.cot[...].reshape(CELLS, 1024)
    R.cs[0] = nn(R.sc[48:, :], cot).astype(BF)
    halo_c = exchange(4, SEG2, R.cs.at[0], R.cr.at[0], behind)
    R.cr[0, 0:48] = nn(R.sc[0:48, :], cot).astype(BF)

    R.tables[...] = jnp.zeros((24, 768), F32)
    R.tables[0:8, 0:759] = R.in_table1[...]
    R.tables[8:24, 0:759] = R.in_table2[...]
    table = R.tables[...]
    high = table.astype(BF).astype(F32)
    mid = (table - high).astype(BF).astype(F32)
    low = table - high - mid
    parts = jnp.concatenate([high, mid, low], axis=0).astype(BF)
    loads.flip.wait()
    parts = nn(parts, R.flip[...])
    loads.pick.wait()
    picked = R.pick[...]

    def extend(first, heads):
        part = jnp.concatenate([parts[24 * k + first:24 * k + first + heads] for k in range(3)], axis=0)
        for v in range(2):
            for l in range(12):
                shift = (1 - v) * 23 + 11 - l
                moved = pltpu.roll(part, (768 - shift) % 768, 1) if shift else part
                at = (v * 12 + l) * 3 * heads
                R.shifted[at:at + 3 * heads] = moved
        got = nn(R.shifted[0:72 * heads].astype(BF), picked)
        for n in range(24):
            at = n * 3 * heads
            R.ext[first:first + heads, n, :] = (
                got[at:at + heads] + got[at + heads:at + 2 * heads] + got[at + 2 * heads:at + 3 * heads])

    extend(0, 8)
    rows = lax.broadcasted_iota(jnp.int32, (CELLS, CELLS), 0)
    cols = lax.broadcasted_iota(jnp.int32, (CELLS, CELLS), 1)
    apart = jnp.where(jnp.logical_xor(rows < HALF, cols < HALF), NEG, 0.0).astype(F32)
    apart = apart * jnp.where(last, 1.0, 0.0).astype(F32)
    R.madd[...] = jnp.concatenate([apart, apart], axis=1)

    def expand(pair):
        one, two = R.ext[2 * pair], R.ext[2 * pair + 1]
        for a in range(6):
            at = slice((5 - a) * 24, (5 - a) * 24 + CELLS)
            R.bias[pair, a * 24:(a + 1) * 24, :] = jnp.concatenate([one[:, at], two[:, at]], axis=1)

    def expand_masked(pair):
        expand(4 + pair)
        R.bias[4 + pair] = R.bias[4 + pair] + R.madd[...]

    loop(4, expand)

    lane = lax.broadcasted_iota(jnp.int32, (1, 128), 1)
    left = jnp.where(lane < 64, 1.0, 0.0).astype(BF)
    right = jnp.where(lane < 64, 0.0, 1.0).astype(BF)
    is_left = lax.broadcasted_iota(jnp.int32, (CELLS, 128), 1) < 64

    def stack(t):
        return jnp.concatenate([t * left, t * right], axis=0)

    def at(part, pair, width):
        return pl.ds(aligned(part * width + pair * 128, 128), 128)

    def heads_of(t):
        return jnp.where(is_left, t[:CELLS], t[CELLS:])

    def attend(q2, k, v, bias):
        score = [nt(b, a) + c for a, b, c in zip(q2, k, bias)]
        expo = [jnp.exp(t - jnp.max(t, axis=0, keepdims=True)) for t in score]
        p = [t * (1.0 / jnp.sum(t, axis=0, keepdims=True)) for t in expo]
        pb = [t.astype(BF) for t in p]
        o = [heads_of(tn(a, b)).astype(BF) for a, b in zip(pb, v)]
        return p, pb, o

    def attend_back(q2, k, v, p, pb, go):
        gw = [nt(a, b) for a, b in zip(v, go)]
        gs = [(a * (b - jnp.sum(a * b, axis=0, keepdims=True))).astype(BF) for a, b in zip(p, gw)]
        gv = [nn(a, b).astype(BF) for a, b in zip(pb, go)]
        gk = [nn(a, b).astype(BF) for a, b in zip(gs, q2)]
        gq = [(heads_of(tn(a, b)) * 0.125).astype(BF) for a, b in zip(gs, k)]
        return gq, gk, gv

    gain1 = R.in_gain1[...]

    def window(w):
        return pl.ds(aligned(w * CELLS, 16), CELLS)

    def tile(n, size=256):
        return pl.ds(aligned(n * size, size), size)

    def span(first, last):
        return slice(first * CELLS, last * CELLS)

    def norm1(w):
        rows = span(w, w + 1)
        dev, inv = norm_stats(R.x1[rows, :].astype(F32))
        R.inv1[rows, :] = inv
        R.hat1[rows, :] = dev * inv
        R.rolled1[rows, :] = (dev * inv * gain1).astype(BF)

    def qkv1(first, last):
        rows = span(first, last)
        for n in range(6):
            R.qkv1[rows, tile(n)] = nn(R.rolled1[rows, :], R.w1[:, tile(n)]).astype(BF)

    def units(which):
        q2 = [stack(R.qkv1[window(w), at(0, pair, 512)] * BF(0.125)) for pair, w in which]
        k = [R.qkv1[window(w), at(1, pair, 512)] for pair, w in which]
        v = [R.qkv1[window(w), at(2, pair, 512)] for pair, w in which]
        return q2, k, v

    def fwd1(which):
        bias = [R.bias[pair] + R.madd[...] if w % 2 else R.bias[pair] for pair, w in which]
        _, pb, o = attend(*units(which), bias)
        for n, (pair, w) in enumerate(which):
            R.prob1[pair * 4 + w] = pb[n]
            R.mixed1[window(w), at(0, pair, 512)] = o[n]

    def proj1(first, last):
        rows = span(first, last)
        for n in range(2):
            branch = nn(R.mixed1[rows, :], R.p1[:, tile(n)]).astype(BF).astype(F32)
            R.out1[rows, tile(n)] = (R.x1[rows, tile(n)].astype(F32) + branch).astype(BF)

    loads.r1.wait()
    R.x1[0:CELLS, :] = nn(R.r1[0:CELLS, 0:336], R.xr[0, 0:336, :]).astype(BF)
    norm1(0)
    loads.w1.wait()
    qkv1(0, 1)
    fwd1([(pair, 0) for pair in range(4)])
    wait(halo0)
    R.x1[span(1, 4), :] = nn(R.r1[span(1, 4), :], R.xr[0]).astype(BF)
    loads.r2.start()
    for w in (1, 2, 3):
        norm1(w)
    qkv1(1, 4)
    fwd1([(0, 1), (0, 2), (1, 1), (1, 2)])
    fwd1([(2, 1), (2, 2), (3, 1), (3, 2)])
    loads.p1.wait()
    proj1(0, 3)
    R.out1[span(3, 4), :] = jnp.zeros((CELLS, 512), BF)

    loads.s2.wait()
    R.xs[1] = nn(R.s1[336:, :], R.out1[...]).astype(BF)
    halo1 = exchange(1, SEG1, R.xs.at[1], R.xr.at[1], behind)
    fwd1([(pair, 3) for pair in range(4)])
    proj1(3, 4)
    R.xr[1, 0:336] = nn(R.s1[0:336, :], R.out1[...]).astype(BF)
    loads.s3.start()
    extend(8, 16)
    loop(8, expand_masked)
    wait(halo_c)
    loads.rc.wait()
    R.ct[...] = nn(R.rc[...], R.cr[0]).astype(BF)
    loads.p2.wait()

    def grad_mixed2(n):
        c = pl.ds(aligned(n * 256, 256), 256)
        R.gm2[:, c] = nt(R.ct[...], R.p2[c, :]).astype(BF)

    loop(4, grad_mixed2)
    R.rolled1t[...] = R.rolled1[...].T
    loads.r2.wait()
    wait(halo1)
    R.merged[...] = nn(R.r1[...], R.xr[1]).astype(BF)
    loads.r3.start()
    loads.wm.wait()
    acc = nn(R.merged[0:CELLS, :], R.wm[0:512, :])
    for s in range(1, 4):
        acc = acc + nn(R.merged[s * CELLS:(s + 1) * CELLS, :], R.wm[s * 512:(s + 1) * 512, :])
    second = acc.astype(BF)
    R.second[...] = second
    gain2 = R.in_gain2[...]
    dev2, inv2 = norm_stats(second.astype(F32))
    hat2 = dev2 * inv2
    rolled2 = (hat2 * gain2).astype(BF)
    R.rolled2[...] = rolled2
    loads.w2.wait()

    def qkv2(n):
        c = pl.ds(aligned(n * 512, 512), 512)
        R.qkv2[:, c] = nn(R.rolled2[...], R.w2[:, c]).astype(BF)

    loop(6, qkv2)

    r2f = rolled2.astype(F32)
    for t in range(4):
        a = r2f[:, t * 256:t * 256 + 128]
        b = r2f[:, t * 256 + 128:t * 256 + 256]
        c = slice(t * 128, t * 128 + 128)
        R.half2[0, :, c] = jnp.where(is_left, a, pltpu.roll(b, 64, 1)).astype(BF)
        R.half2[1, :, c] = jnp.where(is_left, pltpu.roll(a, 64, 1), b).astype(BF)
    core0 = pltpu.make_async_remote_copy(
        src_ref=R.half2.at[1 - core], dst_ref=R.theirs2, send_sem=R.core_send.at[0],
        recv_sem=R.core_recv.at[0], device_id=other, device_id_type=MESH)
    core0.start()

    def both2(u):
        pairs = [u * 4 + n for n in range(4)]
        q2 = [stack(R.qkv2[:, at(0, c, 1024)] * BF(0.125)) for c in pairs]
        k = [R.qkv2[:, at(1, c, 1024)] for c in pairs]
        v = [R.qkv2[:, at(2, c, 1024)] for c in pairs]
        go = [stack(R.gm2[:, at(0, c, 1024)]) for c in pairs]
        p, pb, o = attend(q2, k, v, [R.bias[4 + c] for c in pairs])
        back = attend_back(q2, k, v, p, pb, go)
        for n, c in enumerate(pairs):
            R.mixed2[:, at(0, c, 1024)] = o[n]
            for part in range(3):
                R.dqkv2[0, :, at(part, c, 1024)] = back[part][n]

    loop(2, both2)
    core1 = pltpu.make_async_remote_copy(
        src_ref=R.dqkv2.at[0], dst_ref=R.dqkv2.at[1], send_sem=R.core_send.at[1],
        recv_sem=R.core_recv.at[1], device_id=other, device_id_type=MESH)
    core1.start()

    grad_rolled = nt(R.dqkv2[0, :, 0:1024], R.w2[:, 0:1024])
    grad_rolled = grad_rolled + nt(R.dqkv2[0, :, 1024:2048], R.w2[:, 1024:2048])
    grad_rolled = grad_rolled + nt(R.dqkv2[0, :, 2048:3072], R.w2[:, 2048:3072])

    def norm_back(grad, hat, inv, gain, grad_out):
        grad = grad.astype(BF).astype(F32) * gain
        inner = inv * (grad - jnp.mean(grad, axis=-1, keepdims=True)
                       - hat * jnp.mean(grad * hat, axis=-1, keepdims=True))
        return (grad_out.astype(F32) + inner.astype(BF).astype(F32)).astype(BF)

    R.gs[...] = norm_back(grad_rolled, hat2, inv2, gain2, R.ct[...])
    for s in range(4):
        R.merged[s * CELLS:(s + 1) * CELLS, :] = nt(R.gs[...], R.wm[s * 512:(s + 1) * 512, :]).astype(BF)
    loads.s3.wait()
    R.xs[2] = nn(R.s1[336:, :], R.merged[...]).astype(BF)
    halo2 = exchange(2, SEG1, R.xs.at[2], R.xr.at[2], ahead)
    R.xr[2, 0:336] = nn(R.s1[0:336, :], R.merged[...]).astype(BF)
    loads.s4.start()

    R.halft[0] = R.half2[core].T
    core0.wait()
    R.halft[1] = R.theirs2[...].T
    core1.wait()

    def term2(yy):
        c = tile(yy, 768)
        g = nn(R.halft[0], R.dqkv2[0, :, c]) + nn(R.halft[1], R.dqkv2[1, :, c])
        g = g.astype(BF)
        for zz in range(4):
            for hh in range(2):
                r = (zz * 2 + hh) * 64
                for xx in range(2):
                    at = dict(z=zz, x=hh * 2 + xx, y=yy)
                    for p, order in enumerate(ORDERS):
                        block = (at[order[0]] * 4 + at[order[1]]) * 4 + at[order[2]]
                        lanes = xx * 384 + p * 128
                        R.b2[p, block] = g[r:r + 64, lanes:lanes + 128]

    loop(4, term2)

    def rs_start(buf, recv, sem0, step):
        copies = []
        for p, order in enumerate(ORDERS):
            base = 0
            for s in range(step):
                base = base + place[order[s]] * (16 >> (2 * s))
            size = 16 >> (2 * step)
            axis = order[step]
            for k in (1, 2, 3):
                to = lax.rem(place[axis] + k, 4)
                n = sem0 + (step * 3 + p) * 3 + k - 1
                copies.append(pltpu.make_async_remote_copy(
                    src_ref=buf.at[p, pl.ds(base + to * size, size)],
                    dst_ref=recv.at[p, k - 1],
                    send_sem=R.rs_send.at[n],
                    recv_sem=R.rs_recv.at[n],
                    device_id=along(axis, k),
                    device_id_type=MESH))
        for c in copies:
            c.start()
        return copies

    def rs_add(buf, recv, step, copies):
        wait(copies)
        size = 16 >> (2 * step)
        for p, order in enumerate(ORDERS):
            base = 0
            for s in range(step + 1):
                base = base + place[order[s]] * (16 >> (2 * s))

            step_of = min(size, 65536 // (buf.shape[2] * buf.shape[3]))

            def add(n):
                at = pl.ds(base + n * step_of, step_of)
                near = pl.ds(n * step_of, step_of)
                t = buf[p, at].astype(F32) + recv[p, 0, near].astype(F32)
                t = t + recv[p, 1, near].astype(F32) + recv[p, 2, near].astype(F32)
                buf[p, at] = t.astype(BF)

            loop(size // step_of, add)

    def region(order, step):
        base = 0
        for k in range(step):
            base = base + place[order[k]] * (16 >> (2 * k))
        return base, 16 >> (2 * step)

    def ring(buf, via, recv, step):
        out = []
        for p, order in enumerate(ORDERS):
            base, size = region(order, step)
            half = size // 2
            axis = order[step]
            up, opposite, down = [base + lax.rem(place[axis] + k, 4) * size for k in (1, 2, 3)]
            ends = along(axis, 1), along(axis, 3)
            moves = (
                (opposite, via.at[p, 0], 0), (opposite + half, via.at[p, 1], 1),
                (up + half, recv.at[p, 0, pl.ds(half, half)], 0), (down, recv.at[p, 1, pl.ds(0, half)], 1),
                (up, recv.at[p, 0, pl.ds(0, half)], 0), (down + half, recv.at[p, 1, pl.ds(half, half)], 1))
            out.append([pltpu.make_async_remote_copy(
                src_ref=buf.at[p, pl.ds(start, half)], dst_ref=target,
                send_sem=R.ring_send.at[(step * 3 + p) * 6 + n], recv_sem=R.ring_recv.at[(step * 3 + p) * 6 + n],
                device_id=ends[way], device_id_type=MESH) for n, (start, target, way) in enumerate(moves)])
        return out

    def ring_start(*what):
        copies = ring(*what)
        for pair in (slice(0, 2), slice(2, 4)):
            for part in copies:
                for c in part[pair]:
                    c.start()

    def ring_relay(buf, via, recv, step):
        copies = ring(buf, via, recv, step)
        for p, order in enumerate(ORDERS):
            base, size = region(order, step)
            half = size // 2
            up, down = [base + lax.rem(place[order[step]] + k, 4) * size for k in (1, 3)]
            for way, start in ((0, up), (1, down + half)):
                copies[p][way].wait_recv()
                at = pl.ds(start, half)
                buf[p, at] = (buf[p, at].astype(F32) + via[p, way].astype(F32)).astype(BF)
                copies[p][4 + way].start()

    def ring_finish(buf, via, recv, step):
        copies = ring(buf, via, recv, step)
        for p, order in enumerate(ORDERS):
            for n, c in enumerate(copies[p]):
                c.wait_send()
                if n >= 2:
                    c.wait_recv()
            base, size = region(order, step + 1)[0], region(order, step)[1]
            at = pl.ds(base, size)
            t = buf[p, at].astype(F32) + recv[p, 0].astype(F32) + recv[p, 1].astype(F32)
            buf[p, at] = t.astype(BF)

    def rs_last(buf, recv, p, copies):
        order = ORDERS[p]
        base = (place[order[0]] * 4 + place[order[1]]) * 4 + place[order[2]]
        t = buf[p, base].astype(F32) + recv[p, 0, 0].astype(F32)
        return t + recv[p, 1, 0].astype(F32) + recv[p, 2, 0].astype(F32)

    first_ring = (R.b2, R.b2v0, R.b2r0, 0)
    second_ring = (R.b2, R.b2v1, R.b2r1, 1)
    ring_start(*first_ring)

    def back1(which):
        q2, k, v = units(which)
        go = [stack(R.gm1[window(w), at(0, pair, 512)]) for pair, w in which]
        pb = [R.prob1[pair * 4 + w] for pair, w in which]
        back = attend_back(q2, k, v, [t.astype(F32) for t in pb], pb, go)
        for n, (pair, w) in enumerate(which):
            for part in range(3):
                R.dqkv1[window(w), at(part, pair, 512)] = back[part][n]

    loads.r3.wait()
    R.g1[span(3, 4), :] = nn(R.r1[span(3, 4), 0:336], R.xr[2, 0:336, :]).astype(BF)
    R.gm1[span(3, 4), :] = nt(R.g1[span(3, 4), :], R.p1[...]).astype(BF)
    back1([(pair, 3) for pair in range(4)])
    wait(halo2)
    R.g1[span(0, 3), :] = nn(R.r1[span(0, 3), :], R.xr[2]).astype(BF)
    loads.r4.start()
    for n in range(2):
        R.gm1[span(0, 3), tile(n)] = nt(R.g1[span(0, 3), :], R.p1[tile(n), :]).astype(BF)
    for pair in range(4):
        back1([(pair, w) for w in range(3)])
        if pair == 1:
            ring_relay(*first_ring)

    def to_core(t):
        return pltpu.make_async_remote_copy(
            src_ref=R.b1h.at[t, 1 - core], dst_ref=R.b1c.at[t], send_sem=R.core_send.at[2 + t],
            recv_sem=R.core_recv.at[2 + t], device_id=other, device_id_type=MESH)

    wide = []

    def term1(t):
        if t % 2 == 0:
            wide.append(nn(R.rolled1t[...], R.dqkv1[:, tile(t // 2, 768)]))
        g = wide[-1][:, t % 2 * 384:t % 2 * 384 + 384]
        pick = is_left[0:16]
        for zz in range(4):
            for hh in range(2):
                for cc in range(2):
                    r = ((zz * 2 + hh) * 2 + cc) * 32
                    upper = g[r:r + 16, 128:256]
                    lower = pltpu.roll(g[r + 16:r + 32, 128:256], 64, 1)
                    mixes = (jnp.where(pick, upper, lower), jnp.where(pick, lower, upper))
                    for odd in range(2):
                        lanes = slice(odd * 256, odd * 256 + 128)
                        pieces = (g[r:r + 16, lanes], g[r + 16:r + 32, lanes], mixes[odd])
                        for p in range(3):
                            R.b1h[t, cc, p, zz * 4 + hh * 2 + odd] = pieces[p].astype(BF)
        to_core(t).start()

    loop(4, term1)

    for t in range(4):
        to_core(t).wait()
        for p, order in enumerate(ORDERS):
            g = R.b1h[t, core, p].astype(F32) + R.b1c[t, p].astype(F32)
            for n in range(16):
                at = dict(z=n // 4, x=n % 4, y=t)
                block = (at[order[0]] * 4 + at[order[1]]) * 4 + at[order[2]]
                R.b1[p, block] = g[n].astype(BF)
    mine = R.b1
    small = rs_start(mine, R.b1r0, 27, 0)
    ring_finish(*first_ring)
    ring_start(*second_ring)

    def grad_rolled1(n):
        R.gm1[:, tile(n)] = nt(R.dqkv1[...], R.w1[tile(n), :]).astype(BF)

    def tail1(w):
        r = window(w)
        R.out1[r, :] = norm_back(R.gm1[r, :], R.hat1[r, :], R.inv1[r, :], gain1, R.g1[r, :])

    loop(2, grad_rolled1)
    loop(4, tail1)
    loads.s4.wait()
    R.xs[3] = nn(R.s1[336:, :], R.out1[...]).astype(BF)
    halo3 = exchange(3, SEG1, R.xs.at[3], R.xr.at[3], ahead)
    R.xr[3, 0:336] = nn(R.s1[0:336, :], R.out1[...]).astype(BF)

    ring_relay(*second_ring)

    branch = nn(R.mixed2[...], R.p2[...]).astype(BF).astype(F32)
    R.res[...] = (R.second[...].astype(F32) + branch).astype(BF)
    loads.sr.wait()
    R.cs[1] = nn(R.sr[48:, :], R.res[...]).astype(BF)
    halo_r = exchange(5, SEG2, R.cs.at[1], R.cr.at[1], ahead)
    R.cr[1, 0:48] = nn(R.sr[0:48, :], R.res[...]).astype(BF)

    rs_add(mine, R.b1r0, 0, small)
    small = rs_start(mine, R.b1r1, 27, 1)
    ring_finish(*second_ring)
    big = rs_start(R.b2, R.b2r2, 0, 2)
    wait(halo_r)
    loads.rr.wait()
    R.v_res[...] = nn(R.rr[...], R.cr[1]).astype(BF).reshape(72, 2, 1024)
    puts = [put(0, "res")]
    rs_add(mine, R.b1r1, 1, small)
    small = rs_start(mine, R.b1r2, 27, 2)
    loads.r4.wait()
    wait(halo3)
    R.v_tok[...] = jnp.where(present, nn(R.r1[...], R.xr[3]), 0.0).astype(BF)
    puts.append(put(1, "tok"))
    wait(big)
    for p in range(3):
        R.v_q2[:, p * 128:(p + 1) * 128] = rs_last(R.b2, R.b2r2, p, big)
    puts.append(put(3, "q2"))
    wait(small)
    a, b, m = [rs_last(mine, R.b1r2, p, small) for p in range(3)]
    turned = pltpu.roll(m, 64, 1)
    even = xl == 0
    a_turned = pltpu.roll(a, 64, 1)
    b_turned = pltpu.roll(b, 64, 1)
    pick = is_left[0:16]
    R.v_q1[0:16, 0:128] = jnp.where(even, a, jnp.where(pick, turned, a_turned))
    R.v_q1[16:32, 0:128] = jnp.where(even, b, jnp.where(pick, m, b_turned))
    R.v_q1[0:16, 128:192] = jnp.where(even, m, a_turned)[:, 0:64]
    R.v_q1[16:32, 128:192] = jnp.where(even, turned, b_turned)[:, 0:64]
    puts.append(put(2, "q1"))
    wait(puts)


def hand_on(*refs):
    given, out, held, sem = refs[0:4], refs[4:8], refs[8:12], refs[12]
    come = [pltpu.make_async_copy(given[n], held[n], sem.at[n]) for n in range(4)]
    leave = [pltpu.make_async_copy(held[n], out[n], sem.at[4 + n]) for n in range(4)]
    for c in come:
        c.start()
    for n in range(4):
        come[n].wait()
        leave[n].start()
    for c in leave:
        c.wait()


def shards(tokens, observed, mask_token, gain_one, qkv_one, table_one, proj_one, merge_weight, gain_two, qkv_two,
           table_two, proj_two, cotangent, sizes):
    first = tokens.transpose(0, 2, 1, 3).reshape(576, 512)
    cot = cotangent.transpose(1, 2, 0, 3).reshape(72, 2, 1024)
    seen = observed.transpose(2, 0, 1)
    given = dict(first=first, cot=cot, w1=qkv_one, p1=proj_one, wm=merge_weight, w2=qkv_two, p2=proj_two)
    for k, m in MATRICES.items():
        given[k] = jnp.asarray(m)
    args = [given[k] for k in LOADS]
    args += [seen, mask_token[None], table_one, table_two, gain_one[None], gain_two[None]]
    shapes = (
        jax.ShapeDtypeStruct((72, 2, 1024), BF),
        jax.ShapeDtypeStruct((576, 512), BF),
        jax.ShapeDtypeStruct((32, 192), F32),
        jax.ShapeDtypeStruct((64, 384), F32),
    )
    outs = pl.pallas_call(
        functools.partial(body, sizes),
        out_shape=shapes,
        in_specs=[pl.BlockSpec(memory_space=pl.ANY)] * len(LOADS) + [pl.BlockSpec(memory_space=pltpu.VMEM)] * len(SMALL),
        out_specs=[pl.BlockSpec(memory_space=pl.ANY)] * 4,
        scratch_shapes=list(SCRATCH.values()),
        compiler_params=pltpu.CompilerParams(
            collective_id=0, has_side_effects=True, vmem_limit_bytes=62 * 1024 * 1024),
        cost_estimate=pl.CostEstimate(flops=9 * 10 ** 9, bytes_accessed=24 * 10 ** 6, transcendentals=10 ** 6),
    )(*args)
    res, tok, q1, q2 = pl.pallas_call(
        hand_on,
        out_shape=shapes,
        in_specs=[pl.BlockSpec(memory_space=pl.ANY)] * 4,
        out_specs=[pl.BlockSpec(memory_space=pl.ANY)] * 4,
        scratch_shapes=[pltpu.VMEM(s.shape, s.dtype) for s in shapes] + [pltpu.SemaphoreType.DMA((8,))],
    )(*outs)
    result = res.reshape(12, 6, 2, 1024).transpose(2, 0, 1, 3)
    grad_tokens = tok.reshape(2, 12, 24, 512).transpose(0, 2, 1, 3)
    return (result, grad_tokens, q1, q2)


def solution(mesh):
    sizes = (mesh.shape["lon"], mesh.shape["lat"])
    split = P(None, "lon", "lat", None)

    def run(*args):
        return shards(*args, sizes)

    return jax.shard_map(
        run,
        mesh=mesh,
        in_specs=(split, P(None, "lon", "lat")) + (P(),) * 10 + (split,),
        out_specs=(split, split, P("lon", "lat"), P("lon", "lat")),
        check_vma=False,
    )
```
